32 devices in a mesh: dp: 2 (over x), hd: 4 (over z), sq: 4 (over y, core).
Axes of the slice: x: 2, y: 2, z: 4, core: 2. Of those that a mesh axis runs over, the one named last changes fastest.
Arguments:
- inputs: bfloat16 [4, 1024, 2048], P('dp', ('hd', 'sq')), may hold values from -6 to 6
- cotangent: bfloat16 [4, 1024, 2048], P('dp', ('hd', 'sq')), may hold values from -6 to 6
- w_query: bfloat16 [2048, 2048], P(('dp', 'hd', 'sq')), may hold values from -0.25 to 0.25
- w_key: bfloat16 [2048, 2048], P(('dp', 'hd', 'sq')), may hold values from -0.125 to 0.125
- w_value: bfloat16 [2048, 2048], P(('dp', 'hd', 'sq')), may hold values from -0.125 to 0.125
- w_out: bfloat16 [2048, 2048], P(('dp', 'hd', 'sq')), may hold values from -0.5 to 0.5
- b_query: bfloat16 [2048], P(('dp', 'hd', 'sq')), may hold values from -3 to 3
- b_value: bfloat16 [2048], P(('dp', 'hd', 'sq')), may hold values from -0.59765625 to 0.59765625
- b_out: bfloat16 [2048], P(('dp', 'hd', 'sq')), may hold values from -1.796875 to 1.796875
- ln1_gain: bfloat16 [2048], P(('dp', 'hd', 'sq')), may hold values from 0.099609375 to 1.8984375
- ln1_bias: bfloat16 [2048], P(('dp', 'hd', 'sq')), may hold values from -1.796875 to 1.796875
- w_up: bfloat16 [2048, 8192], P(('dp', 'hd', 'sq')), may hold values from -0.125 to 0.125
- b_up: bfloat16 [8192], P(('dp', 'hd', 'sq')), may hold values from -3 to 3
- w_down: bfloat16 [8192, 2048], P(('dp', 'hd', 'sq')), may hold values from -0.0625 to 0.0625
- b_down: bfloat16 [2048], P(('dp', 'hd', 'sq')), may hold values from -1.796875 to 1.796875
- ln2_gain: bfloat16 [2048], P(('dp', 'hd', 'sq')), may hold values from 0.099609375 to 1.8984375
- ln2_bias: bfloat16 [2048], P(('dp', 'hd', 'sq')), may hold values from -1.796875 to 1.796875
Outputs:
- outputs: bfloat16 [4, 1024, 2048], P('dp', ('hd', 'sq'))
- input_grad: float32 [4, 1024, 2048], P('dp', ('hd', 'sq'))
- grad_w_query: float32 [2048, 2048], P(('dp', 'hd', 'sq'))
- grad_w_key: float32 [2048, 2048], P(('dp', 'hd', 'sq'))
- grad_w_value: float32 [2048, 2048], P(('dp', 'hd', 'sq'))
- grad_w_out: float32 [2048, 2048], P(('dp', 'hd', 'sq'))
- grad_b_query: float32 [2048], P(('dp', 'hd', 'sq'))
- grad_b_value: float32 [2048], P(('dp', 'hd', 'sq'))
- grad_b_out: float32 [2048], P(('dp', 'hd', 'sq'))
- grad_ln1_gain: float32 [2048], P(('dp', 'hd', 'sq'))
- grad_ln1_bias: float32 [2048], P(('dp', 'hd', 'sq'))
- grad_w_up: float32 [2048, 8192], P(('dp', 'hd', 'sq'))
- grad_b_up: float32 [8192], P(('dp', 'hd', 'sq'))
- grad_w_down: float32 [8192, 2048], P(('dp', 'hd', 'sq'))
- grad_b_down: float32 [2048], P(('dp', 'hd', 'sq'))
- grad_ln2_gain: float32 [2048], P(('dp', 'hd', 'sq'))
- grad_ln2_bias: float32 [2048], P(('dp', 'hd', 'sq'))
The draws below stay inside these ranges and needn't reach their ends.
All inputs are finite; a program needn't handle non-finite values.
Results may differ from the reference program's by a relative error of at most 0.025.
Values may be sent and summed in bfloat16 or wider, within the bound.
A program may use at most 288 MiB of HBM per device.

```python
import jax
import jax.numpy as jnp
from jax import lax

D = 2048
H = 16
HD = 128
FF = 8192
LEN = 1024
SEQS = 4


def level_of(own_key, extent, cuts, low, top_value):
    factor_of = 1.0
    for dim, blocks in cuts:
        steps = jax.random.uniform(jax.random.fold_in(jax.random.fold_in(own_key, 6), dim), (blocks,), jnp.float32, low / len(cuts), top_value / len(cuts))
        factor_of = factor_of * jnp.repeat(jnp.exp(steps), extent[dim] // blocks).reshape((-1,) + (1,) * (len(extent) - 1 - dim))
    return factor_of


def scatter_about(key, extent, scale, bound, shards=(), kind=jnp.bfloat16):
    values = jax.random.normal(key, extent, jnp.float32) * scale
    if len(shards) > 0:
        values = level_of(key, extent, shards, -0.22, 0.18) * values
    return jnp.clip(values, min=-bound, max=bound).astype(kind)


def setup_inputs(seed: int = 0) -> dict:
    seeds = jax.random.split(jax.random.key(seed), 18)
    inputs = scatter_about(seeds[0], (SEQS, LEN, D), 1.0, 6.0, ((0, 2), (1, 16)))
    cotangent = scatter_about(seeds[1], (SEQS, LEN, D), 1.0, 6.0, ((0, 2), (1, 16)))
    w_query = scatter_about(seeds[2], (D, D), (D // 4) ** -0.5, 0.25, ((0, 32),))
    w_key = scatter_about(seeds[3], (D, D), D ** -0.5, 0.125, ((0, 32),))
    w_value = scatter_about(seeds[4], (D, D), D ** -0.5, 0.125, ((0, 32),))
    w_out = scatter_about(seeds[5], (D, D), (D // 16) ** -0.5, 0.5, ((0, 32),))
    b_query = scatter_about(seeds[6], (D,), 0.5, 3.0, ((0, 32),))
    b_value = scatter_about(seeds[7], (D,), 0.1, 0.59765625, ((0, 32),))
    b_out = scatter_about(seeds[8], (D,), 0.3, 1.796875, ((0, 32),))
    ln1_gain = jnp.clip(1.0 + 0.18 * jax.random.normal(seeds[9], (D,), jnp.float32), 0.099609375, 1.8984375).astype(jnp.bfloat16)
    ln1_bias = scatter_about(seeds[10], (D,), 0.3, 1.796875, ((0, 32),))
    w_up = scatter_about(seeds[11], (D, FF), D ** -0.5, 0.125, ((0, 32),))
    b_up = scatter_about(seeds[12], (FF,), 0.5, 3.0, ((0, 32),))
    w_down = scatter_about(seeds[13], (FF, D), FF ** -0.5, 0.0625, ((0, 32),))
    b_down = scatter_about(seeds[14], (D,), 0.3, 1.796875, ((0, 32),))
    ln2_gain = jnp.clip(1.0 + 0.18 * jax.random.normal(seeds[15], (D,), jnp.float32), 0.099609375, 1.8984375).astype(jnp.bfloat16)
    ln2_bias = scatter_about(seeds[16], (D,), 0.3, 1.796875, ((0, 32),))
    return dict(inputs=inputs, cotangent=cotangent, w_query=w_query, w_key=w_key, w_value=w_value, w_out=w_out, b_query=b_query, b_value=b_value, b_out=b_out, ln1_gain=ln1_gain, ln1_bias=ln1_bias, w_up=w_up, b_up=b_up, w_down=w_down, b_down=b_down, ln2_gain=ln2_gain, ln2_bias=ln2_bias)


@jax.custom_vjp
def low(v):
    return lax.optimization_barrier(v.astype(jnp.bfloat16)).astype(jnp.float32)

@jax.custom_vjp
def low_back(v):
    return v

def low_keep(v):
    return (low(v), None)

def low_pass(kept, grad):
    return (grad,)

def back_keep(v):
    return (v, None)

def back_low(kept, grad):
    return (low(grad),)
low.defvjp(low_keep, low_pass)
low_back.defvjp(back_keep, back_low)
EPSILON = 1e-12

def matmul(left_side, right_side):
    return jnp.dot(left_side, right_side, precision=lax.Precision.HIGHEST)

def layer_norm(values, gamma_vec, beta_vec):
    average = lax.optimization_barrier(jnp.mean(values, axis=-1, keepdims=True))
    centred = values - average
    variance = lax.optimization_barrier(jnp.mean(centred * centred, axis=-1, keepdims=True))
    return centred * lax.rsqrt(variance + EPSILON) * gamma_vec + beta_vec

def to_heads(values):
    return values.reshape(values.shape[0], H, HD).transpose(1, 0, 2)

def head_attention(pieces):
    queries_h, keys_h, values_h = pieces
    scores = low_back(matmul(queries_h, keys_h.T) * HD ** (-0.5))
    softmaxed = jax.nn.softmax(scores, axis=-1)
    return matmul(low(softmaxed), values_h)

def layer(row_in, w_query, w_key, w_value, w_out, b_query, b_value, b_out, ln1_gain, ln1_bias, w_up, b_up, w_down, b_down, ln2_gain, ln2_bias):
    queries = low_back(low(matmul(row_in, w_query) + b_query))
    keys_all = low_back(low(matmul(row_in, w_key)))
    values_all = low_back(low(matmul(row_in, w_value) + b_value))
    mixed = lax.map(jax.checkpoint(head_attention), (to_heads(queries), to_heads(keys_all), to_heads(values_all)))
    context = mixed.transpose(1, 0, 2).reshape(row_in.shape[0], H * HD)
    context = low_back(low(context))
    branch = low_back(matmul(context, w_out) + b_out)
    normed_one = layer_norm(row_in + branch, ln1_gain, ln1_bias)
    hidden = low_back(matmul(low(normed_one), w_up) + b_up)
    activated = low(jax.nn.gelu(hidden, approximate=True))
    second_branch = low_back(matmul(activated, w_down) + b_down)
    return layer_norm(normed_one + second_branch, ln2_gain, ln2_bias)

def reference(inputs, cotangent, w_query, w_key, w_value, w_out, b_query, b_value, b_out, ln1_gain, ln1_bias, w_up, b_up, w_down, b_down, ln2_gain, ln2_bias):
    raw = (w_query, w_key, w_value, w_out, b_query, b_value, b_out, ln1_gain, ln1_bias, w_up, b_up, w_down, b_down, ln2_gain, ln2_bias)
    params = tuple((param.astype(jnp.float32) for param in raw))

    def one_sequence(totals, pieces):
        row_in, row_cot = pieces
        result, pullback = jax.vjp(layer, row_in.astype(jnp.float32), *params)
        grads = pullback(row_cot.astype(jnp.float32))
        totals = jax.tree.map(jnp.add, totals, tuple(grads[1:]))
        return (totals, (result.astype(jnp.bfloat16), grads[0]))
    zeros = tuple((jnp.zeros(param.shape, jnp.float32) for param in params))
    totals, (outputs, input_grad) = lax.scan(one_sequence, zeros, (inputs, cotangent))
    return (outputs, input_grad, totals[0], totals[1], totals[2], totals[3], totals[4], totals[5], totals[6], totals[7], totals[8], totals[9], totals[10], totals[11], totals[12], totals[13], totals[14])
```

```python
import functools

import jax
import jax.numpy as jnp
from jax import lax
from jax.experimental import pallas as pl
from jax.experimental.pallas import tpu as pltpu
from jax.sharding import Mesh
from jax.sharding import PartitionSpec as P

F32 = jnp.float32
BF16 = jnp.bfloat16
HD = 128
EPSILON = 1e-12
TP = 8
STRIP = 16
VMEM_LIMIT = 60 * 2**20
AXES = ("x", "zh", "zl", "y", "c")
SCALE = HD ** (-0.5)


class Sizes:
    def __init__(self, groups_x, width, hidden, tokens):
        self.nx = groups_x
        self.parts = 2 * groups_x
        self.width = width
        self.hidden = hidden
        self.tokens = tokens
        self.half = tokens // 2
        self.rows_all = TP * tokens
        self.row_shard = width // (TP * self.parts)
        self.hid_shard = hidden // (TP * self.parts)
        self.pieces = HD // self.row_shard
        self.heads = width // HD // TP
        self.cols = self.heads * HD
        self.hid = hidden // TP
        self.slab = width // self.parts


class Place:
    def __init__(self, sizes):
        self.x, self.zh, self.zl, self.y, self.c = (lax.axis_index(a) for a in AXES)
        self.nx = sizes.nx
        self.t = self.zl * 4 + self.y * 2 + self.c
        self.p = self.x * 2 + self.zh
        self.pz = self.x * 2 + (1 - self.zh)
        self.to_c = {"c": 1 - self.c}
        self.to_y = {"y": 1 - self.y}
        self.to_z = {"zl": 1 - self.zl}
        self.to_h = {"zh": 1 - self.zh}

    def peer(self, flip):
        target = {}
        if flip & 4:
            target["zl"] = 1 - self.zl
        if flip & 2:
            target["y"] = 1 - self.y
        if flip & 1:
            target["c"] = 1 - self.c
        return target

    def index_of(self, flip):
        zl = 1 - self.zl if flip & 4 else self.zl
        y = 1 - self.y if flip & 2 else self.y
        c = 1 - self.c if flip & 1 else self.c
        return zl * 4 + y * 2 + c

    def to_x(self, step):
        return {"x": lax.rem(self.x + step, self.nx)}

    def x_of(self, step):
        return lax.rem(self.x + step, self.nx)


class Copies:
    def __init__(self, send, recv, local):
        self.send, self.recv, self.local_sems = send, recv, local
        self.n_remote = 0
        self.n_local = 0
        self.sent = []
        self.kept = []

    def remote(self, src, dst, target):
        i = self.n_remote
        self.n_remote += 1
        copy = pltpu.make_async_remote_copy(
            src_ref=src,
            dst_ref=dst,
            send_sem=self.send.at[i],
            recv_sem=self.recv.at[i],
            device_id=target,
            device_id_type=pl.DeviceIdType.MESH,
        )
        copy.start()
        self.sent.append(copy)
        return copy

    def local(self, src, dst):
        i = self.n_local
        self.n_local += 1
        copy = pltpu.make_async_copy(src, dst, self.local_sems.at[i])
        copy.start()
        return copy

    def keep(self, src, dst):
        self.kept.append(self.local(src, dst))

    def left(self, copy):
        copy.wait_send()
        self.sent = [other for other in self.sent if other is not copy]

    def finish(self):
        for copy in self.kept:
            copy.wait()
        for copy in self.sent:
            copy.wait_send()


def greet(targets):
    barrier = pltpu.get_barrier_semaphore()
    for target in targets:
        pl.semaphore_signal(
            barrier, inc=1, device_id=target, device_id_type=pl.DeviceIdType.MESH
        )
    pl.semaphore_wait(barrier, len(targets))


def dot(left, right):
    return jnp.dot(left, right, preferred_element_type=F32)


def dot_nt(left, right):
    return lax.dot_general(left, right, (((1,), (1,)), ((), ())), preferred_element_type=F32)


def dot_tn(left, right):
    return lax.dot_general(left, right, (((0,), (0,)), ((), ())), preferred_element_type=F32)


def tile(i, size):
    return pl.ds(pl.multiple_of(i * size, size), size)


def loop(count, body):
    def step(i, carry):
        body(i)
        return carry

    lax.fori_loop(0, count, step, 0)


def normed(values):
    average = jnp.mean(values, axis=1, keepdims=True)
    centred = values - average
    variance = jnp.mean(centred * centred, axis=1, keepdims=True)
    scale = lax.rsqrt(variance + EPSILON)
    return centred * scale, scale


def normed_back(grad, xhat, scale):
    along = jnp.mean(grad * xhat, axis=1, keepdims=True)
    return scale * (grad - jnp.mean(grad, axis=1, keepdims=True) - xhat * along)


class Gather:
    def __init__(self, net, at, sz, buf, start, count):
        self.net, self.at, self.sz, self.buf = net, at, sz, buf
        self.start, self.count = start, count
        half = sz.width // 2
        self.cols = (pl.ds(0, half), pl.ds(half, half))
        self.sib = [None] * 4

    def part(self, slot, core, cols=None):
        rows = pl.ds((slot * 2 + core) * self.sz.tokens + self.start, self.count)
        return self.buf.at[rows, :] if cols is None else self.buf.at[rows, cols]

    def send(self):
        net, at = self.net, self.at
        self.from_y = [None, None]
        self.from_z = [None, None]
        for h in (0, 1):
            self.from_y[h] = net.remote(
                self.part(0, 0, self.cols[h]), self.part(1, 0, self.cols[h]), at.to_y
            )
            self.from_z[1 - h] = net.remote(
                self.part(0, 0, self.cols[1 - h]), self.part(2, 0, self.cols[1 - h]), at.to_z
            )
        self.share(0)

    def share(self, slot):
        self.sib[slot] = self.net.remote(self.part(slot, 0), self.part(slot, 1), self.at.to_c)

    def relay(self):
        net, at = self.net, self.at
        self.from_y[0].wait_recv()
        to_z = net.remote(
            self.part(1, 0, self.cols[0]), self.part(3, 0, self.cols[0]), at.to_z
        )
        self.from_z[1].wait_recv()
        to_y = net.remote(
            self.part(2, 0, self.cols[1]), self.part(3, 0, self.cols[1]), at.to_y
        )
        self.diag = (to_z, to_y)
        self.from_y[1].wait_recv()
        self.share(1)
        self.from_z[0].wait_recv()
        self.share(2)

    def relay_last(self):
        for copy in self.diag:
            copy.wait_recv()
        self.share(3)

    def ready(self, slot):
        self.sib[slot].wait_recv()


class Scatter:
    def __init__(self, net, at, sz, bufs):
        self.net, self.at, self.sz = net, at, sz
        self.mine, self.theirs, self.got, self.diag, self.diag_got, self.out, self.inn = bufs
        self.sib = [None] * 4

    @staticmethod
    def scratch(sz):
        t, d = sz.tokens, sz.width
        return [
            pltpu.VMEM((4 * t, d), F32),
            pltpu.VMEM((4 * t, d), BF16),
            pltpu.VMEM((4 * t, d), BF16),
            pltpu.VMEM((t, d), BF16),
            pltpu.VMEM((t, d), BF16),
            pltpu.VMEM((2 * t, d), BF16),
            pltpu.VMEM((2 * t, d), BF16),
        ]

    def put(self, slot, cols, value):
        t = self.sz.tokens
        self.mine[pl.ds(slot * t, t), cols] = value[:t]
        self.theirs[pl.ds(slot * t, t), cols] = value[t:].astype(BF16)

    def share(self, slot):
        rows = pl.ds(slot * self.sz.tokens, self.sz.tokens)
        self.sib[slot] = self.net.remote(self.theirs.at[rows, :], self.got.at[rows, :], self.at.to_c)

    def add(self, slot, start, count, dst, dst_start, extra=None):
        base = slot * self.sz.tokens + start

        def body(i):
            rows = pl.ds(pl.multiple_of(base + i * STRIP, STRIP), STRIP)
            total = self.mine[rows, :] + self.got[rows, :].astype(F32)
            if extra is not None:
                there = pl.ds(pl.multiple_of(start + i * STRIP, STRIP), STRIP)
                total = total + extra[there, :].astype(F32)
            dst[pl.ds(pl.multiple_of(dst_start + i * STRIP, STRIP), STRIP), :] = total.astype(BF16)

        loop(count // STRIP, body)

    def send_diag(self):
        net, at, h = self.net, self.at, self.sz.half
        self.sib[3].wait_recv()
        self.add(3, 0, 2 * h, self.diag, 0)
        low, high = pl.ds(0, h), pl.ds(h, h)
        self.d_low = net.remote(self.diag.at[low, :], self.diag_got.at[low, :], at.to_y)
        self.d_high = net.remote(self.diag.at[high, :], self.diag_got.at[high, :], at.to_z)

    def half_out(self, side, start, target):
        rows = pl.ds(side * self.sz.tokens + start, self.sz.half)
        return self.net.remote(self.out.at[rows, :], self.inn.at[rows, :], target)

    def send_free(self):
        at, t, h = self.at, self.sz.tokens, self.sz.half
        self.sib[1].wait_recv()
        self.add(1, 0, h, self.out, 0)
        self.y_low = self.half_out(0, 0, at.to_y)
        self.sib[2].wait_recv()
        self.add(2, h, h, self.out, t + h)
        self.z_high = self.half_out(1, h, at.to_z)

    def send_joined(self):
        at, t, h = self.at, self.sz.tokens, self.sz.half
        self.d_high.wait_recv()
        self.add(1, h, h, self.out, h, self.diag_got)
        self.y_high = self.half_out(0, h, at.to_y)
        self.d_low.wait_recv()
        self.add(2, 0, h, self.out, t, self.diag_got)
        self.z_low = self.half_out(1, 0, at.to_z)

    def settle(self):
        for copy in [*self.sib, self.d_low, self.d_high, self.y_low, self.z_high, self.y_high, self.z_low]:
            self.net.left(copy)

    def wait(self):
        self.sib[0].wait_recv()
        for copy in (self.y_low, self.z_high, self.y_high, self.z_low):
            copy.wait_recv()

    def total(self, i):
        t = self.sz.tokens
        rows = tile(i, STRIP)
        far = pl.ds(pl.multiple_of(t + i * STRIP, STRIP), STRIP)
        return (
            self.mine[rows, :]
            + self.got[rows, :].astype(F32)
            + self.inn[rows, :].astype(F32)
            + self.inn[far, :].astype(F32)
        )


class Spread:
    def __init__(self, net, at, view, own, across):
        self.net, self.at, self.view = net, at, view
        self.own, self.across = own, across
        self.from_h = net.remote(view(own), view(own), at.to_h)
        self.from_x = [
            net.remote(view(own), view(own), at.to_x(step)) for step in range(1, at.nx)
        ]
        self.relayed = []

    def relay(self):
        self.from_h.wait_recv()
        self.relayed = [
            self.net.remote(self.view(self.across), self.view(self.across), self.at.to_x(step))
            for step in range(1, self.at.nx)
        ]

    def near(self):
        for copy in self.from_x:
            copy.wait_recv()

    def far(self):
        for copy in self.relayed:
            copy.wait_recv()


def attention_forward_kernel(
    sz,
    xin, wqkv_pack, wup_pack, wout, wdown, vec_pack,
    x_all, wqkv, w_out_own, w_up, w_down, vec_all, bup_all, qkv_all, ctx_all, first_in, first_all,
    xs, wq, wo_got, wo, vecs, vec, bup, acc, qkv, ctx, fin, first, *rest,
):
    *sum_bufs, send, recv, local = rest
    at = Place(sz)
    net = Copies(send, recv, local)
    t, d, h = sz.tokens, sz.width, sz.half
    rw, rf = sz.row_shard, sz.hid_shard
    flips = range(1, TP)
    greet(
        [at.peer(f) for f in flips] + [at.to_h] + [at.to_x(s) for s in range(1, sz.nx)]
    )

    own_rows = pl.ds(at.zh * h, h)
    from_h = net.remote(xin.at[1 - at.zh], xs.at[own_rows, :], at.to_h)
    own_x = net.local(xin.at[at.zh], xs.at[own_rows, :])

    def wq_rows(p, member, count=1):
        return pl.ds((p * TP + member) * rw, count * rw)

    own_wq = net.local(wqkv_pack.at[at.t], wq.at[wq_rows(at.p, at.t), :])
    own_vec = net.local(vec_pack, vecs.at[at.p * TP + at.t])
    own_wu = net.local(wup_pack.at[at.t], w_up.at[wq_rows(at.p, at.t), :])
    own_wd = net.local(wdown, w_down.at[pl.ds(at.p * rf, rf), :])
    own_wo = net.local(wout, wo_got.at[at.p])
    vec_in = [net.remote(vec_pack, vecs.at[at.p * TP + at.t], at.peer(f)) for f in flips]
    wq_in = [None] + [
        net.remote(wqkv_pack.at[at.index_of(f)], wq.at[wq_rows(at.p, at.t), :], at.peer(f))
        for f in flips
    ]
    own_x.wait()
    near_rows = Gather(net, at, sz, xs, at.zh * h, h)
    near_rows.send()

    def chip_block(buf, f):
        member = at.index_of(f) - at.c
        return lambda p: buf.at[wq_rows(p, member, 2), :]

    wq_spread = []
    for f in (0, 2, 4, 6):
        if f == 0:
            own_wq.wait()
        else:
            wq_in[f].wait_recv()
        wq_in[f + 1].wait_recv()
        wq_spread.append(Spread(net, at, chip_block(wq, f), at.p, at.pz))
    own_vec.wait()
    for copy in vec_in:
        copy.wait_recv()
    vec_spread = Spread(net, at, lambda p: vecs.at[pl.ds(p * TP, TP)], at.p, at.pz)
    wu_in = [None] + [
        net.remote(wup_pack.at[at.index_of(f)], w_up.at[wq_rows(at.p, at.t), :], at.peer(f))
        for f in flips
    ]
    from_h.wait_recv()
    far_rows = Gather(net, at, sz, xs, (1 - at.zh) * h, h)
    far_rows.send()
    near_rows.relay()
    own_wo.wait()
    wo_spread = Spread(net, at, lambda p: wo_got.at[p], at.p, at.pz)
    vec_spread.relay()
    far_rows.relay()
    near_rows.relay_last()
    far_rows.relay_last()

    def accumulate(zh, first_part):
        def body(i):
            rows = tile(i, 256)
            total = jnp.zeros((256, 3 * sz.cols), F32) if first_part else acc[rows, :]
            for x in range(sz.nx):
                block = tile(x * 2 + zh, sz.slab)
                total = total + dot(xs[rows, block], wq[block, :])
            acc[rows, :] = total

        loop(sz.rows_all // 256, body)

    for slot in range(4):
        near_rows.ready(slot)
        far_rows.ready(slot)
    for item in wq_spread:
        item.near()
    net.keep(xs, x_all)
    accumulate(at.zh, True)
    for item in wq_spread:
        item.relay()
    own_wu.wait()
    own_wd.wait()
    wu_spread = []
    for f in (0, 2, 4, 6):
        if f:
            wu_in[f].wait_recv()
        wu_in[f + 1].wait_recv()
        wu_spread.append(Spread(net, at, chip_block(w_up, f), at.p, at.pz))
    for item in wq_spread:
        item.far()
    vec_spread.near()
    vec_spread.far()
    for j in range(d // HD):
        piece = vecs[j * sz.pieces, 0:8]
        for k in range(1, sz.pieces):
            piece = piece + vecs[j * sz.pieces + k, 0:8]
        vec[:, j * HD : (j + 1) * HD] = piece
    if rf >= HD:
        for p in range(sz.parts):
            for j in range(rf // HD):
                lanes = pl.ds(p * rf + j * HD, HD)
                bup[0:1, lanes] = vecs[p * TP + at.t, 8 + j : 9 + j]
    else:
        for j in range(sz.hid // HD):
            each = HD // rf
            row = vecs[j * each * TP + at.t, 8:9]
            for k in range(1, each):
                row = row + vecs[(j * each + k) * TP + at.t, 8:9]
            bup[0:1, j * HD : (j + 1) * HD] = row
    net.keep(vec, vec_all)
    net.keep(bup, bup_all)
    accumulate(1 - at.zh, False)

    group = at.t // sz.pieces
    member = at.t - group * sz.pieces
    per = TP // sz.pieces
    for k in range(sz.heads):
        head = (member * sz.heads + k) * per + group
        lanes = tile(head, HD)

        def biased(i, k=k, lanes=lanes):
            rows = tile(i, 256)
            for which in range(3):
                cols = slice(which * sz.cols + k * HD, which * sz.cols + (k + 1) * HD)
                value = acc[rows, cols]
                if which != 1:
                    value = value + vec[which // 2 : which // 2 + 1, lanes]
                qkv[rows, cols] = value.astype(BF16)

        loop(sz.rows_all // 256, biased)
    net.keep(wq, wqkv)
    net.keep(qkv, qkv_all)

    def attend(k):
        q_cols = slice(k * HD, (k + 1) * HD)
        k_cols = slice(sz.cols + k * HD, sz.cols + (k + 1) * HD)
        v_cols = slice(2 * sz.cols + k * HD, 2 * sz.cols + (k + 1) * HD)

        def body(i):
            rows = tile(i, 256)
            scores = dot_nt(qkv[rows, q_cols], qkv[:, k_cols]) * SCALE
            top = jnp.max(scores, axis=1, keepdims=True)
            exps = jnp.exp(scores - top)
            probs = exps * (1.0 / jnp.sum(exps, axis=1, keepdims=True))
            ctx[rows, q_cols] = dot(probs.astype(BF16), qkv[:, v_cols]).astype(BF16)

        loop(sz.rows_all // 256, body)

    attend(0)
    wo_spread.relay()
    for item in wu_spread[:1]:
        item.relay()
    for k in range(1, sz.heads):
        attend(k)
    wd_chunk = rf // 4
    wd_spread = [
        Spread(net, at, lambda p, j=j: w_down.at[pl.ds(p * rf + j * wd_chunk, wd_chunk), :], at.p, at.pz)
        for j in range(4)
    ]
    net.keep(ctx, ctx_all)

    wo_spread.near()
    wo_spread.far()

    def wo_rows(k, piece):
        return pl.ds((k * sz.pieces + piece) * rw, rw)

    for k in range(sz.heads):
        net.local(wo_got.at[member * sz.heads + k], wo.at[wo_rows(k, member), :]).wait()
    wo_in = []
    for f in range(1, sz.pieces):
        other = at.index_of(f) - group * sz.pieces
        for k in range(sz.heads):
            wo_in.append(
                net.remote(wo_got.at[other * sz.heads + k], wo.at[wo_rows(k, member), :], at.peer(f))
            )
    for copy in wo_in:
        copy.wait_recv()
    net.keep(wo, w_out_own)

    sums = Scatter(net, at, sz, sum_bufs)
    for slot in (3, 1, 2, 0):
        rows = pl.ds(slot * 2 * t, 2 * t)

        def body(i, rows=rows, slot=slot):
            cols = tile(i, 512)
            sums.put(slot, cols, dot(ctx[rows, :], wo[:, cols]))

        loop(d // 512, body)
        sums.share(slot)
        if slot == 3:
            sums.send_diag()
    sums.send_free()
    for item in wu_spread[1:2]:
        item.relay()
    sums.send_joined()
    for item in wu_spread[2:3]:
        item.relay()
    sums.wait()

    def norm(i):
        rows = tile(i, STRIP)
        value = xs[rows, :].astype(F32) + sums.total(i) + vec[2:3, :]
        fin[rows, :] = value
        xhat, _ = normed(value)
        first[rows, :] = (xhat * vec[3:4, :] + vec[4:5, :]).astype(BF16)

    loop(t // STRIP, norm)
    net.keep(fin, first_in)
    net.local(first, first_all.at[pl.ds(0, t), :]).wait()
    firsts = Gather(net, at, sz, first_all, 0, t)
    firsts.send()
    for item in wu_spread[3:]:
        item.relay()
    firsts.relay()
    firsts.relay_last()
    for slot in range(4):
        firsts.ready(slot)
    for item in wd_spread:
        item.relay()
    for item in wu_spread + wd_spread:
        item.near()
        item.far()
    net.finish()


def attention_forward(sz, xin, wqkv_pack, wup_pack, wout, wdown, vec_pack):
    t, d, r = sz.tokens, sz.width, sz.rows_all
    shape = jax.ShapeDtypeStruct
    anywhere = pl.BlockSpec(memory_space=pl.ANY)
    outs = (
        shape((r, d), BF16),
        shape((d, 3 * sz.cols), BF16),
        shape((sz.cols, d), BF16),
        shape((d, sz.hid), BF16),
        shape((sz.hid, d), BF16),
        shape((8, d), F32),
        shape((8, sz.hid), F32),
        shape((r, 3 * sz.cols), BF16),
        shape((r, sz.cols), BF16),
        shape((t, d), F32),
        shape((r, d), BF16),
    )
    scratch = [
        pltpu.VMEM((r, d), BF16),
        pltpu.VMEM((d, 3 * sz.cols), BF16),
        pltpu.VMEM((sz.parts, sz.row_shard, d), BF16),
        pltpu.VMEM((sz.cols, d), BF16),
        pltpu.VMEM((sz.parts * TP, 16, HD), F32),
        pltpu.VMEM((8, d), F32),
        pltpu.VMEM((8, sz.hid), F32),
        pltpu.VMEM((r, 3 * sz.cols), F32),
        pltpu.VMEM((r, 3 * sz.cols), BF16),
        pltpu.VMEM((r, sz.cols), BF16),
        pltpu.VMEM((t, d), F32),
        pltpu.VMEM((t, d), BF16),
        *Scatter.scratch(sz),
        pltpu.SemaphoreType.DMA((80 + 28 * sz.nx,)),
        pltpu.SemaphoreType.DMA((80 + 28 * sz.nx,)),
        pltpu.SemaphoreType.DMA((24,)),
    ]
    return pl.pallas_call(
        functools.partial(attention_forward_kernel, sz),
        out_shape=outs,
        in_specs=[anywhere] * 6,
        out_specs=[anywhere] * len(outs),
        scratch_shapes=scratch,
        compiler_params=pltpu.CompilerParams(
            collective_id=0, has_side_effects=True, vmem_limit_bytes=VMEM_LIMIT
        ),
        name="attention_forward",
    )(xin, wqkv_pack, wup_pack, wout, wdown, vec_pack)


GELU_A = 0.7978845608028654
GELU_B = 0.044715


def gate(values):
    inner = jnp.tanh(GELU_A * (values + GELU_B * values * values * values))
    return 0.5 * values * (1.0 + inner)


def gate_slope(values):
    square = values * values
    inner = jnp.tanh(GELU_A * (values + GELU_B * square * values))
    rise = GELU_A * (1.0 + 3.0 * GELU_B * square)
    return 0.5 * (1.0 + inner) + 0.5 * values * (1.0 - inner * inner) * rise


def feed_forward_kernel(
    sz,
    first_all, first_in, w_up, w_down, vec_all, bup_all, cot_in,
    outputs, grad_first_in, grad_low, grad_w_up, grad_w_down, grad_vec,
    fa, wu, wd, vec, bup, fin, cot, hid, act, gh, g2, g2s, out, gv, dwu, dwd, *rest,
):
    *sum_bufs, send, recv, local = rest
    at = Place(sz)
    net = Copies(send, recv, local)
    t, d, h = sz.tokens, sz.width, sz.half
    two = 2 * t
    loads = {slot: net.local(first_all.at[pl.ds(slot * two, two), :], fa.at[pl.ds(slot * two, two), :])
             for slot in (3,)}
    load_up = net.local(w_up, wu)
    load_bup = net.local(bup_all, bup)
    for slot in (1, 2, 0):
        loads[slot] = net.local(
            first_all.at[pl.ds(slot * two, two), :], fa.at[pl.ds(slot * two, two), :]
        )
    load_down = net.local(w_down, wd)
    load_vec = net.local(vec_all, vec)
    load_fin = net.local(first_in, fin)
    own_rows = pl.ds(at.zh * h, h)
    load_cot = net.local(cot_in.at[at.zh], cot.at[own_rows, :])
    greet([at.to_c, at.to_y, at.to_z, at.to_h])
    cot_far = net.remote(cot_in.at[1 - at.zh], cot.at[own_rows, :], at.to_h)
    gv[...] = jnp.zeros_like(gv)

    sums = Scatter(net, at, sz, sum_bufs)
    load_up.wait()
    load_bup.wait()
    for slot in (3, 1, 2, 0):
        loads[slot].wait()
        rows = pl.ds(slot * two, two)

        def up(i, rows=rows):
            cols = tile(i, 512)
            value = dot(fa[rows, :], wu[:, cols]) + bup[0:1, cols]
            hid[rows, cols] = value
            act[rows, cols] = gate(value).astype(BF16)

        loop(sz.hid // 512, up)
        if slot == 3:
            load_down.wait()

        def down(i, rows=rows, slot=slot):
            cols = tile(i, 512)
            sums.put(slot, cols, dot(act[rows, :], wd[:, cols]))

        loop(d // 512, down)
        sums.share(slot)
        if slot == 1:
            sums.send_diag()
    sums.send_free()
    sums.send_joined()
    load_vec.wait()
    load_fin.wait()
    load_cot.wait()
    cot_far.wait_recv()
    sums.wait()

    def strip_sum(row, value):
        gv[row : row + 1, :] = gv[row : row + 1, :] + jnp.sum(value, axis=0, keepdims=True)

    def second_norm(i):
        rows = tile(i, STRIP)
        xhat, _ = normed(fin[rows, :])
        value = xhat * vec[3:4, :] + vec[4:5, :] + sums.total(i) + vec[5:6, :]
        xhat, scale = normed(value)
        out[rows, :] = (xhat * vec[6:7, :] + vec[7:8, :]).astype(BF16)
        grad = cot[rows, :].astype(F32)
        strip_sum(6, grad * xhat)
        strip_sum(7, grad)
        grad = normed_back(grad * vec[6:7, :], xhat, scale)
        g2s[rows, :] = grad
        low = grad.astype(BF16)
        g2[rows, :] = low
        strip_sum(5, low.astype(F32))

    loop(t // STRIP, second_norm)
    gather = Gather(net, at, sz, g2, 0, t)
    gather.send()
    net.keep(out.at[own_rows, :], outputs.at[at.zh])
    out_far = net.remote(out.at[pl.ds((1 - at.zh) * h, h), :], outputs.at[at.zh], at.to_h)
    sums.settle()

    def back(slot):
        gather.ready(slot)
        rows = pl.ds(slot * two, two)

        def down(i):
            cols = tile(i, 512)
            value = dot_nt(g2[rows, :], wd[cols, :])
            gh[rows, cols] = (value * gate_slope(hid[rows, cols])).astype(BF16)

        loop(sz.hid // 512, down)

        def up(i):
            cols = tile(i, 512)
            sums.put(slot, cols, dot_nt(gh[rows, :], wu[cols, :]))

        loop(d // 512, up)
        sums.share(slot)

    back(0)
    gather.relay()
    back(1)
    back(2)
    sums.send_free()
    gather.relay_last()
    back(3)
    sums.send_diag()

    def down_grad(i):
        rows, cols = tile(i // (d // 512), 512), tile(i % (d // 512), 512)
        dwd[rows, cols] = dot_tn(act[:, rows], g2[:, cols]).astype(BF16)

    loop((sz.hid // 512) * (d // 512), down_grad)
    net.keep(dwd, grad_w_down)
    sums.send_joined()

    def up_grad(i):
        rows, cols = tile(i // (sz.hid // 512), 512), tile(i % (sz.hid // 512), 512)
        dwu[rows, cols] = dot_tn(fa[:, rows], gh[:, cols]).astype(BF16)

    loop((sz.hid // 512) * (d // 512), up_grad)
    net.keep(dwu, grad_w_up)
    for p in range(sz.parts):
        rf = sz.hid_shard
        gv[8:9, p * sz.slab : p * sz.slab + rf] = jnp.sum(
            gh[:, p * rf : (p + 1) * rf].astype(F32), axis=0, keepdims=True
        )
    sums.wait()

    def first_norm(i):
        rows = tile(i, STRIP)
        xhat, scale = normed(fin[rows, :])
        grad = g2s[rows, :] + sums.total(i)
        strip_sum(3, grad * xhat)
        strip_sum(4, grad)
        grad = normed_back(grad * vec[3:4, :], xhat, scale)
        g2s[rows, :] = grad
        low = grad.astype(BF16)
        out_low[rows, :] = low
        strip_sum(2, low.astype(F32))

    out_low = cot
    loop(t // STRIP, first_norm)
    net.keep(g2s, grad_first_in)
    net.keep(out_low, grad_low)
    net.keep(gv, grad_vec)
    out_far.wait_recv()
    net.finish()


def feed_forward(sz, *args):
    t, d, r = sz.tokens, sz.width, sz.rows_all
    shape = jax.ShapeDtypeStruct
    anywhere = pl.BlockSpec(memory_space=pl.ANY)
    outs = (
        shape((2, sz.half, d), BF16),
        shape((t, d), F32),
        shape((t, d), BF16),
        shape((d, sz.hid), BF16),
        shape((sz.hid, d), BF16),
        shape((16, d), F32),
    )
    scratch = [
        pltpu.VMEM((r, d), BF16),
        pltpu.VMEM((d, sz.hid), BF16),
        pltpu.VMEM((sz.hid, d), BF16),
        pltpu.VMEM((8, d), F32),
        pltpu.VMEM((8, sz.hid), F32),
        pltpu.VMEM((t, d), F32),
        pltpu.VMEM((t, d), BF16),
        pltpu.VMEM((r, sz.hid), F32),
        pltpu.VMEM((r, sz.hid), BF16),
        pltpu.VMEM((r, sz.hid), BF16),
        pltpu.VMEM((r, d), BF16),
        pltpu.VMEM((t, d), F32),
        pltpu.VMEM((t, d), BF16),
        pltpu.VMEM((16, d), F32),
        pltpu.VMEM((d, sz.hid), BF16),
        pltpu.VMEM((sz.hid, d), BF16),
        *Scatter.scratch(sz),
        pltpu.SemaphoreType.DMA((40,)),
        pltpu.SemaphoreType.DMA((40,)),
        pltpu.SemaphoreType.DMA((24,)),
    ]
    return pl.pallas_call(
        functools.partial(feed_forward_kernel, sz),
        out_shape=outs,
        in_specs=[anywhere] * 7,
        out_specs=[anywhere] * len(outs),
        scratch_shapes=scratch,
        compiler_params=pltpu.CompilerParams(
            collective_id=1, has_side_effects=True, vmem_limit_bytes=VMEM_LIMIT
        ),
        name="feed_forward",
    )(*args)


class Reduce:
    def __init__(self, net, at, view, bufs, chunks, held, result):
        self.net, self.at, self.view, self.chunks = net, at, view, chunks
        self.got, self.own, self.out, self.inn = bufs
        self.rows = self.out.shape[0] // chunks
        self.result = result
        self.held = held
        self.groups = (at.x * 2 + (1 - at.zh), at.x * 2 + at.zh)

    @staticmethod
    def scratch(sz, rows, cols, dtype, held):
        return [
            pltpu.VMEM((sz.nx - 1, 2, rows, cols), dtype),
            pltpu.VMEM((2, 8, 128) if held else (2, rows, cols), dtype),
            pltpu.VMEM((rows, cols), dtype),
            pltpu.VMEM((rows, cols), dtype),
        ]

    def chunk(self, j):
        return pl.ds(j * self.rows, self.rows)

    def start(self):
        at, net = self.at, self.net
        self.from_x = {}
        for which in (0, 1):
            zh = 1 - at.zh if which == 0 else at.zh
            for j in range(self.chunks):
                for step in range(1, at.nx):
                    p = at.x_of(step) * 2 + zh
                    self.from_x[which, j, step] = net.remote(
                        self.view(p, j), self.got.at[step - 1, which, self.chunk(j), :], at.to_x(step)
                    )
        if not self.held:
            self.loads = {
                (which, j): net.local(self.view(self.groups[which], j), self.own.at[which, self.chunk(j), :])
                for which in (0, 1)
                for j in range(self.chunks)
            }
        self.from_h = {}

    def term(self, which, j, i):
        rows = pl.ds(pl.multiple_of(j * self.rows + i * STRIP, STRIP), STRIP)
        if self.held:
            total = self.view(self.groups[which], j)[tile(i, STRIP), :].astype(F32)
        else:
            total = self.own[which, rows, :].astype(F32)
        for step in range(1, self.at.nx):
            total = total + self.got[step - 1, which, rows, :].astype(F32)
        return rows, total

    def ready(self, which, j):
        for step in range(1, self.at.nx):
            self.from_x[which, j, step].wait_recv()
        if not self.held:
            self.loads[which, j].wait()

    def hop(self, j):
        self.ready(0, j)

        def body(i):
            rows, total = self.term(0, j, i)
            self.out[rows, :] = total.astype(self.out.dtype)

        loop(self.rows // STRIP, body)
        self.from_h[j] = self.net.remote(
            self.out.at[self.chunk(j), :], self.inn.at[self.chunk(j), :], self.at.to_h
        )

    def close(self, j):
        self.ready(1, j)
        self.from_h[j].wait_recv()

        def body(i):
            rows, total = self.term(1, j, i)
            self.result[rows, :] = (total + self.inn[rows, :].astype(F32)).astype(self.result.dtype)

        loop(self.rows // STRIP, body)


def attention_backward_kernel(
    sz,
    grad_low, grad_first_in, x_all, wqkv, w_out_own, qkv_all, ctx_all, grad_w_up, grad_w_down, grad_vec,
    input_grad, out_wqkv, out_wo, out_wup, out_wdown, out_vec, out_bup,
    gb, xs, wq, wo, qkv, ctx, gfi, gv, dctx, dqkv, dk, dv, ig, dwq, dwo, dwo_own, res_q, res_o, res_u, res_d, res_v,
    vec_got, vec_sum, bup_out, *rest,
):
    *bufs, send, recv, local = rest
    sum_bufs, bufs = bufs[:7], bufs[7:]
    at = Place(sz)
    net = Copies(send, recv, local)
    t, d, h = sz.tokens, sz.width, sz.half
    two = 2 * t
    rw, rf = sz.row_shard, sz.hid_shard
    flips = range(1, TP)
    load_gb = net.local(grad_low, gb.at[pl.ds(0, t), :])
    load_wo = net.local(w_out_own, wo)
    load_qkv = net.local(qkv_all, qkv)
    load_ctx = net.local(ctx_all, ctx)
    load_gv = net.local(grad_vec, gv)
    greet([at.peer(f) for f in flips] + [at.to_h] + [at.to_x(s) for s in range(1, sz.nx)])
    load_gb.wait()
    gather = Gather(net, at, sz, gb, 0, t)
    gather.send()

    up_rows, down_rows = sz.slab // 4, rf // 4
    sum_u = Reduce(
        net, at, lambda p, j: grad_w_up.at[pl.ds(p * sz.slab + j * up_rows, up_rows), :],
        bufs[0:4], 4, False, res_u,
    )
    sum_d = Reduce(
        net, at, lambda p, j: grad_w_down.at[pl.ds(p * rf + j * down_rows, down_rows), :],
        bufs[4:8], 4, False, res_d,
    )
    sum_q = Reduce(
        net, at, lambda p, j: dwq.at[pl.ds(p * sz.slab + j * up_rows, up_rows), :], bufs[8:12], 4, True, res_q
    )
    sum_o = Reduce(net, at, lambda p, j: dwo_own.at[p], bufs[12:16], 1, True, res_o)
    sum_v = Reduce(
        net, at, lambda p, j: gv.at[:, pl.ds(pl.multiple_of(p * sz.slab, sz.slab), sz.slab)],
        bufs[16:20], 1, True, res_v,
    )
    sum_u.start()
    sum_d.start()
    load_x = net.local(x_all, xs)
    load_wq = net.local(wqkv, wq)
    load_gfi = net.local(grad_first_in, gfi)
    hops = [(s, j) for s in (sum_u, sum_d) for j in range(4)]
    closes = list(hops)

    def pump(count):
        for _ in range(min(count, len(hops))):
            item, j = hops.pop(0)
            item.hop(j)

    load_wo.wait()

    def context_grad(slot):
        gather.ready(slot)
        rows = pl.ds(slot * two, two)
        dctx[rows, :] = dot_nt(gb[rows, :], wo[...]).astype(BF16)

    context_grad(0)
    gather.relay()
    context_grad(1)
    context_grad(2)
    gather.relay_last()
    pump(1)
    context_grad(3)
    load_qkv.wait()

    def attend_back(k):
        q_cols = slice(k * HD, (k + 1) * HD)
        k_cols = slice(sz.cols + k * HD, sz.cols + (k + 1) * HD)
        v_cols = slice(2 * sz.cols + k * HD, 2 * sz.cols + (k + 1) * HD)
        turned = qkv[:, k_cols].T

        def body(i):
            rows = tile(i, 256)
            queries, grads = qkv[rows, q_cols], dctx[rows, q_cols]
            scores = dot_nt(qkv[:, k_cols], queries) * SCALE
            exps = jnp.exp(scores - jnp.max(scores, axis=0, keepdims=True))
            probs = exps * (1.0 / jnp.sum(exps, axis=0, keepdims=True))
            value_part = dot(probs.astype(BF16), grads)
            slopes = probs * dot_nt(qkv[:, v_cols], grads)
            score_grads = (slopes - probs * jnp.sum(slopes, axis=0, keepdims=True)).astype(BF16)
            key_part = dot(score_grads, queries)
            first = i == 0
            dv[...] = jnp.where(first, value_part, dv[...] + value_part)
            dk[...] = jnp.where(first, key_part, dk[...] + key_part)
            dqkv[rows, q_cols] = (dot(turned, score_grads).T * SCALE).astype(BF16)

        loop(sz.rows_all // 256, body)
        dqkv[:, k_cols] = (dk[...] * SCALE).astype(BF16)
        dqkv[:, v_cols] = dv[...].astype(BF16)

    attend_back(0)
    pump(1)
    for k in range(1, sz.heads):
        attend_back(k)
    pump(1)
    load_wq.wait()

    sums = Scatter(net, at, sz, sum_bufs)
    for slot in (3, 1, 2, 0):
        rows = pl.ds(slot * two, two)

        def body(i, rows=rows, slot=slot):
            cols = tile(i, 512)
            sums.put(slot, cols, dot_nt(dqkv[rows, :], wq[cols, :]))

        loop(d // 512, body)
        sums.share(slot)
        if slot == 1:
            sums.send_diag()
    sums.send_free()
    pump(1)
    load_x.wait()
    load_ctx.wait()

    def qkv_grad(i):
        rows = tile(i, 512)
        dwq[rows, :] = dot_tn(xs[:, rows], dqkv[...]).astype(BF16)

    loop(d // 512, qkv_grad)
    sum_q.start()
    sums.send_joined()

    def out_grad(i):
        cols = tile(i, 512)
        dwo[:, cols] = dot_tn(ctx[...], gb[:, cols]).astype(BF16)

    loop(d // 512, out_grad)
    group = at.t // sz.pieces
    member = at.t - group * sz.pieces
    per = TP // sz.pieces
    wo_in = []
    for k in range(sz.heads):
        for f in range(1, sz.pieces):
            other = at.index_of(f) - group * sz.pieces
            wo_in.append(
                net.remote(
                    dwo.at[pl.ds((k * sz.pieces + other) * rw, rw), :],
                    dwo_own.at[member * sz.heads + k],
                    at.peer(f),
                )
            )
        net.local(
            dwo.at[pl.ds((k * sz.pieces + member) * rw, rw), :], dwo_own.at[member * sz.heads + k]
        ).wait()
    load_gv.wait()
    for k in range(sz.heads):
        lanes = tile((member * sz.heads + k) * per + group, HD)
        gv[0:1, lanes] = jnp.sum(dqkv[:, k * HD : (k + 1) * HD].astype(F32), axis=0, keepdims=True)
        at_v = 2 * sz.cols + k * HD
        gv[1:2, lanes] = jnp.sum(dqkv[:, at_v : at_v + HD].astype(F32), axis=0, keepdims=True)
    for copy in wo_in:
        copy.wait_recv()
    sum_o.start()
    sum_v.start()
    load_gfi.wait()
    sums.wait()

    def final(i):
        rows = tile(i, STRIP)
        ig[rows, :] = (gfi[rows, :] + sums.total(i)).astype(BF16)

    loop(t // STRIP, final)
    pump(8)
    own_rows = pl.ds(at.zh * h, h)
    net.keep(ig.at[own_rows, :], input_grad.at[at.zh])
    ig_far = net.remote(ig.at[pl.ds((1 - at.zh) * h, h), :], input_grad.at[at.zh], at.to_h)
    for j in range(4):
        sum_q.hop(j)
    sum_o.hop(0)
    sum_v.hop(0)

    for item, j in closes:
        item.close(j)
    net.keep(res_d, out_wdown)
    net.keep(res_u.at[pl.ds(at.t * rw, rw), :], out_wup.at[at.t])
    back_in = [
        net.remote(res_u.at[pl.ds(at.index_of(f) * rw, rw), :], out_wup.at[at.t], at.peer(f)) for f in flips
    ]
    for j in range(4):
        sum_q.close(j)
    net.keep(res_q.at[pl.ds(at.t * rw, rw), :], out_wqkv.at[at.t])
    back_in += [
        net.remote(res_q.at[pl.ds(at.index_of(f) * rw, rw), :], out_wqkv.at[at.t], at.peer(f)) for f in flips
    ]
    sum_o.close(0)
    net.keep(res_o, out_wo)
    sum_v.close(0)

    def lanes_of(index):
        return pl.ds(pl.multiple_of(index // sz.pieces * HD, HD), HD)

    vec_got[at.t] = res_v[0:8, lanes_of(at.t)]
    vec_in = [
        net.remote(res_v.at[pl.ds(0, 8), lanes_of(at.index_of(f))], vec_got.at[at.t], at.peer(f)) for f in flips
    ]
    bup_out[...] = res_v[8:16, 0:rf]
    net.keep(bup_out, out_bup)
    for copy in vec_in:
        copy.wait_recv()
    total = vec_got[0]
    for member in range(1, TP):
        total = total + vec_got[member]
    vec_sum[...] = total
    net.keep(vec_sum, out_vec)
    for copy in back_in:
        copy.wait_recv()
    ig_far.wait_recv()
    net.finish()


def attention_backward(sz, *args):
    t, d, r = sz.tokens, sz.width, sz.rows_all
    rw, rf = sz.row_shard, sz.hid_shard
    wide = 3 * sz.cols
    shape = jax.ShapeDtypeStruct
    anywhere = pl.BlockSpec(memory_space=pl.ANY)
    outs = (
        shape((2, sz.half, d), BF16),
        shape((TP, rw, wide), BF16),
        shape((rw, d), BF16),
        shape((TP, rw, sz.hid), BF16),
        shape((rf, d), BF16),
        shape((8, HD), F32),
        shape((8, rf), F32),
    )
    scratch = [
        pltpu.VMEM((r, d), BF16),
        pltpu.VMEM((r, d), BF16),
        pltpu.VMEM((d, wide), BF16),
        pltpu.VMEM((sz.cols, d), BF16),
        pltpu.VMEM((r, wide), BF16),
        pltpu.VMEM((r, sz.cols), BF16),
        pltpu.VMEM((t, d), F32),
        pltpu.VMEM((16, d), F32),
        pltpu.VMEM((r, sz.cols), BF16),
        pltpu.VMEM((r, wide), BF16),
        pltpu.VMEM((r, HD), F32),
        pltpu.VMEM((r, HD), F32),
        pltpu.VMEM((t, d), BF16),
        pltpu.VMEM((d, wide), BF16),
        pltpu.VMEM((sz.cols, d), BF16),
        pltpu.VMEM((sz.parts, rw, d), BF16),
        pltpu.VMEM((sz.slab, wide), BF16),
        pltpu.VMEM((rw, d), BF16),
        pltpu.VMEM((sz.slab, sz.hid), BF16),
        pltpu.VMEM((rf, d), BF16),
        pltpu.VMEM((16, sz.slab), F32),
        pltpu.VMEM((TP, 8, HD), F32),
        pltpu.VMEM((8, HD), F32),
        pltpu.VMEM((8, rf), F32),
        *Scatter.scratch(sz),
        *Reduce.scratch(sz, sz.slab, sz.hid, BF16, False),
        *Reduce.scratch(sz, rf, d, BF16, False),
        *Reduce.scratch(sz, sz.slab, wide, BF16, True),
        *Reduce.scratch(sz, rw, d, BF16, True),
        *Reduce.scratch(sz, 16, sz.slab, F32, True),
        pltpu.SemaphoreType.DMA((70 + 28 * sz.nx,)),
        pltpu.SemaphoreType.DMA((70 + 28 * sz.nx,)),
        pltpu.SemaphoreType.DMA((48,)),
    ]
    return pl.pallas_call(
        functools.partial(attention_backward_kernel, sz),
        out_shape=outs,
        in_specs=[anywhere] * 10,
        out_specs=[anywhere] * len(outs),
        scratch_shapes=scratch,
        compiler_params=pltpu.CompilerParams(
            collective_id=2, has_side_effects=True, vmem_limit_bytes=VMEM_LIMIT
        ),
        name="attention_backward",
    )(*args)


def per_device(
    sz, inputs, cotangent, w_query, w_key, w_value, w_out, b_query, b_value, b_out, ln1_gain, ln1_bias,
    w_up, b_up, w_down, b_down, ln2_gain, ln2_bias,
):
    rw, rf, d = sz.row_shard, sz.hid_shard, sz.width
    groups = TP // sz.pieces
    t = lax.axis_index("zl") * 4 + lax.axis_index("y") * 2 + lax.axis_index("c")
    p = lax.axis_index("x") * 2 + lax.axis_index("zh")

    def by_member(weight):
        split = weight.reshape(rw, sz.pieces, sz.heads, groups, HD)
        return split.transpose(3, 1, 0, 2, 4).reshape(TP, rw, sz.cols)

    wqkv_pack = jnp.concatenate([by_member(w) for w in (w_query, w_key, w_value)], axis=2)
    wup_pack = w_up.reshape(rw, sz.parts, TP, rf).transpose(2, 0, 1, 3).reshape(TP, rw, sz.hid)
    rows = jnp.stack(
        [v.astype(F32) for v in (b_query, b_value, b_out, ln1_gain, ln1_bias, b_down, ln2_gain, ln2_bias)]
    )
    low = lax.dynamic_update_slice(jnp.zeros((8, HD), F32), rows, (0, (t % sz.pieces) * rw))
    up = b_up.astype(F32)
    if rf >= HD:
        high = jnp.zeros((8, HD), F32).at[: rf // HD].set(up.reshape(rf // HD, HD))
    else:
        high = lax.dynamic_update_slice(
            jnp.zeros((8, HD), F32), up[None], (0, (p % (HD // rf)) * rf)
        )
    vec_pack = jnp.concatenate([low, high], axis=0)

    x_all, wqkv, w_out_own, up_own, down_own, vec_all, bup_all, qkv, ctx, first_in, first_all = attention_forward(
        sz, inputs, wqkv_pack, wup_pack, w_out, w_down, vec_pack
    )
    outputs, grad_first_in, grad_low, grad_up, grad_down, grad_vec = feed_forward(
        sz, first_all, first_in, up_own, down_own, vec_all, bup_all, cotangent
    )
    input_grad, out_wqkv, out_wo, out_wup, out_wdown, out_vec, out_bup = attention_backward(
        sz, grad_low, grad_first_in, x_all, wqkv, w_out_own, qkv, ctx, grad_up, grad_down, grad_vec
    )

    def by_rows(which):
        part = out_wqkv[:, :, which * sz.cols : (which + 1) * sz.cols]
        split = part.reshape(groups, sz.pieces, rw, sz.heads, HD)
        return split.transpose(2, 1, 3, 0, 4).reshape(rw, d).astype(F32)

    grad_wup = out_wup.reshape(TP, rw, sz.parts, rf).transpose(1, 2, 0, 3).reshape(rw, sz.hidden)
    vec = lax.dynamic_slice(out_vec, (0, (t % sz.pieces) * rw), (8, rw))
    return (
        outputs,
        input_grad.astype(F32),
        by_rows(0),
        by_rows(1),
        by_rows(2),
        out_wo.astype(F32),
        vec[0],
        vec[1],
        vec[2],
        vec[3],
        vec[4],
        grad_wup.astype(F32),
        out_bup[0],
        out_wdown.astype(F32),
        vec[5],
        vec[6],
        vec[7],
    )


def solution(mesh):
    nx = mesh.shape["dp"]
    plane = Mesh(mesh.devices.reshape(nx, 2, mesh.shape["hd"] // 2, 2, mesh.shape["sq"] // 2), AXES)
    rows, matrix, vector = P("x", AXES[1:], None), P(AXES, None), P(AXES)

    def run(*args):
        batch, length, width = args[0].shape
        sz = Sizes(nx, width, args[11].shape[1], batch // nx * length // (2 * TP))
        call = jax.shard_map(
            functools.partial(per_device, sz),
            mesh=plane,
            in_specs=(rows, rows) + (matrix,) * 4 + (vector,) * 5 + (matrix, vector, matrix) + (vector,) * 3,
            out_specs=(rows, rows) + (matrix,) * 4 + (vector,) * 5 + (matrix, vector, matrix) + (vector,) * 3,
            check_vma=False,
        )
        return call(*args)

    return run
```

```python
import functools

import jax
import jax.numpy as jnp
from jax import lax
from jax.experimental import pallas as pl
from jax.experimental.pallas import tpu as pltpu
from jax.sharding import Mesh
from jax.sharding import PartitionSpec as P

F32 = jnp.float32
BF16 = jnp.bfloat16
HD = 128
EPSILON = 1e-12
TP = 8
STRIP = 16
VMEM_LIMIT = 60 * 2**20
AXES = ("x", "zh", "zl", "y", "c")
SCALE = HD ** (-0.5)


class Sizes:
    def __init__(self, groups_x, width, hidden, tokens):
        self.nx = groups_x
        self.parts = 2 * groups_x
        self.width = width
        self.hidden = hidden
        self.tokens = tokens
        self.half = tokens // 2
        self.rows_all = TP * tokens
        self.row_shard = width // (TP * self.parts)
        self.hid_shard = hidden // (TP * self.parts)
        self.pieces = HD // self.row_shard
        self.heads = width // HD // TP
        self.cols = self.heads * HD
        self.hid = hidden // TP
        self.slab = width // self.parts


class Place:
    def __init__(self, sizes):
        self.x, self.zh, self.zl, self.y, self.c = (lax.axis_index(a) for a in AXES)
        self.nx = sizes.nx
        self.t = self.zl * 4 + self.y * 2 + self.c
        self.p = self.x * 2 + self.zh
        self.pz = self.x * 2 + (1 - self.zh)
        self.to_c = {"c": 1 - self.c}
        self.to_y = {"y": 1 - self.y}
        self.to_z = {"zl": 1 - self.zl}
        self.to_h = {"zh": 1 - self.zh}

    def peer(self, flip):
        target = {}
        if flip & 4:
            target["zl"] = 1 - self.zl
        if flip & 2:
            target["y"] = 1 - self.y
        if flip & 1:
            target["c"] = 1 - self.c
        return target

    def index_of(self, flip):
        zl = 1 - self.zl if flip & 4 else self.zl
        y = 1 - self.y if flip & 2 else self.y
        c = 1 - self.c if flip & 1 else self.c
        return zl * 4 + y * 2 + c

    def to_x(self, step):
        return {"x": lax.rem(self.x + step, self.nx)}

    def x_of(self, step):
        return lax.rem(self.x + step, self.nx)


class Copies:
    def __init__(self, send, recv, local):
        self.send, self.recv, self.local_sems = send, recv, local
        self.n_remote = 0
        self.n_local = 0
        self.sent = []
        self.kept = []

    def remote(self, src, dst, target):
        i = self.n_remote
        self.n_remote += 1
        copy = pltpu.make_async_remote_copy(
            src_ref=src,
            dst_ref=dst,
            send_sem=self.send.at[i],
            recv_sem=self.recv.at[i],
            device_id=target,
            device_id_type=pl.DeviceIdType.MESH,
        )
        copy.start()
        self.sent.append(copy)
        return copy

    def local(self, src, dst):
        i = self.n_local
        self.n_local += 1
        copy = pltpu.make_async_copy(src, dst, self.local_sems.at[i])
        copy.start()
        return copy

    def keep(self, src, dst):
        self.kept.append(self.local(src, dst))

    def left(self, copy):
        copy.wait_send()
        self.sent = [other for other in self.sent if other is not copy]

    def finish(self):
        for copy in self.kept:
            copy.wait()
        for copy in self.sent:
            copy.wait_send()


def greet(targets):
    barrier = pltpu.get_barrier_semaphore()
    for target in targets:
        pl.semaphore_signal(
            barrier, inc=1, device_id=target, device_id_type=pl.DeviceIdType.MESH
        )
    pl.semaphore_wait(barrier, len(targets))


def dot(left, right):
    return jnp.dot(left, right, preferred_element_type=F32)


def dot_nt(left, right):
    return lax.dot_general(left, right, (((1,), (1,)), ((), ())), preferred_element_type=F32)


def dot_tn(left, right):
    return lax.dot_general(left, right, (((0,), (0,)), ((), ())), preferred_element_type=F32)


def tile(i, size):
    return pl.ds(pl.multiple_of(i * size, size), size)


def loop(count, body):
    def step(i, carry):
        body(i)
        return carry

    lax.fori_loop(0, count, step, 0)


def normed(values):
    average = jnp.mean(values, axis=1, keepdims=True)
    centred = values - average
    variance = jnp.mean(centred * centred, axis=1, keepdims=True)
    scale = lax.rsqrt(variance + EPSILON)
    return centred * scale, scale


def normed_back(grad, xhat, scale):
    along = jnp.mean(grad * xhat, axis=1, keepdims=True)
    return scale * (grad - jnp.mean(grad, axis=1, keepdims=True) - xhat * along)


class Gather:
    def __init__(self, net, at, sz, buf, start, count, tall=False):
        self.net, self.at, self.sz, self.buf = net, at, sz, buf
        self.start, self.count, self.tall = start, count, tall
        half = sz.width // 2
        self.cols = (pl.ds(0, half), pl.ds(half, half))
        self.sib = [None] * 4

    def part(self, slot, core, cols=None):
        rows = pl.ds((slot * 2 + core) * self.sz.tokens + self.start, self.count)
        return self.buf.at[rows, :] if cols is None else self.buf.at[rows, cols]

    def send(self):
        net, at = self.net, self.at
        self.from_y = [None, None]
        self.from_z = [None, None]
        for h in (0, 1):
            self.from_y[h] = net.remote(
                self.part(0, 0, self.cols[h]), self.part(1, 0, self.cols[h]), at.to_y
            )
            self.from_z[1 - h] = net.remote(
                self.part(0, 0, self.cols[1 - h]), self.part(2, 0, self.cols[1 - h]), at.to_z
            )
        self.share(0)

    def share(self, slot):
        self.sib[slot] = self.net.remote(self.part(slot, 0), self.part(slot, 1), self.at.to_c)

    def relay(self):
        net, at = self.net, self.at
        if self.tall:
            to_y = []
            for h in (1, 0):
                self.from_z[h].wait_recv()
                to_y.append(
                    net.remote(
                        self.part(2, 0, self.cols[h]), self.part(3, 0, self.cols[h]), at.to_y
                    )
                )
            self.diag = tuple(to_y)
            self.share(2)
            for copy in self.from_y:
                copy.wait_recv()
            self.share(1)
            return
        self.from_y[0].wait_recv()
        to_z = net.remote(
            self.part(1, 0, self.cols[0]), self.part(3, 0, self.cols[0]), at.to_z
        )
        self.from_z[1].wait_recv()
        to_y = net.remote(
            self.part(2, 0, self.cols[1]), self.part(3, 0, self.cols[1]), at.to_y
        )
        self.diag = (to_z, to_y)
        self.from_y[1].wait_recv()
        self.share(1)
        self.from_z[0].wait_recv()
        self.share(2)

    def relay_last(self):
        for copy in self.diag:
            copy.wait_recv()
        self.share(3)

    def ready(self, slot):
        self.sib[slot].wait_recv()


class Scatter:
    def __init__(self, net, at, sz, bufs, tall=False):
        self.net, self.at, self.sz, self.tall = net, at, sz, tall
        self.mine, self.theirs, self.got, self.diag, self.diag_got, self.out, self.inn = bufs
        self.sib = [None] * 4

    @staticmethod
    def scratch(sz):
        t, d = sz.tokens, sz.width
        return [
            pltpu.VMEM((4 * t, d), F32),
            pltpu.VMEM((4 * t, d), BF16),
            pltpu.VMEM((4 * t, d), BF16),
            pltpu.VMEM((t, d), BF16),
            pltpu.VMEM((t, d), BF16),
            pltpu.VMEM((2 * t, d), BF16),
            pltpu.VMEM((2 * t, d), BF16),
        ]

    def put(self, slot, cols, value):
        t = self.sz.tokens
        self.mine[pl.ds(slot * t, t), cols] = value[:t]
        self.theirs[pl.ds(slot * t, t), cols] = value[t:].astype(BF16)

    def share(self, slot):
        rows = pl.ds(slot * self.sz.tokens, self.sz.tokens)
        self.sib[slot] = self.net.remote(self.theirs.at[rows, :], self.got.at[rows, :], self.at.to_c)

    def add(self, slot, start, count, dst, dst_start, extra=None):
        base = slot * self.sz.tokens + start

        def body(i):
            rows = pl.ds(pl.multiple_of(base + i * STRIP, STRIP), STRIP)
            total = self.mine[rows, :] + self.got[rows, :].astype(F32)
            if extra is not None:
                there = pl.ds(pl.multiple_of(start + i * STRIP, STRIP), STRIP)
                total = total + extra[there, :].astype(F32)
            dst[pl.ds(pl.multiple_of(dst_start + i * STRIP, STRIP), STRIP), :] = total.astype(BF16)

        loop(count // STRIP, body)

    def send_diag(self):
        net, at, h = self.net, self.at, self.sz.half
        self.sib[3].wait_recv()
        self.add(3, 0, 2 * h, self.diag, 0)
        low, high = pl.ds(0, h), pl.ds(h, h)
        self.d_low = net.remote(self.diag.at[low, :], self.diag_got.at[low, :], at.to_y)
        self.d_high = net.remote(
            self.diag.at[high, :], self.diag_got.at[high, :], at.to_y if self.tall else at.to_z
        )

    def half_out(self, side, start, target):
        rows = pl.ds(side * self.sz.tokens + start, self.sz.half)
        return self.net.remote(self.out.at[rows, :], self.inn.at[rows, :], target)

    def send_free(self):
        at, t, h = self.at, self.sz.tokens, self.sz.half
        self.sib[1].wait_recv()
        self.add(1, 0, h, self.out, 0)
        self.y_low = self.half_out(0, 0, at.to_y)
        if self.tall:
            self.add(1, h, h, self.out, h)
            self.y_high = self.half_out(0, h, at.to_y)
            return
        self.sib[2].wait_recv()
        self.add(2, h, h, self.out, t + h)
        self.z_high = self.half_out(1, h, at.to_z)

    def send_joined(self):
        at, t, h = self.at, self.sz.tokens, self.sz.half
        if self.tall:
            self.sib[2].wait_recv()
            self.d_low.wait_recv()
            self.add(2, 0, h, self.out, t, self.diag_got)
            self.z_low = self.half_out(1, 0, at.to_z)
            self.d_high.wait_recv()
            self.add(2, h, h, self.out, t + h, self.diag_got)
            self.z_high = self.half_out(1, h, at.to_z)
            return
        self.d_high.wait_recv()
        self.add(1, h, h, self.out, h, self.diag_got)
        self.y_high = self.half_out(0, h, at.to_y)
        self.d_low.wait_recv()
        self.add(2, 0, h, self.out, t, self.diag_got)
        self.z_low = self.half_out(1, 0, at.to_z)

    def settle(self):
        for copy in [*self.sib, self.d_low, self.d_high, self.y_low, self.z_high, self.y_high, self.z_low]:
            self.net.left(copy)

    def wait(self):
        self.sib[0].wait_recv()
        for copy in (self.y_low, self.z_high, self.y_high, self.z_low):
            copy.wait_recv()

    def total(self, i):
        t = self.sz.tokens
        rows = tile(i, STRIP)
        far = pl.ds(pl.multiple_of(t + i * STRIP, STRIP), STRIP)
        return (
            self.mine[rows, :]
            + self.got[rows, :].astype(F32)
            + self.inn[rows, :].astype(F32)
            + self.inn[far, :].astype(F32)
        )


class Spread:
    def __init__(self, net, at, view, source=None):
        self.net, self.at, self.view = net, at, view
        self.source = view(at.p) if source is None else source
        self.relayed = []

    def across(self):
        self.from_h = self.net.remote(self.source, self.view(self.at.p), self.at.to_h)

    def along(self):
        self.from_x = [
            self.net.remote(self.source, self.view(self.at.p), self.at.to_x(step))
            for step in range(1, self.at.nx)
        ]

    def relay(self):
        self.from_h.wait_recv()
        there = self.view(self.at.pz)
        self.relayed = [
            self.net.remote(there, there, self.at.to_x(step)) for step in range(1, self.at.nx)
        ]

    def near(self):
        for copy in self.from_x:
            copy.wait_recv()

    def far(self):
        for copy in self.relayed:
            copy.wait_recv()


def attention_forward_kernel(
    sz,
    xin, wqkv_pack, wup_pack, wout, wdown, vec_pack,
    x_all, wqkv, w_out_own, w_up, w_down, vec_all, bup_all, qkv_all, ctx_all, first_in, first_low,
    xs, wq, wo_got, wo, vecs, vec, bup, acc, qkv, ctx, fin, first, wu_own, wd_own, *rest,
):
    *sum_bufs, send, recv, local = rest
    at = Place(sz)
    net = Copies(send, recv, local)
    t, d, h = sz.tokens, sz.width, sz.half
    rw, rf = sz.row_shard, sz.hid_shard
    flips = range(1, TP)
    greet(
        [at.peer(f) for f in flips] + [at.to_h] + [at.to_x(s) for s in range(1, sz.nx)]
    )

    own_rows = pl.ds(at.zh * h, h)
    from_h = net.remote(xin.at[1 - at.zh], xs.at[own_rows, :], at.to_h)
    own_x = net.local(xin.at[at.zh], xs.at[own_rows, :])

    def wq_rows(p, member, count=1):
        return pl.ds((p * TP + member) * rw, count * rw)

    own_wq = net.local(wqkv_pack.at[at.t], wq.at[wq_rows(at.p, at.t), :])
    own_vec = net.local(vec_pack, vecs.at[at.p * TP + at.t])
    own_wo = net.local(wout, wo_got.at[at.p])
    wu_here = net.local(wup_pack.at[at.t], wu_own)
    wd_here = net.local(wdown.at[pl.ds(0, rf // 2), :], wd_own)
    wq_in = [None] + [
        net.remote(wqkv_pack.at[at.index_of(f)], wq.at[wq_rows(at.p, at.t), :], at.peer(f))
        for f in flips
    ]
    vec_in = [net.remote(vec_pack, vecs.at[at.p * TP + at.t], at.peer(f)) for f in flips]
    own_x.wait()
    near_rows = Gather(net, at, sz, xs, at.zh * h, h, tall=True)
    near_rows.send()

    def chip_block(buf, f):
        member = at.index_of(f) - at.c
        return lambda p: buf.at[wq_rows(p, member, 2), :]

    wq_spread = [Spread(net, at, chip_block(wq, f)) for f in (0, 2, 4, 6)]
    for f, item in zip((0, 2, 4, 6), wq_spread):
        if f == 0:
            own_wq.wait()
        else:
            wq_in[f].wait_recv()
        wq_in[f + 1].wait_recv()
        item.across()
        item.along()
    own_vec.wait()
    for copy in vec_in:
        copy.wait_recv()
    vec_spread = Spread(net, at, lambda p: vecs.at[pl.ds(p * TP, TP)])
    wo_spread = Spread(net, at, lambda p: wo_got.at[p], wout)
    vec_spread.across()
    vec_spread.along()
    wo_spread.along()
    from_h.wait_recv()
    far_rows = Gather(net, at, sz, xs, (1 - at.zh) * h, h, tall=True)
    far_rows.send()
    near_rows.relay()
    far_rows.relay()
    wq_spread[0].relay()
    near_rows.relay_last()
    far_rows.relay_last()
    vec_spread.relay()
    wq_spread[1].relay()
    wo_spread.across()
    wu_here.wait()
    own_wu = net.local(wu_own, w_up.at[wq_rows(at.p, at.t), :])
    wd_here.wait()
    net.keep(wd_own, w_down.at[pl.ds(at.p * (rf // 2), rf // 2), :])
    wu_in = [None] + [
        net.remote(wup_pack.at[at.index_of(f)], w_up.at[wq_rows(at.p, at.t), :], at.peer(f))
        for f in flips
    ]

    def accumulate(zh, first_part):
        def body(i):
            rows = tile(i, 256)
            total = jnp.zeros((256, 3 * sz.cols), F32) if first_part else acc[rows, :]
            for x in range(sz.nx):
                block = tile(x * 2 + zh, sz.slab)
                total = total + dot(xs[rows, block], wq[block, :])
            acc[rows, :] = total

        loop(sz.rows_all // 256, body)

    for slot in range(4):
        near_rows.ready(slot)
        far_rows.ready(slot)
    for item in wq_spread:
        item.near()
    net.keep(xs, x_all)
    accumulate(at.zh, True)
    for item in wq_spread[2:]:
        item.relay()
    wd_chunk = rf // 4
    wd_spread = [
        Spread(
            net,
            at,
            lambda p, j=j: w_down.at[pl.ds(p * 2 * wd_chunk + j * wd_chunk, wd_chunk), :],
            wdown.at[pl.ds(j * wd_chunk, wd_chunk), :],
        )
        for j in range(2)
    ]
    for item in wd_spread:
        item.across()
    vec_spread.near()
    vec_spread.far()
    for j in range(d // HD):
        piece = vecs[j * sz.pieces, 0:8]
        for k in range(1, sz.pieces):
            piece = piece + vecs[j * sz.pieces + k, 0:8]
        vec[:, j * HD : (j + 1) * HD] = piece
    if rf >= HD:
        for p in range(sz.parts):
            for j in range(rf // HD):
                lanes = pl.ds(p * rf + j * HD, HD)
                bup[0:1, lanes] = vecs[p * TP + at.t, 8 + j : 9 + j]
    else:
        for j in range(sz.hid // HD):
            each = HD // rf
            row = vecs[j * each * TP + at.t, 8:9]
            for k in range(1, each):
                row = row + vecs[(j * each + k) * TP + at.t, 8:9]
            bup[0:1, j * HD : (j + 1) * HD] = row
    net.keep(vec, vec_all)
    net.keep(bup, bup_all)
    for item in wq_spread:
        item.far()
    accumulate(1 - at.zh, False)
    wo_spread.relay()
    for item in wd_spread:
        item.along()

    group = at.t // sz.pieces
    member = at.t - group * sz.pieces
    per = TP // sz.pieces
    for k in range(sz.heads):
        head = (member * sz.heads + k) * per + group
        lanes = tile(head, HD)

        def biased(i, k=k, lanes=lanes):
            rows = tile(i, 256)
            for which in range(3):
                cols = slice(which * sz.cols + k * HD, which * sz.cols + (k + 1) * HD)
                value = acc[rows, cols]
                if which != 1:
                    value = value + vec[which // 2 : which // 2 + 1, lanes]
                qkv[rows, cols] = value.astype(BF16)

        loop(sz.rows_all // 256, biased)
    net.keep(wq, wqkv)
    net.keep(qkv, qkv_all)

    def attend(k):
        q_cols = slice(k * HD, (k + 1) * HD)
        k_cols = slice(sz.cols + k * HD, sz.cols + (k + 1) * HD)
        v_cols = slice(2 * sz.cols + k * HD, 2 * sz.cols + (k + 1) * HD)

        def body(i):
            rows = tile(i, 256)
            scores = dot_nt(qkv[rows, q_cols], qkv[:, k_cols]) * SCALE
            top = jnp.max(scores, axis=1, keepdims=True)
            exps = jnp.exp(scores - top)
            probs = exps * (1.0 / jnp.sum(exps, axis=1, keepdims=True))
            ctx[rows, q_cols] = dot(probs.astype(BF16), qkv[:, v_cols]).astype(BF16)

        loop(sz.rows_all // 256, body)

    for k in range(sz.heads):
        attend(k)
    net.keep(ctx, ctx_all)

    own_wo.wait()
    wo_spread.near()
    wo_spread.far()

    def wo_rows(k, piece):
        return pl.ds((k * sz.pieces + piece) * rw, rw)

    for k in range(sz.heads):
        net.local(wo_got.at[member * sz.heads + k], wo.at[wo_rows(k, member), :]).wait()
    wo_in = []
    for f in range(1, sz.pieces):
        other = at.index_of(f) - group * sz.pieces
        for k in range(sz.heads):
            wo_in.append(
                net.remote(wo_got.at[other * sz.heads + k], wo.at[wo_rows(k, member), :], at.peer(f))
            )
    for copy in wo_in:
        copy.wait_recv()
    net.keep(wo, w_out_own)
    wu_spread = [Spread(net, at, chip_block(w_up, f)) for f in (0, 2, 4, 6)]
    own_wu.wait()
    for f, item in zip((0, 2, 4, 6), wu_spread):
        if f:
            wu_in[f].wait_recv()
        wu_in[f + 1].wait_recv()
        item.across()
    for item in wu_spread:
        item.along()

    sums = Scatter(net, at, sz, sum_bufs, tall=True)
    for slot in (3, 1, 2, 0):
        rows = pl.ds(slot * 2 * t, 2 * t)

        def body(i, rows=rows, slot=slot):
            cols = tile(i, 512)
            sums.put(slot, cols, dot(ctx[rows, :], wo[:, cols]))

        loop(d // 512, body)
        sums.share(slot)
        if slot == 3:
            sums.send_diag()
    sums.send_free()
    sums.send_joined()
    for item in wd_spread:
        item.relay()
    sums.wait()

    def norm(i):
        rows = tile(i, STRIP)
        value = xs[rows, :].astype(F32) + sums.total(i) + vec[2:3, :]
        fin[rows, :] = value
        xhat, _ = normed(value)
        first[rows, :] = (xhat * vec[3:4, :] + vec[4:5, :]).astype(BF16)

    loop(t // STRIP, norm)
    net.keep(fin, first_in)
    net.keep(first, first_low)
    for item in wu_spread:
        item.relay()
    for item in wu_spread + wd_spread:
        item.near()
        item.far()
    net.finish()


def attention_forward(sz, xin, wqkv_pack, wup_pack, wout, wdown, vec_pack):
    t, d, r = sz.tokens, sz.width, sz.rows_all
    shape = jax.ShapeDtypeStruct
    anywhere = pl.BlockSpec(memory_space=pl.ANY)
    outs = (
        shape((r, d), BF16),
        shape((d, 3 * sz.cols), BF16),
        shape((sz.cols, d), BF16),
        shape((d, sz.hid), BF16),
        shape((sz.hid // 2, d), BF16),
        shape((8, d), F32),
        shape((8, sz.hid), F32),
        shape((r, 3 * sz.cols), BF16),
        shape((r, sz.cols), BF16),
        shape((t, d), F32),
        shape((t, d), BF16),
    )
    scratch = [
        pltpu.VMEM((r, d), BF16),
        pltpu.VMEM((d, 3 * sz.cols), BF16),
        pltpu.VMEM((sz.parts, sz.row_shard, d), BF16),
        pltpu.VMEM((sz.cols, d), BF16),
        pltpu.VMEM((sz.parts * TP, 16, HD), F32),
        pltpu.VMEM((8, d), F32),
        pltpu.VMEM((8, sz.hid), F32),
        pltpu.VMEM((r, 3 * sz.cols), F32),
        pltpu.VMEM((r, 3 * sz.cols), BF16),
        pltpu.VMEM((r, sz.cols), BF16),
        pltpu.VMEM((t, d), F32),
        pltpu.VMEM((t, d), BF16),
        pltpu.VMEM((sz.row_shard, sz.hid), BF16),
        pltpu.VMEM((sz.hid_shard // 2, d), BF16),
        *Scatter.scratch(sz),
        pltpu.SemaphoreType.DMA((80 + 28 * sz.nx,)),
        pltpu.SemaphoreType.DMA((80 + 28 * sz.nx,)),
        pltpu.SemaphoreType.DMA((24,)),
    ]
    return pl.pallas_call(
        functools.partial(attention_forward_kernel, sz),
        out_shape=outs,
        in_specs=[anywhere] * 6,
        out_specs=[anywhere] * len(outs),
        scratch_shapes=scratch,
        compiler_params=pltpu.CompilerParams(
            collective_id=0, has_side_effects=True, vmem_limit_bytes=VMEM_LIMIT
        ),
        name="attention_forward",
    )(xin, wqkv_pack, wup_pack, wout, wdown, vec_pack)


GELU_A = 0.7978845608028654
GELU_B = 0.044715


def gate(values):
    inner = jnp.tanh(GELU_A * (values + GELU_B * values * values * values))
    return 0.5 * values * (1.0 + inner)


def gate_slope(values):
    square = values * values
    inner = jnp.tanh(GELU_A * (values + GELU_B * square * values))
    rise = GELU_A * (1.0 + 3.0 * GELU_B * square)
    return 0.5 * (1.0 + inner) + 0.5 * values * (1.0 - inner * inner) * rise


def feed_forward_kernel(
    sz,
    first_low, first_in, w_up, w_down_half, vec_all, bup_all, cot_in, wdown,
    outputs, grad_first_in, grad_low, grad_w_up, grad_w_down, grad_vec, down_sum, down_in,
    fa, wu, wd, vec, bup, fin, cot, hid, act, gh, g2, g2s, out, gv, dwu, dwd, *rest,
):
    *bufs, send, recv, local = rest
    sum_bufs, bufs = bufs[:7], bufs[7:]
    at = Place(sz)
    net = Copies(send, recv, local)
    t, d, h = sz.tokens, sz.width, sz.half
    two = 2 * t
    rf = sz.hid_shard
    load_first = net.local(first_low, fa.at[pl.ds(0, t), :])
    load_up = net.local(w_up, wu)
    load_bup = net.local(bup_all, bup)
    load_down = [
        net.local(w_down_half.at[pl.ds(p * (rf // 2), rf // 2), :], wd.at[pl.ds(p * rf, rf // 2), :])
        for p in range(sz.parts)
    ]
    late_own = pl.ds(at.p * rf + rf // 2, rf // 2)
    load_down.append(net.local(wdown.at[pl.ds(rf // 2, rf // 2), :], wd.at[late_own, :]))
    load_vec = net.local(vec_all, vec)
    load_fin = net.local(first_in, fin)
    own_rows = pl.ds(at.zh * h, h)
    load_cot = net.local(cot_in.at[at.zh], cot.at[own_rows, :])
    greet([at.to_c, at.to_y, at.to_z, at.to_h] + [at.to_x(s) for s in range(1, sz.nx)])
    load_first.wait()
    firsts = Gather(net, at, sz, fa, 0, t, tall=True)
    firsts.send()
    wd_chunk = rf // 4
    wd_spread = [
        Spread(
            net,
            at,
            lambda p, j=j: wd.at[pl.ds(p * rf + j * wd_chunk, wd_chunk), :],
            wdown.at[pl.ds(j * wd_chunk, wd_chunk), :],
        )
        for j in (2, 3)
    ]
    for item in wd_spread:
        item.across()
        item.along()
    gv[...] = jnp.zeros_like(gv)

    sums = Scatter(net, at, sz, sum_bufs)
    load_up.wait()
    load_bup.wait()

    def project_up(slot):
        firsts.ready(slot)
        rows = pl.ds(slot * two, two)

        def up(i):
            cols = tile(i, 512)
            value = dot(fa[rows, :], wu[:, cols]) + bup[0:1, cols]
            hid[rows, cols] = value
            act[rows, cols] = gate(value).astype(BF16)

        loop(sz.hid // 512, up)

    project_up(0)
    firsts.relay()
    wd_spread[0].relay()
    project_up(2)
    project_up(1)
    firsts.relay_last()
    project_up(3)
    wd_spread[1].relay()
    cot_far = net.remote(cot_in.at[1 - at.zh], cot.at[own_rows, :], at.to_h)
    for copy in load_down:
        copy.wait()
    for item in wd_spread:
        item.near()
        item.far()
    for slot in (3, 1, 2, 0):
        rows = pl.ds(slot * two, two)

        def down(i, rows=rows, slot=slot):
            cols = tile(i, 512)
            sums.put(slot, cols, dot(act[rows, :], wd[:, cols]))

        loop(d // 512, down)
        sums.share(slot)
        if slot == 1:
            sums.send_diag()
    sums.send_free()
    sums.send_joined()
    load_vec.wait()
    load_fin.wait()
    load_cot.wait()
    cot_far.wait_recv()
    sums.wait()

    def strip_sum(row, value):
        gv[row : row + 1, :] = gv[row : row + 1, :] + jnp.sum(value, axis=0, keepdims=True)

    def second_norm(i):
        rows = tile(i, STRIP)
        xhat, _ = normed(fin[rows, :])
        value = xhat * vec[3:4, :] + vec[4:5, :] + sums.total(i) + vec[5:6, :]
        xhat, scale = normed(value)
        out[rows, :] = (xhat * vec[6:7, :] + vec[7:8, :]).astype(BF16)
        grad = cot[rows, :].astype(F32)
        strip_sum(6, grad * xhat)
        strip_sum(7, grad)
        grad = normed_back(grad * vec[6:7, :], xhat, scale)
        g2s[rows, :] = grad
        low = grad.astype(BF16)
        g2[rows, :] = low
        strip_sum(5, low.astype(F32))

    loop(t // STRIP, second_norm)
    gather = Gather(net, at, sz, g2, 0, t)
    gather.send()
    net.keep(out.at[own_rows, :], outputs.at[at.zh])
    out_far = net.remote(out.at[pl.ds((1 - at.zh) * h, h), :], outputs.at[at.zh], at.to_h)
    sums.settle()

    def back(slot):
        gather.ready(slot)
        rows = pl.ds(slot * two, two)

        def down(i):
            cols = tile(i, 512)
            value = dot_nt(g2[rows, :], wd[cols, :])
            gh[rows, cols] = (value * gate_slope(hid[rows, cols])).astype(BF16)

        loop(sz.hid // 512, down)

        def up(i):
            cols = tile(i, 512)
            sums.put(slot, cols, dot_nt(gh[rows, :], wu[cols, :]))

        loop(d // 512, up)
        sums.share(slot)

    back(0)
    gather.relay()
    back(1)
    back(2)
    sums.send_free()
    gather.relay_last()
    back(3)
    sums.send_diag()

    def down_grad(i):
        rows, cols = tile(i // (d // 512), 512), tile(i % (d // 512), 512)
        dwd[rows, cols] = dot_tn(act[:, rows], g2[:, cols]).astype(BF16)

    loop((sz.hid // 512) * (d // 512), down_grad)
    net.keep(dwd, grad_w_down)
    down_rows = sz.hid_shard // 4
    sum_d = Reduce(
        net, at, lambda p, j: dwd.at[pl.ds(p * sz.hid_shard + j * down_rows, down_rows), :], bufs, 4, True, None
    )
    sum_d.start(0)
    sums.send_joined()
    sum_d.hop(0)

    def up_grad(i):
        rows, cols = tile(i // (sz.hid // 512), 512), tile(i % (sz.hid // 512), 512)
        dwu[rows, cols] = dot_tn(fa[:, rows], gh[:, cols]).astype(BF16)

    loop((sz.hid // 512) * (d // 512), up_grad)
    net.keep(dwu, grad_w_up)
    sum_d.hop(1)
    for p in range(sz.parts):
        rf = sz.hid_shard
        gv[8:9, p * sz.slab : p * sz.slab + rf] = jnp.sum(
            gh[:, p * rf : (p + 1) * rf].astype(F32), axis=0, keepdims=True
        )
    sums.wait()

    def first_norm(i):
        rows = tile(i, STRIP)
        xhat, scale = normed(fin[rows, :])
        grad = g2s[rows, :] + sums.total(i)
        strip_sum(3, grad * xhat)
        strip_sum(4, grad)
        grad = normed_back(grad * vec[3:4, :], xhat, scale)
        g2s[rows, :] = grad
        low = grad.astype(BF16)
        out_low[rows, :] = low
        strip_sum(2, low.astype(F32))

    out_low = cot
    loop(t // STRIP, first_norm)
    net.keep(g2s, grad_first_in)
    net.keep(out_low, grad_low)
    net.keep(gv, grad_vec)
    for j in (2, 3):
        sum_d.add(j)
    late = pl.ds(2 * down_rows, 2 * down_rows)
    early = pl.ds(0, 2 * down_rows)
    net.keep(sum_d.out.at[late, :], down_sum)
    for j in (0, 1):
        sum_d.from_h[j].wait_recv()
    net.keep(sum_d.inn.at[early, :], down_in)
    out_far.wait_recv()
    net.finish()


def feed_forward(sz, *args):
    t, d, r = sz.tokens, sz.width, sz.rows_all
    shape = jax.ShapeDtypeStruct
    anywhere = pl.BlockSpec(memory_space=pl.ANY)
    outs = (
        shape((2, sz.half, d), BF16),
        shape((t, d), F32),
        shape((t, d), BF16),
        shape((d, sz.hid), BF16),
        shape((sz.hid, d), BF16),
        shape((16, d), F32),
        shape((sz.hid_shard // 2, d), BF16),
        shape((sz.hid_shard // 2, d), BF16),
    )
    scratch = [
        pltpu.VMEM((r, d), BF16),
        pltpu.VMEM((d, sz.hid), BF16),
        pltpu.VMEM((sz.hid, d), BF16),
        pltpu.VMEM((8, d), F32),
        pltpu.VMEM((8, sz.hid), F32),
        pltpu.VMEM((t, d), F32),
        pltpu.VMEM((t, d), BF16),
        pltpu.VMEM((r, sz.hid), F32),
        pltpu.VMEM((r, sz.hid), BF16),
        pltpu.VMEM((r, sz.hid), BF16),
        pltpu.VMEM((r, d), BF16),
        pltpu.VMEM((t, d), F32),
        pltpu.VMEM((t, d), BF16),
        pltpu.VMEM((16, d), F32),
        pltpu.VMEM((d, sz.hid), BF16),
        pltpu.VMEM((sz.hid, d), BF16),
        *Scatter.scratch(sz),
        *Reduce.scratch(sz, sz.hid_shard, d, BF16, True, 1),
        pltpu.SemaphoreType.DMA((64 + 8 * sz.nx,)),
        pltpu.SemaphoreType.DMA((64 + 8 * sz.nx,)),
        pltpu.SemaphoreType.DMA((24,)),
    ]
    return pl.pallas_call(
        functools.partial(feed_forward_kernel, sz),
        out_shape=outs,
        in_specs=[anywhere] * 8,
        out_specs=[anywhere] * len(outs),
        scratch_shapes=scratch,
        compiler_params=pltpu.CompilerParams(
            collective_id=1, has_side_effects=True, vmem_limit_bytes=VMEM_LIMIT
        ),
        name="feed_forward",
    )(*args)


class Reduce:
    def __init__(self, net, at, view, bufs, chunks, held, result):
        self.net, self.at, self.view, self.chunks = net, at, view, chunks
        self.got, self.own, self.out, self.inn = bufs
        self.rows = self.out.shape[0] // chunks
        self.result = result
        self.held = held
        self.groups = (at.x * 2 + (1 - at.zh), at.x * 2 + at.zh)
        self.from_x, self.from_h, self.loads = {}, {}, {}

    @staticmethod
    def scratch(sz, rows, cols, dtype, held, kinds=2):
        return [
            pltpu.VMEM((sz.nx - 1, kinds, rows, cols), dtype),
            pltpu.VMEM((2, 8, 128) if held else (2, rows, cols), dtype),
            pltpu.VMEM((rows, cols), dtype),
            pltpu.VMEM((rows, cols), dtype),
        ]

    def chunk(self, j):
        return pl.ds(j * self.rows, self.rows)

    def start(self, which):
        at, net = self.at, self.net
        zh = 1 - at.zh if which == 0 else at.zh
        for j in range(self.chunks):
            for step in range(1, at.nx):
                p = at.x_of(step) * 2 + zh
                self.from_x[which, j, step] = net.remote(
                    self.view(p, j), self.got.at[step - 1, which, self.chunk(j), :], at.to_x(step)
                )
            if not self.held:
                self.loads[which, j] = net.local(
                    self.view(self.groups[which], j), self.own.at[which, self.chunk(j), :]
                )

    def term(self, which, j, i):
        rows = pl.ds(pl.multiple_of(j * self.rows + i * STRIP, STRIP), STRIP)
        if self.held:
            total = self.view(self.groups[which], j)[tile(i, STRIP), :].astype(F32)
        else:
            total = self.own[which, rows, :].astype(F32)
        for step in range(1, self.at.nx):
            total = total + self.got[step - 1, which, rows, :].astype(F32)
        return rows, total

    def ready(self, which, j):
        for step in range(1, self.at.nx):
            self.from_x[which, j, step].wait_recv()
        if not self.held:
            self.loads[which, j].wait()

    def add(self, j):
        self.ready(0, j)

        def body(i):
            rows, total = self.term(0, j, i)
            self.out[rows, :] = total.astype(self.out.dtype)

        loop(self.rows // STRIP, body)

    def hop(self, j):
        self.add(j)
        self.send(j)

    def send(self, j):
        self.from_h[j] = self.net.remote(
            self.out.at[self.chunk(j), :], self.inn.at[self.chunk(j), :], self.at.to_h
        )

    def close(self, j):
        self.ready(1, j)
        if j in self.from_h:
            self.from_h[j].wait_recv()

        def body(i):
            rows, total = self.term(1, j, i)
            self.result[rows, :] = (total + self.inn[rows, :].astype(F32)).astype(self.result.dtype)

        loop(self.rows // STRIP, body)


def attention_backward_kernel(
    sz,
    grad_low, grad_first_in, x_all, wqkv, w_out_own, qkv_all, ctx_all, grad_w_up, grad_w_down, grad_vec, down_sum, down_in,
    input_grad, out_wqkv, out_wo, out_wup, out_wdown, out_vec, out_bup,
    gb, xs, wq, wo, qkv, ctx, gfi, gv, dctx, dqkv, dk, dv, ig, dwq, dwo, dwo_own, res_q, res_o, res_u, res_d, res_v,
    vec_got, vec_sum, bup_out, *rest,
):
    *bufs, send, recv, local = rest
    sum_bufs, bufs = bufs[:7], bufs[7:]
    at = Place(sz)
    net = Copies(send, recv, local)
    t, d, h = sz.tokens, sz.width, sz.half
    two = 2 * t
    rw, rf = sz.row_shard, sz.hid_shard
    flips = range(1, TP)
    load_gb = net.local(grad_low, gb.at[pl.ds(0, t), :])
    load_wo = net.local(w_out_own, wo)
    load_qkv = net.local(qkv_all, qkv)
    load_ctx = net.local(ctx_all, ctx)
    load_gv = net.local(grad_vec, gv)
    greet([at.peer(f) for f in flips] + [at.to_h] + [at.to_x(s) for s in range(1, sz.nx)])
    load_gb.wait()
    gather = Gather(net, at, sz, gb, 0, t, tall=True)
    gather.send()

    up_rows, down_rows = sz.slab // 4, rf // 4
    sum_u = Reduce(
        net, at, lambda p, j: grad_w_up.at[pl.ds(p * sz.slab + j * up_rows, up_rows), :],
        bufs[0:4], 4, False, res_u,
    )
    sum_d = Reduce(
        net, at, lambda p, j: grad_w_down.at[pl.ds(p * rf + j * down_rows, down_rows), :],
        bufs[4:8], 4, False, res_d,
    )
    sum_q = Reduce(
        net, at, lambda p, j: dwq.at[pl.ds(p * sz.slab + j * up_rows, up_rows), :], bufs[8:12], 4, True, res_q
    )
    sum_o = Reduce(net, at, lambda p, j: dwo_own.at[p], bufs[12:16], 1, True, res_o)
    sum_v = Reduce(
        net, at, lambda p, j: gv.at[:, pl.ds(pl.multiple_of(p * sz.slab, sz.slab), sz.slab)],
        bufs[16:20], 1, True, res_v,
    )
    late = pl.ds(2 * down_rows, 2 * down_rows)
    load_sum = net.local(down_sum, sum_d.out.at[late, :])
    load_in = net.local(down_in, sum_d.inn.at[pl.ds(0, 2 * down_rows), :])
    sum_u.start(0)
    load_sum.wait()
    for j in (2, 3):
        sum_d.send(j)
    sum_u.start(1)
    load_x = net.local(x_all, xs)
    load_wq = net.local(wqkv, wq)
    load_gfi = net.local(grad_first_in, gfi)
    hops = [(sum_u, j) for j in range(4)]
    closes = [(s, j) for s in (sum_u, sum_d) for j in range(4)]

    def pump(count):
        for _ in range(min(count, len(hops))):
            item, j = hops.pop(0)
            item.hop(j)

    load_wo.wait()

    def context_grad(slot):
        gather.ready(slot)
        rows = pl.ds(slot * two, two)
        dctx[rows, :] = dot_nt(gb[rows, :], wo[...]).astype(BF16)

    context_grad(0)
    gather.relay()
    pump(1)
    context_grad(1)
    context_grad(2)
    gather.relay_last()
    pump(1)
    context_grad(3)
    pump(1)
    load_qkv.wait()

    def attend_back(k):
        q_cols = slice(k * HD, (k + 1) * HD)
        k_cols = slice(sz.cols + k * HD, sz.cols + (k + 1) * HD)
        v_cols = slice(2 * sz.cols + k * HD, 2 * sz.cols + (k + 1) * HD)
        turned = qkv[:, k_cols].T

        def body(i):
            rows = tile(i, 256)
            queries, grads = qkv[rows, q_cols], dctx[rows, q_cols]
            scores = dot_nt(qkv[:, k_cols], queries) * SCALE
            exps = jnp.exp(scores - jnp.max(scores, axis=0, keepdims=True))
            probs = exps * (1.0 / jnp.sum(exps, axis=0, keepdims=True))
            value_part = dot(probs.astype(BF16), grads)
            slopes = probs * dot_nt(qkv[:, v_cols], grads)
            score_grads = (slopes - probs * jnp.sum(slopes, axis=0, keepdims=True)).astype(BF16)
            key_part = dot(score_grads, queries)
            first = i == 0
            dv[...] = jnp.where(first, value_part, dv[...] + value_part)
            dk[...] = jnp.where(first, key_part, dk[...] + key_part)
            dqkv[rows, q_cols] = (dot(turned, score_grads).T * SCALE).astype(BF16)

        loop(sz.rows_all // 256, body)
        dqkv[:, k_cols] = (dk[...] * SCALE).astype(BF16)
        dqkv[:, v_cols] = dv[...].astype(BF16)

    attend_back(0)
    pump(2)
    for k in range(1, sz.heads):
        attend_back(k)
    pump(2)
    load_wq.wait()

    sums = Scatter(net, at, sz, sum_bufs, tall=True)
    for slot in (3, 1, 2, 0):
        rows = pl.ds(slot * two, two)

        def body(i, rows=rows, slot=slot):
            cols = tile(i, 512)
            sums.put(slot, cols, dot_nt(dqkv[rows, :], wq[cols, :]))

        loop(d // 512, body)
        sums.share(slot)
        if slot == 1:
            sums.send_diag()
    sums.send_free()
    pump(1)
    load_x.wait()
    load_ctx.wait()

    def qkv_grad(i):
        rows = tile(i, 512)
        dwq[rows, :] = dot_tn(xs[:, rows], dqkv[...]).astype(BF16)

    loop(d // 512, qkv_grad)
    sum_q.start(0)
    sum_d.start(1)
    sums.send_joined()

    def out_grad(i):
        cols = tile(i, 512)
        dwo[:, cols] = dot_tn(ctx[...], gb[:, cols]).astype(BF16)

    loop(d // 512, out_grad)
    group = at.t // sz.pieces
    member = at.t - group * sz.pieces
    per = TP // sz.pieces
    wo_in = []
    for k in range(sz.heads):
        for f in range(1, sz.pieces):
            other = at.index_of(f) - group * sz.pieces
            wo_in.append(
                net.remote(
                    dwo.at[pl.ds((k * sz.pieces + other) * rw, rw), :],
                    dwo_own.at[member * sz.heads + k],
                    at.peer(f),
                )
            )
        net.local(
            dwo.at[pl.ds((k * sz.pieces + member) * rw, rw), :], dwo_own.at[member * sz.heads + k]
        ).wait()
    load_gv.wait()
    for k in range(sz.heads):
        lanes = tile((member * sz.heads + k) * per + group, HD)
        gv[0:1, lanes] = jnp.sum(dqkv[:, k * HD : (k + 1) * HD].astype(F32), axis=0, keepdims=True)
        at_v = 2 * sz.cols + k * HD
        gv[1:2, lanes] = jnp.sum(dqkv[:, at_v : at_v + HD].astype(F32), axis=0, keepdims=True)
    for copy in wo_in:
        copy.wait_recv()
    sum_o.start(0)
    sum_v.start(0)
    sum_q.hop(0)
    sum_q.start(1)
    sum_o.start(1)
    sum_v.start(1)
    load_gfi.wait()
    sum_q.hop(1)
    sums.wait()

    def final(i):
        rows = tile(i, STRIP)
        ig[rows, :] = (gfi[rows, :] + sums.total(i)).astype(BF16)

    loop(t // STRIP, final)
    own_rows = pl.ds(at.zh * h, h)
    net.keep(ig.at[own_rows, :], input_grad.at[at.zh])
    ig_far = net.remote(ig.at[pl.ds((1 - at.zh) * h, h), :], input_grad.at[at.zh], at.to_h)
    for j in (2, 3):
        sum_q.hop(j)
    sum_o.hop(0)
    sum_v.hop(0)
    load_in.wait()

    for item, j in closes:
        item.close(j)
    net.keep(res_d, out_wdown)
    net.keep(res_u.at[pl.ds(at.t * rw, rw), :], out_wup.at[at.t])
    back_in = [
        net.remote(res_u.at[pl.ds(at.index_of(f) * rw, rw), :], out_wup.at[at.t], at.peer(f)) for f in flips
    ]
    for j in range(4):
        sum_q.close(j)
    net.keep(res_q.at[pl.ds(at.t * rw, rw), :], out_wqkv.at[at.t])
    back_in += [
        net.remote(res_q.at[pl.ds(at.index_of(f) * rw, rw), :], out_wqkv.at[at.t], at.peer(f)) for f in flips
    ]
    sum_o.close(0)
    net.keep(res_o, out_wo)
    sum_v.close(0)

    def lanes_of(index):
        return pl.ds(pl.multiple_of(index // sz.pieces * HD, HD), HD)

    vec_got[at.t] = res_v[0:8, lanes_of(at.t)]
    vec_in = [
        net.remote(res_v.at[pl.ds(0, 8), lanes_of(at.index_of(f))], vec_got.at[at.t], at.peer(f)) for f in flips
    ]
    bup_out[...] = res_v[8:16, 0:rf]
    net.keep(bup_out, out_bup)
    for copy in vec_in:
        copy.wait_recv()
    total = vec_got[0]
    for member in range(1, TP):
        total = total + vec_got[member]
    vec_sum[...] = total
    net.keep(vec_sum, out_vec)
    for copy in back_in:
        copy.wait_recv()
    ig_far.wait_recv()
    net.finish()


def attention_backward(sz, *args):
    t, d, r = sz.tokens, sz.width, sz.rows_all
    rw, rf = sz.row_shard, sz.hid_shard
    wide = 3 * sz.cols
    shape = jax.ShapeDtypeStruct
    anywhere = pl.BlockSpec(memory_space=pl.ANY)
    outs = (
        shape((2, sz.half, d), BF16),
        shape((TP, rw, wide), BF16),
        shape((rw, d), BF16),
        shape((TP, rw, sz.hid), BF16),
        shape((rf, d), BF16),
        shape((8, HD), F32),
        shape((8, rf), F32),
    )
    scratch = [
        pltpu.VMEM((r, d), BF16),
        pltpu.VMEM((r, d), BF16),
        pltpu.VMEM((d, wide), BF16),
        pltpu.VMEM((sz.cols, d), BF16),
        pltpu.VMEM((r, wide), BF16),
        pltpu.VMEM((r, sz.cols), BF16),
        pltpu.VMEM((t, d), F32),
        pltpu.VMEM((16, d), F32),
        pltpu.VMEM((r, sz.cols), BF16),
        pltpu.VMEM((r, wide), BF16),
        pltpu.VMEM((r, HD), F32),
        pltpu.VMEM((r, HD), F32),
        pltpu.VMEM((t, d), BF16),
        pltpu.VMEM((d, wide), BF16),
        pltpu.VMEM((sz.cols, d), BF16),
        pltpu.VMEM((sz.parts, rw, d), BF16),
        pltpu.VMEM((sz.slab, wide), BF16),
        pltpu.VMEM((rw, d), BF16),
        pltpu.VMEM((sz.slab, sz.hid), BF16),
        pltpu.VMEM((rf, d), BF16),
        pltpu.VMEM((16, sz.slab), F32),
        pltpu.VMEM((TP, 8, HD), F32),
        pltpu.VMEM((8, HD), F32),
        pltpu.VMEM((8, rf), F32),
        *Scatter.scratch(sz),
        *Reduce.scratch(sz, sz.slab, sz.hid, BF16, False),
        *Reduce.scratch(sz, rf, d, BF16, False),
        *Reduce.scratch(sz, sz.slab, wide, BF16, True),
        *Reduce.scratch(sz, rw, d, BF16, True),
        *Reduce.scratch(sz, 16, sz.slab, F32, True),
        pltpu.SemaphoreType.DMA((70 + 28 * sz.nx,)),
        pltpu.SemaphoreType.DMA((70 + 28 * sz.nx,)),
        pltpu.SemaphoreType.DMA((48,)),
    ]
    return pl.pallas_call(
        functools.partial(attention_backward_kernel, sz),
        out_shape=outs,
        in_specs=[anywhere] * 12,
        out_specs=[anywhere] * len(outs),
        scratch_shapes=scratch,
        compiler_params=pltpu.CompilerParams(
            collective_id=2, has_side_effects=True, vmem_limit_bytes=VMEM_LIMIT
        ),
        name="attention_backward",
    )(*args)


def per_device(
    sz, inputs, cotangent, w_query, w_key, w_value, w_out, b_query, b_value, b_out, ln1_gain, ln1_bias,
    w_up, b_up, w_down, b_down, ln2_gain, ln2_bias,
):
    rw, rf, d = sz.row_shard, sz.hid_shard, sz.width
    groups = TP // sz.pieces
    t = lax.axis_index("zl") * 4 + lax.axis_index("y") * 2 + lax.axis_index("c")
    p = lax.axis_index("x") * 2 + lax.axis_index("zh")

    def by_member(weight):
        split = weight.reshape(rw, sz.pieces, sz.heads, groups, HD)
        return split.transpose(3, 1, 0, 2, 4).reshape(TP, rw, sz.cols)

    wqkv_pack = jnp.concatenate([by_member(w) for w in (w_query, w_key, w_value)], axis=2)
    wup_pack = w_up.reshape(rw, sz.parts, TP, rf).transpose(2, 0, 1, 3).reshape(TP, rw, sz.hid)
    rows = jnp.stack(
        [v.astype(F32) for v in (b_query, b_value, b_out, ln1_gain, ln1_bias, b_down, ln2_gain, ln2_bias)]
    )
    low = lax.dynamic_update_slice(jnp.zeros((8, HD), F32), rows, (0, (t % sz.pieces) * rw))
    up = b_up.astype(F32)
    if rf >= HD:
        high = jnp.zeros((8, HD), F32).at[: rf // HD].set(up.reshape(rf // HD, HD))
    else:
        high = lax.dynamic_update_slice(
            jnp.zeros((8, HD), F32), up[None], (0, (p % (HD // rf)) * rf)
        )
    vec_pack = jnp.concatenate([low, high], axis=0)

    x_all, wqkv, w_out_own, up_own, down_own, vec_all, bup_all, qkv, ctx, first_in, first_low = attention_forward(
        sz, inputs, wqkv_pack, wup_pack, w_out, w_down, vec_pack
    )
    outputs, grad_first_in, grad_low, grad_up, grad_down, grad_vec, down_sum, down_in = feed_forward(
        sz, first_low, first_in, up_own, down_own, vec_all, bup_all, cotangent, w_down
    )
    input_grad, out_wqkv, out_wo, out_wup, out_wdown, out_vec, out_bup = attention_backward(
        sz, grad_low, grad_first_in, x_all, wqkv, w_out_own, qkv, ctx, grad_up, grad_down, grad_vec, down_sum, down_in
    )

    def by_rows(which):
        part = out_wqkv[:, :, which * sz.cols : (which + 1) * sz.cols]
        split = part.reshape(groups, sz.pieces, rw, sz.heads, HD)
        return split.transpose(2, 1, 3, 0, 4).reshape(rw, d).astype(F32)

    grad_wup = out_wup.reshape(TP, rw, sz.parts, rf).transpose(1, 2, 0, 3).reshape(rw, sz.hidden)
    vec = lax.dynamic_slice(out_vec, (0, (t % sz.pieces) * rw), (8, rw))
    return (
        outputs,
        input_grad.astype(F32),
        by_rows(0),
        by_rows(1),
        by_rows(2),
        out_wo.astype(F32),
        vec[0],
        vec[1],
        vec[2],
        vec[3],
        vec[4],
        grad_wup.astype(F32),
        out_bup[0],
        out_wdown.astype(F32),
        vec[5],
        vec[6],
        vec[7],
    )


def solution(mesh):
    nx = mesh.shape["dp"]
    plane = Mesh(mesh.devices.reshape(nx, 2, mesh.shape["hd"] // 2, 2, mesh.shape["sq"] // 2), AXES)
    rows, matrix, vector = P("x", AXES[1:], None), P(AXES, None), P(AXES)

    def run(*args):
        batch, length, width = args[0].shape
        sz = Sizes(nx, width, args[11].shape[1], batch // nx * length // (2 * TP))
        call = jax.shard_map(
            functools.partial(per_device, sz),
            mesh=plane,
            in_specs=(rows, rows) + (matrix,) * 4 + (vector,) * 5 + (matrix, vector, matrix) + (vector,) * 3,
            out_specs=(rows, rows) + (matrix,) * 4 + (vector,) * 5 + (matrix, vector, matrix) + (vector,) * 3,
            check_vma=False,
        )
        return call(*args)

    return run
```

```python
import functools

import jax
import jax.numpy as jnp
from jax import lax
from jax.experimental import pallas as pl
from jax.experimental.pallas import tpu as pltpu
from jax.sharding import Mesh
from jax.sharding import PartitionSpec as P

F32 = jnp.float32
BF16 = jnp.bfloat16
HD = 128
EPSILON = 1e-12
TP = 8
STRIP = 16
VMEM_LIMIT = 60 * 2**20
AXES = ("x", "zh", "zl", "y", "c")
SCALE = HD ** (-0.5)


class Sizes:
    def __init__(self, groups_x, width, hidden, tokens):
        self.nx = groups_x
        self.parts = 2 * groups_x
        self.width = width
        self.hidden = hidden
        self.tokens = tokens
        self.half = tokens // 2
        self.rows_all = TP * tokens
        self.row_shard = width // (TP * self.parts)
        self.hid_shard = hidden // (TP * self.parts)
        self.pieces = HD // self.row_shard
        self.heads = width // HD // TP
        self.cols = self.heads * HD
        self.hid = hidden // TP
        self.slab = width // self.parts
        self.by_lanes = self.hid_shard % HD == 0


class Place:
    def __init__(self, sizes):
        self.x, self.zh, self.zl, self.y, self.c = (lax.axis_index(a) for a in AXES)
        self.nx = sizes.nx
        self.t = self.zl * 4 + self.y * 2 + self.c
        self.p = self.x * 2 + self.zh
        self.pz = self.x * 2 + (1 - self.zh)
        self.to_c = {"c": 1 - self.c}
        self.to_y = {"y": 1 - self.y}
        self.to_z = {"zl": 1 - self.zl}
        self.to_h = {"zh": 1 - self.zh}

    def peer(self, flip):
        target = {}
        if flip & 4:
            target["zl"] = 1 - self.zl
        if flip & 2:
            target["y"] = 1 - self.y
        if flip & 1:
            target["c"] = 1 - self.c
        return target

    def index_of(self, flip):
        zl = 1 - self.zl if flip & 4 else self.zl
        y = 1 - self.y if flip & 2 else self.y
        c = 1 - self.c if flip & 1 else self.c
        return zl * 4 + y * 2 + c

    def head_lanes(self, sz, member, k):
        group = member // sz.pieces
        head = ((member - group * sz.pieces) * sz.heads + k) * (TP // sz.pieces) + group
        return pl.ds(pl.multiple_of(head * HD, HD), HD)

    def to_x(self, step):
        return {"x": lax.rem(self.x + step, self.nx)}

    def x_of(self, step):
        return lax.rem(self.x + step, self.nx)


class Copies:
    def __init__(self, send, recv, local):
        self.send, self.recv, self.local_sems = send, recv, local
        self.n_remote = 0
        self.n_local = 0
        self.sent = []
        self.kept = []

    def remote(self, src, dst, target):
        i = self.n_remote
        self.n_remote += 1
        copy = pltpu.make_async_remote_copy(
            src_ref=src,
            dst_ref=dst,
            send_sem=self.send.at[i],
            recv_sem=self.recv.at[i],
            device_id=target,
            device_id_type=pl.DeviceIdType.MESH,
        )
        copy.start()
        self.sent.append(copy)
        return copy

    def remote_parts(self, pairs, whole, target):
        i = self.n_remote
        self.n_remote += 1

        def copy(src, dst):
            return pltpu.make_async_remote_copy(
                src_ref=src,
                dst_ref=dst,
                send_sem=self.send.at[i],
                recv_sem=self.recv.at[i],
                device_id=target,
                device_id_type=pl.DeviceIdType.MESH,
            )

        for src, dst in pairs:
            copy(src, dst).start()
        total = copy(whole, whole)
        self.sent.append(total)
        return total

    def local_parts(self, pairs, whole):
        i = self.n_local
        self.n_local += 1
        for src, dst in pairs:
            pltpu.make_async_copy(src, dst, self.local_sems.at[i]).start()
        return pltpu.make_async_copy(whole, whole, self.local_sems.at[i])

    def local(self, src, dst):
        i = self.n_local
        self.n_local += 1
        copy = pltpu.make_async_copy(src, dst, self.local_sems.at[i])
        copy.start()
        return copy

    def keep(self, src, dst):
        self.kept.append(self.local(src, dst))

    def left(self, copy):
        copy.wait_send()
        self.sent = [other for other in self.sent if other is not copy]

    def finish(self):
        for copy in self.kept:
            copy.wait()
        for copy in self.sent:
            copy.wait_send()


def greet(targets):
    barrier = pltpu.get_barrier_semaphore()
    for target in targets:
        pl.semaphore_signal(
            barrier, inc=1, device_id=target, device_id_type=pl.DeviceIdType.MESH
        )
    pl.semaphore_wait(barrier, len(targets))


def dot(left, right):
    return jnp.dot(left, right, preferred_element_type=F32)


def dot_nt(left, right):
    return lax.dot_general(left, right, (((1,), (1,)), ((), ())), preferred_element_type=F32)


def dot_tn(left, right):
    return lax.dot_general(left, right, (((0,), (0,)), ((), ())), preferred_element_type=F32)


def tile(i, size):
    return pl.ds(pl.multiple_of(i * size, size), size)


def loop(count, body):
    def step(i, carry):
        body(i)
        return carry

    lax.fori_loop(0, count, step, 0)


def normed(values):
    average = jnp.mean(values, axis=1, keepdims=True)
    centred = values - average
    variance = jnp.mean(centred * centred, axis=1, keepdims=True)
    scale = lax.rsqrt(variance + EPSILON)
    return centred * scale, scale


def normed_back(grad, xhat, scale):
    along = jnp.mean(grad * xhat, axis=1, keepdims=True)
    return scale * (grad - jnp.mean(grad, axis=1, keepdims=True) - xhat * along)


class Gather:
    def __init__(self, net, at, sz, buf, start, count, tall=False):
        self.net, self.at, self.sz, self.buf = net, at, sz, buf
        self.start, self.count, self.tall = start, count, tall
        half = sz.width // 2
        self.cols = (pl.ds(0, half), pl.ds(half, half))
        self.sib = [None] * 4

    def part(self, slot, core, cols=None):
        rows = pl.ds((slot * 2 + core) * self.sz.tokens + self.start, self.count)
        return self.buf.at[rows, :] if cols is None else self.buf.at[rows, cols]

    def send(self):
        net, at = self.net, self.at
        self.from_y = [None, None]
        self.from_z = [None, None]
        for h in (0, 1):
            self.from_y[h] = net.remote(
                self.part(0, 0, self.cols[h]), self.part(1, 0, self.cols[h]), at.to_y
            )
            self.from_z[1 - h] = net.remote(
                self.part(0, 0, self.cols[1 - h]), self.part(2, 0, self.cols[1 - h]), at.to_z
            )
        self.share(0)

    def share(self, slot):
        self.sib[slot] = self.net.remote(self.part(slot, 0), self.part(slot, 1), self.at.to_c)

    def relay(self):
        net, at = self.net, self.at
        if self.tall:
            to_y = []
            for h in (1, 0):
                self.from_z[h].wait_recv()
                to_y.append(
                    net.remote(
                        self.part(2, 0, self.cols[h]), self.part(3, 0, self.cols[h]), at.to_y
                    )
                )
            self.diag = tuple(to_y)
            self.share(2)
            for copy in self.from_y:
                copy.wait_recv()
            self.share(1)
            return
        self.from_y[0].wait_recv()
        to_z = net.remote(
            self.part(1, 0, self.cols[0]), self.part(3, 0, self.cols[0]), at.to_z
        )
        self.from_z[1].wait_recv()
        to_y = net.remote(
            self.part(2, 0, self.cols[1]), self.part(3, 0, self.cols[1]), at.to_y
        )
        self.diag = (to_z, to_y)
        self.from_y[1].wait_recv()
        self.share(1)
        self.from_z[0].wait_recv()
        self.share(2)

    def relay_last(self):
        for copy in self.diag:
            copy.wait_recv()
        self.share(3)

    def ready(self, slot):
        self.sib[slot].wait_recv()


class Scatter:
    def __init__(self, net, at, sz, bufs, tall=False):
        self.net, self.at, self.sz, self.tall = net, at, sz, tall
        self.mine, self.theirs, self.got, self.diag, self.diag_got, self.out, self.inn = bufs
        self.sib = [None] * 4

    @staticmethod
    def scratch(sz):
        t, d = sz.tokens, sz.width
        return [
            pltpu.VMEM((4 * t, d), F32),
            pltpu.VMEM((4 * t, d), BF16),
            pltpu.VMEM((4 * t, d), BF16),
            pltpu.VMEM((t, d), BF16),
            pltpu.VMEM((t, d), BF16),
            pltpu.VMEM((2 * t, d), BF16),
            pltpu.VMEM((2 * t, d), BF16),
        ]

    def put(self, slot, cols, value):
        t = self.sz.tokens
        self.mine[pl.ds(slot * t, t), cols] = value[:t]
        self.theirs[pl.ds(slot * t, t), cols] = value[t:].astype(BF16)

    def share(self, slot):
        rows = pl.ds(slot * self.sz.tokens, self.sz.tokens)
        self.sib[slot] = self.net.remote(self.theirs.at[rows, :], self.got.at[rows, :], self.at.to_c)

    def add(self, slot, start, count, dst, dst_start, extra=None):
        base = slot * self.sz.tokens + start

        def body(i):
            rows = pl.ds(pl.multiple_of(base + i * STRIP, STRIP), STRIP)
            total = self.mine[rows, :] + self.got[rows, :].astype(F32)
            if extra is not None:
                there = pl.ds(pl.multiple_of(start + i * STRIP, STRIP), STRIP)
                total = total + extra[there, :].astype(F32)
            dst[pl.ds(pl.multiple_of(dst_start + i * STRIP, STRIP), STRIP), :] = total.astype(BF16)

        loop(count // STRIP, body)

    def send_diag(self):
        net, at, h = self.net, self.at, self.sz.half
        self.sib[3].wait_recv()
        self.add(3, 0, 2 * h, self.diag, 0)
        low, high = pl.ds(0, h), pl.ds(h, h)
        self.d_low = net.remote(self.diag.at[low, :], self.diag_got.at[low, :], at.to_y)
        self.d_high = net.remote(
            self.diag.at[high, :], self.diag_got.at[high, :], at.to_y if self.tall else at.to_z
        )

    def half_out(self, side, start, target):
        rows = pl.ds(side * self.sz.tokens + start, self.sz.half)
        return self.net.remote(self.out.at[rows, :], self.inn.at[rows, :], target)

    def send_free(self):
        at, t, h = self.at, self.sz.tokens, self.sz.half
        self.sib[1].wait_recv()
        self.add(1, 0, h, self.out, 0)
        self.y_low = self.half_out(0, 0, at.to_y)
        if self.tall:
            self.add(1, h, h, self.out, h)
            self.y_high = self.half_out(0, h, at.to_y)
            return
        self.sib[2].wait_recv()
        self.add(2, h, h, self.out, t + h)
        self.z_high = self.half_out(1, h, at.to_z)

    def send_joined(self):
        at, t, h = self.at, self.sz.tokens, self.sz.half
        if self.tall:
            self.sib[2].wait_recv()
            self.d_low.wait_recv()
            self.add(2, 0, h, self.out, t, self.diag_got)
            self.z_low = self.half_out(1, 0, at.to_z)
            self.d_high.wait_recv()
            self.add(2, h, h, self.out, t + h, self.diag_got)
            self.z_high = self.half_out(1, h, at.to_z)
            return
        self.d_high.wait_recv()
        self.add(1, h, h, self.out, h, self.diag_got)
        self.y_high = self.half_out(0, h, at.to_y)
        self.d_low.wait_recv()
        self.add(2, 0, h, self.out, t, self.diag_got)
        self.z_low = self.half_out(1, 0, at.to_z)

    def settle(self):
        for copy in [*self.sib, self.d_low, self.d_high, self.y_low, self.z_high, self.y_high, self.z_low]:
            self.net.left(copy)

    def wait(self):
        self.sib[0].wait_recv()
        for copy in (self.y_low, self.z_high, self.y_high, self.z_low):
            copy.wait_recv()

    def total(self, i):
        t = self.sz.tokens
        rows = tile(i, STRIP)
        far = pl.ds(pl.multiple_of(t + i * STRIP, STRIP), STRIP)
        return (
            self.mine[rows, :]
            + self.got[rows, :].astype(F32)
            + self.inn[rows, :].astype(F32)
            + self.inn[far, :].astype(F32)
        )


class Spread:
    def __init__(self, net, at, view, source=None):
        self.net, self.at, self.view = net, at, view
        self.source = view(at.p) if source is None else source
        self.relayed = []

    def across(self):
        self.from_h = self.net.remote(self.source, self.view(self.at.p), self.at.to_h)

    def along(self):
        self.from_x = [
            self.net.remote(self.source, self.view(self.at.p), self.at.to_x(step))
            for step in range(1, self.at.nx)
        ]

    def relay(self):
        self.from_h.wait_recv()
        there = self.view(self.at.pz)
        self.relayed = [
            self.net.remote(there, there, self.at.to_x(step)) for step in range(1, self.at.nx)
        ]

    def near(self):
        for copy in self.from_x:
            copy.wait_recv()

    def far(self):
        for copy in self.relayed:
            copy.wait_recv()


def attention_forward_kernel(
    sz,
    xin, w_query, w_key, w_value, wout, wup_rows, wdown, vec_pack,
    x_all, wqkv, w_out_own, w_up, w_down, vec_all, bup_all, qkv_all, ctx_all, first_in, first_low,
    xs, wq, wo_got, wo, vecs, vec, bup, acc, qkv, ctx, fin, first, wu_own, wd_own, *rest,
):
    *sum_bufs, send, recv, local = rest
    at = Place(sz)
    net = Copies(send, recv, local)
    t, d, h = sz.tokens, sz.width, sz.half
    rw, rf = sz.row_shard, sz.hid_shard
    flips = range(1, TP)
    greet(
        [at.peer(f) for f in flips] + [at.to_h] + [at.to_x(s) for s in range(1, sz.nx)]
    )

    own_rows = pl.ds(at.zh * h, h)
    from_h = net.remote(xin.at[1 - at.zh], xs.at[own_rows, :], at.to_h)
    own_x = net.local(xin.at[at.zh], xs.at[own_rows, :])

    def wq_rows(p, member, count=1):
        return pl.ds((p * TP + member) * rw, count * rw)

    def wq_parts(member):
        return [
            (
                source.at[:, at.head_lanes(sz, member, k)],
                wq.at[wq_rows(at.p, at.t), pl.ds(which * sz.cols + k * HD, HD)],
            )
            for which, source in enumerate((w_query, w_key, w_value))
            for k in range(sz.heads)
        ]

    def wu_parts(member, dst):
        if not sz.by_lanes:
            return [(wup_rows.at[member], dst)]
        return [
            (
                wup_rows.at[:, pl.ds(pl.multiple_of((p * TP + member) * rf, rf), rf)],
                dst.at[:, pl.ds(p * rf, rf)],
            )
            for p in range(sz.parts)
        ]

    wq_mine, wu_mine = wq.at[wq_rows(at.p, at.t), :], w_up.at[wq_rows(at.p, at.t), :]
    own_wq = net.local_parts(wq_parts(at.t), wq_mine)
    own_vec = net.local(vec_pack, vecs.at[at.p * TP + at.t])
    own_wo = net.local(wout, wo_got.at[at.p])
    wu_here = net.local_parts(wu_parts(at.t, wu_own), wu_own)
    wd_here = net.local(wdown.at[pl.ds(0, rf // 2), :], wd_own)
    wq_in = [None] + [
        net.remote_parts(wq_parts(at.index_of(f)), wq_mine, at.peer(f)) for f in flips
    ]
    vec_in = [net.remote(vec_pack, vecs.at[at.p * TP + at.t], at.peer(f)) for f in flips]
    own_x.wait()
    near_rows = Gather(net, at, sz, xs, at.zh * h, h, tall=True)
    near_rows.send()

    def chip_block(buf, f):
        member = at.index_of(f) - at.c
        return lambda p: buf.at[wq_rows(p, member, 2), :]

    wq_spread = [Spread(net, at, chip_block(wq, f)) for f in (0, 2, 4, 6)]
    for f, item in zip((0, 2, 4, 6), wq_spread):
        if f == 0:
            own_wq.wait()
        else:
            wq_in[f].wait_recv()
        wq_in[f + 1].wait_recv()
        item.across()
        item.along()
    own_vec.wait()
    for copy in vec_in:
        copy.wait_recv()
    vec_spread = Spread(net, at, lambda p: vecs.at[pl.ds(p * TP, TP)])
    wo_spread = Spread(net, at, lambda p: wo_got.at[p], wout)
    vec_spread.across()
    vec_spread.along()
    wo_spread.along()
    from_h.wait_recv()
    far_rows = Gather(net, at, sz, xs, (1 - at.zh) * h, h, tall=True)
    far_rows.send()
    near_rows.relay()
    far_rows.relay()
    wq_spread[0].relay()
    near_rows.relay_last()
    far_rows.relay_last()
    vec_spread.relay()
    wq_spread[1].relay()
    wo_spread.across()
    wu_here.wait()
    own_wu = net.local(wu_own, w_up.at[wq_rows(at.p, at.t), :])
    wd_here.wait()
    net.keep(wd_own, w_down.at[pl.ds(at.p * (rf // 2), rf // 2), :])
    wu_in = [None] + [
        net.remote_parts(wu_parts(at.index_of(f), wu_mine), wu_mine, at.peer(f)) for f in flips
    ]

    def accumulate(zh, first_part):
        def body(i):
            rows = tile(i, 256)
            total = jnp.zeros((256, 3 * sz.cols), F32) if first_part else acc[rows, :]
            for x in range(sz.nx):
                block = tile(x * 2 + zh, sz.slab)
                total = total + dot(xs[rows, block], wq[block, :])
            acc[rows, :] = total

        loop(sz.rows_all // 256, body)

    for slot in range(4):
        near_rows.ready(slot)
        far_rows.ready(slot)
    for item in wq_spread:
        item.near()
    net.keep(xs, x_all)
    accumulate(at.zh, True)
    for item in wq_spread[2:]:
        item.relay()
    wd_chunk = rf // 4
    wd_spread = [
        Spread(
            net,
            at,
            lambda p, j=j: w_down.at[pl.ds(p * 2 * wd_chunk + j * wd_chunk, wd_chunk), :],
            wdown.at[pl.ds(j * wd_chunk, wd_chunk), :],
        )
        for j in range(2)
    ]
    for item in wd_spread:
        item.across()
    vec_spread.near()
    vec_spread.far()
    for j in range(d // HD):
        piece = vecs[j * sz.pieces, 0:8]
        for k in range(1, sz.pieces):
            piece = piece + vecs[j * sz.pieces + k, 0:8]
        vec[:, j * HD : (j + 1) * HD] = piece
    if rf >= HD:
        for p in range(sz.parts):
            for j in range(rf // HD):
                lanes = pl.ds(p * rf + j * HD, HD)
                bup[0:1, lanes] = vecs[p * TP + at.t, 8 + j : 9 + j]
    else:
        for j in range(sz.hid // HD):
            each = HD // rf
            row = vecs[j * each * TP + at.t, 8:9]
            for k in range(1, each):
                row = row + vecs[(j * each + k) * TP + at.t, 8:9]
            bup[0:1, j * HD : (j + 1) * HD] = row
    net.keep(vec, vec_all)
    net.keep(bup, bup_all)
    for item in wq_spread:
        item.far()
    accumulate(1 - at.zh, False)
    wo_spread.relay()
    for item in wd_spread:
        item.along()

    group = at.t // sz.pieces
    member = at.t - group * sz.pieces
    for k in range(sz.heads):
        lanes = at.head_lanes(sz, at.t, k)

        def biased(i, k=k, lanes=lanes):
            rows = tile(i, 256)
            for which in range(3):
                cols = slice(which * sz.cols + k * HD, which * sz.cols + (k + 1) * HD)
                value = acc[rows, cols]
                if which != 1:
                    value = value + vec[which // 2 : which // 2 + 1, lanes]
                qkv[rows, cols] = value.astype(BF16)

        loop(sz.rows_all // 256, biased)
    net.keep(wq, wqkv)
    net.keep(qkv, qkv_all)

    def attend(k):
        q_cols = slice(k * HD, (k + 1) * HD)
        k_cols = slice(sz.cols + k * HD, sz.cols + (k + 1) * HD)
        v_cols = slice(2 * sz.cols + k * HD, 2 * sz.cols + (k + 1) * HD)

        def body(i):
            rows = tile(i, 256)
            scores = dot_nt(qkv[rows, q_cols], qkv[:, k_cols]) * SCALE
            top = jnp.max(scores, axis=1, keepdims=True)
            exps = jnp.exp(scores - top)
            probs = exps * (1.0 / jnp.sum(exps, axis=1, keepdims=True))
            ctx[rows, q_cols] = dot(probs.astype(BF16), qkv[:, v_cols]).astype(BF16)

        loop(sz.rows_all // 256, body)

    for k in range(sz.heads):
        attend(k)
    net.keep(ctx, ctx_all)

    own_wo.wait()
    wo_spread.near()
    wo_spread.far()

    def wo_rows(k, piece):
        return pl.ds((k * sz.pieces + piece) * rw, rw)

    for k in range(sz.heads):
        net.local(wo_got.at[member * sz.heads + k], wo.at[wo_rows(k, member), :]).wait()
    wo_in = []
    for f in range(1, sz.pieces):
        other = at.index_of(f) - group * sz.pieces
        for k in range(sz.heads):
            wo_in.append(
                net.remote(wo_got.at[other * sz.heads + k], wo.at[wo_rows(k, member), :], at.peer(f))
            )
    for copy in wo_in:
        copy.wait_recv()
    net.keep(wo, w_out_own)
    wu_spread = [Spread(net, at, chip_block(w_up, f)) for f in (0, 2, 4, 6)]
    own_wu.wait()
    for f, item in zip((0, 2, 4, 6), wu_spread):
        if f:
            wu_in[f].wait_recv()
        wu_in[f + 1].wait_recv()
        item.across()
    for item in wu_spread:
        item.along()

    sums = Scatter(net, at, sz, sum_bufs, tall=True)
    for slot in (3, 1, 2, 0):
        rows = pl.ds(slot * 2 * t, 2 * t)

        def body(i, rows=rows, slot=slot):
            cols = tile(i, 512)
            sums.put(slot, cols, dot(ctx[rows, :], wo[:, cols]))

        loop(d // 512, body)
        sums.share(slot)
        if slot == 3:
            sums.send_diag()
    sums.send_free()
    sums.send_joined()
    for item in wd_spread:
        item.relay()
    sums.wait()

    def norm(i):
        rows = tile(i, STRIP)
        value = xs[rows, :].astype(F32) + sums.total(i) + vec[2:3, :]
        fin[rows, :] = value
        xhat, _ = normed(value)
        first[rows, :] = (xhat * vec[3:4, :] + vec[4:5, :]).astype(BF16)

    loop(t // STRIP, norm)
    net.keep(fin, first_in)
    net.keep(first, first_low)
    for item in wu_spread:
        item.relay()
    for item in wu_spread + wd_spread:
        item.near()
        item.far()
    net.finish()


def attention_forward(sz, *args):
    t, d, r = sz.tokens, sz.width, sz.rows_all
    shape = jax.ShapeDtypeStruct
    anywhere = pl.BlockSpec(memory_space=pl.ANY)
    outs = (
        shape((r, d), BF16),
        shape((d, 3 * sz.cols), BF16),
        shape((sz.cols, d), BF16),
        shape((d, sz.hid), BF16),
        shape((sz.hid // 2, d), BF16),
        shape((8, d), F32),
        shape((8, sz.hid), F32),
        shape((r, 3 * sz.cols), BF16),
        shape((r, sz.cols), BF16),
        shape((t, d), F32),
        shape((t, d), BF16),
    )
    scratch = [
        pltpu.VMEM((r, d), BF16),
        pltpu.VMEM((d, 3 * sz.cols), BF16),
        pltpu.VMEM((sz.parts, sz.row_shard, d), BF16),
        pltpu.VMEM((sz.cols, d), BF16),
        pltpu.VMEM((sz.parts * TP, 16, HD), F32),
        pltpu.VMEM((8, d), F32),
        pltpu.VMEM((8, sz.hid), F32),
        pltpu.VMEM((r, 3 * sz.cols), F32),
        pltpu.VMEM((r, 3 * sz.cols), BF16),
        pltpu.VMEM((r, sz.cols), BF16),
        pltpu.VMEM((t, d), F32),
        pltpu.VMEM((t, d), BF16),
        pltpu.VMEM((sz.row_shard, sz.hid), BF16),
        pltpu.VMEM((sz.hid_shard // 2, d), BF16),
        *Scatter.scratch(sz),
        pltpu.SemaphoreType.DMA((80 + 28 * sz.nx,)),
        pltpu.SemaphoreType.DMA((80 + 28 * sz.nx,)),
        pltpu.SemaphoreType.DMA((24,)),
    ]
    return pl.pallas_call(
        functools.partial(attention_forward_kernel, sz),
        out_shape=outs,
        in_specs=[anywhere] * 8,
        out_specs=[anywhere] * len(outs),
        scratch_shapes=scratch,
        compiler_params=pltpu.CompilerParams(
            collective_id=0, has_side_effects=True, vmem_limit_bytes=VMEM_LIMIT
        ),
        name="attention_forward",
    )(*args)


GELU_A = 0.7978845608028654
GELU_B = 0.044715


def gate(values):
    inner = jnp.tanh(GELU_A * (values + GELU_B * values * values * values))
    return 0.5 * values * (1.0 + inner)


def gate_slope(values):
    square = values * values
    inner = jnp.tanh(GELU_A * (values + GELU_B * square * values))
    rise = GELU_A * (1.0 + 3.0 * GELU_B * square)
    return 0.5 * (1.0 + inner) + 0.5 * values * (1.0 - inner * inner) * rise


def feed_forward_kernel(
    sz,
    first_low, first_in, w_up, w_down_half, vec_all, bup_all, cot_in, wdown,
    outputs, grad_first_in, grad_low, grad_w_up, grad_w_down, grad_vec, down_sum, down_in,
    fa, wu, wd, vec, bup, fin, cot, hid, act, gh, g2, g2s, out, gv, dwu, dwd, *rest,
):
    *bufs, send, recv, local = rest
    sum_bufs, bufs = bufs[:7], bufs[7:]
    at = Place(sz)
    net = Copies(send, recv, local)
    t, d, h = sz.tokens, sz.width, sz.half
    two = 2 * t
    rf = sz.hid_shard
    load_first = net.local(first_low, fa.at[pl.ds(0, t), :])
    load_up = net.local(w_up, wu)
    load_bup = net.local(bup_all, bup)
    load_down = [
        net.local(w_down_half.at[pl.ds(p * (rf // 2), rf // 2), :], wd.at[pl.ds(p * rf, rf // 2), :])
        for p in range(sz.parts)
    ]
    late_own = pl.ds(at.p * rf + rf // 2, rf // 2)
    load_down.append(net.local(wdown.at[pl.ds(rf // 2, rf // 2), :], wd.at[late_own, :]))
    load_vec = net.local(vec_all, vec)
    load_fin = net.local(first_in, fin)
    own_rows = pl.ds(at.zh * h, h)
    load_cot = net.local(cot_in.at[at.zh], cot.at[own_rows, :])
    greet([at.to_c, at.to_y, at.to_z, at.to_h] + [at.to_x(s) for s in range(1, sz.nx)])
    load_first.wait()
    firsts = Gather(net, at, sz, fa, 0, t, tall=True)
    firsts.send()
    wd_chunk = rf // 4
    wd_spread = [
        Spread(
            net,
            at,
            lambda p, j=j: wd.at[pl.ds(p * rf + j * wd_chunk, wd_chunk), :],
            wdown.at[pl.ds(j * wd_chunk, wd_chunk), :],
        )
        for j in (2, 3)
    ]
    for item in wd_spread:
        item.across()
        item.along()
    gv[...] = jnp.zeros_like(gv)

    sums = Scatter(net, at, sz, sum_bufs)
    load_up.wait()
    load_bup.wait()

    def project_up(slot):
        firsts.ready(slot)
        rows = pl.ds(slot * two, two)

        def up(i):
            cols = tile(i, 512)
            value = dot(fa[rows, :], wu[:, cols]) + bup[0:1, cols]
            hid[rows, cols] = value
            act[rows, cols] = gate(value).astype(BF16)

        loop(sz.hid // 512, up)

    project_up(0)
    firsts.relay()
    wd_spread[0].relay()
    project_up(2)
    project_up(1)
    firsts.relay_last()
    project_up(3)
    wd_spread[1].relay()
    cot_far = net.remote(cot_in.at[1 - at.zh], cot.at[own_rows, :], at.to_h)
    for copy in load_down:
        copy.wait()
    for item in wd_spread:
        item.near()
        item.far()
    for slot in (3, 1, 2, 0):
        rows = pl.ds(slot * two, two)

        def down(i, rows=rows, slot=slot):
            cols = tile(i, 512)
            sums.put(slot, cols, dot(act[rows, :], wd[:, cols]))

        loop(d // 512, down)
        sums.share(slot)
        if slot == 1:
            sums.send_diag()
    sums.send_free()
    sums.send_joined()
    load_vec.wait()
    load_fin.wait()
    load_cot.wait()
    cot_far.wait_recv()
    sums.wait()

    def strip_sum(row, value):
        gv[row : row + 1, :] = gv[row : row + 1, :] + jnp.sum(value, axis=0, keepdims=True)

    def second_norm(i):
        rows = tile(i, STRIP)
        xhat, _ = normed(fin[rows, :])
        value = xhat * vec[3:4, :] + vec[4:5, :] + sums.total(i) + vec[5:6, :]
        xhat, scale = normed(value)
        out[rows, :] = (xhat * vec[6:7, :] + vec[7:8, :]).astype(BF16)
        grad = cot[rows, :].astype(F32)
        strip_sum(6, grad * xhat)
        strip_sum(7, grad)
        grad = normed_back(grad * vec[6:7, :], xhat, scale)
        g2s[rows, :] = grad
        low = grad.astype(BF16)
        g2[rows, :] = low
        strip_sum(5, low.astype(F32))

    loop(t // STRIP, second_norm)
    gather = Gather(net, at, sz, g2, 0, t)
    gather.send()
    net.keep(out.at[own_rows, :], outputs.at[at.zh])
    out_far = net.remote(out.at[pl.ds((1 - at.zh) * h, h), :], outputs.at[at.zh], at.to_h)
    sums.settle()

    def back(slot):
        gather.ready(slot)
        rows = pl.ds(slot * two, two)

        def down(i):
            cols = tile(i, 512)
            value = dot_nt(g2[rows, :], wd[cols, :])
            gh[rows, cols] = (value * gate_slope(hid[rows, cols])).astype(BF16)

        loop(sz.hid // 512, down)

        def up(i):
            cols = tile(i, 512)
            sums.put(slot, cols, dot_nt(gh[rows, :], wu[cols, :]))

        loop(d // 512, up)
        sums.share(slot)

    back(0)
    gather.relay()
    back(1)
    back(2)
    sums.send_free()
    gather.relay_last()
    back(3)
    sums.send_diag()

    def down_grad(i):
        rows, cols = tile(i // (d // 512), 512), tile(i % (d // 512), 512)
        dwd[rows, cols] = dot_tn(act[:, rows], g2[:, cols]).astype(BF16)

    loop((sz.hid // 512) * (d // 512), down_grad)
    net.keep(dwd, grad_w_down)
    down_rows = sz.hid_shard // 4
    sum_d = Reduce(
        net, at, lambda p, j: dwd.at[pl.ds(p * sz.hid_shard + j * down_rows, down_rows), :], bufs, 4, True, None
    )
    sum_d.start(0)
    sums.send_joined()
    sum_d.hop(0)

    def up_grad(i):
        rows, cols = tile(i // (sz.hid // 512), 512), tile(i % (sz.hid // 512), 512)
        dwu[rows, cols] = dot_tn(fa[:, rows], gh[:, cols]).astype(BF16)

    loop((sz.hid // 512) * (d // 512), up_grad)
    net.keep(dwu, grad_w_up)
    sum_d.hop(1)
    for p in range(sz.parts):
        rf = sz.hid_shard
        gv[8:9, p * sz.slab : p * sz.slab + rf] = jnp.sum(
            gh[:, p * rf : (p + 1) * rf].astype(F32), axis=0, keepdims=True
        )
    sums.wait()

    def first_norm(i):
        rows = tile(i, STRIP)
        xhat, scale = normed(fin[rows, :])
        grad = g2s[rows, :] + sums.total(i)
        strip_sum(3, grad * xhat)
        strip_sum(4, grad)
        grad = normed_back(grad * vec[3:4, :], xhat, scale)
        g2s[rows, :] = grad
        low = grad.astype(BF16)
        out_low[rows, :] = low
        strip_sum(2, low.astype(F32))

    out_low = cot
    loop(t // STRIP, first_norm)
    net.keep(g2s, grad_first_in)
    net.keep(out_low, grad_low)
    net.keep(gv, grad_vec)
    for j in (2, 3):
        sum_d.add(j)
    late = pl.ds(2 * down_rows, 2 * down_rows)
    early = pl.ds(0, 2 * down_rows)
    net.keep(sum_d.out.at[late, :], down_sum)
    for j in (0, 1):
        sum_d.from_h[j].wait_recv()
    net.keep(sum_d.inn.at[early, :], down_in)
    out_far.wait_recv()
    net.finish()


def feed_forward(sz, *args):
    t, d, r = sz.tokens, sz.width, sz.rows_all
    shape = jax.ShapeDtypeStruct
    anywhere = pl.BlockSpec(memory_space=pl.ANY)
    outs = (
        shape((2, sz.half, d), BF16),
        shape((t, d), F32),
        shape((t, d), BF16),
        shape((d, sz.hid), BF16),
        shape((sz.hid, d), BF16),
        shape((16, d), F32),
        shape((sz.hid_shard // 2, d), BF16),
        shape((sz.hid_shard // 2, d), BF16),
    )
    scratch = [
        pltpu.VMEM((r, d), BF16),
        pltpu.VMEM((d, sz.hid), BF16),
        pltpu.VMEM((sz.hid, d), BF16),
        pltpu.VMEM((8, d), F32),
        pltpu.VMEM((8, sz.hid), F32),
        pltpu.VMEM((t, d), F32),
        pltpu.VMEM((t, d), BF16),
        pltpu.VMEM((r, sz.hid), F32),
        pltpu.VMEM((r, sz.hid), BF16),
        pltpu.VMEM((r, sz.hid), BF16),
        pltpu.VMEM((r, d), BF16),
        pltpu.VMEM((t, d), F32),
        pltpu.VMEM((t, d), BF16),
        pltpu.VMEM((16, d), F32),
        pltpu.VMEM((d, sz.hid), BF16),
        pltpu.VMEM((sz.hid, d), BF16),
        *Scatter.scratch(sz),
        *Reduce.scratch(sz, sz.hid_shard, d, BF16, True, 1),
        pltpu.SemaphoreType.DMA((64 + 8 * sz.nx,)),
        pltpu.SemaphoreType.DMA((64 + 8 * sz.nx,)),
        pltpu.SemaphoreType.DMA((24,)),
    ]
    return pl.pallas_call(
        functools.partial(feed_forward_kernel, sz),
        out_shape=outs,
        in_specs=[anywhere] * 8,
        out_specs=[anywhere] * len(outs),
        scratch_shapes=scratch,
        compiler_params=pltpu.CompilerParams(
            collective_id=1, has_side_effects=True, vmem_limit_bytes=VMEM_LIMIT
        ),
        name="feed_forward",
    )(*args)


class Reduce:
    def __init__(self, net, at, view, bufs, chunks, held, result):
        self.net, self.at, self.view, self.chunks = net, at, view, chunks
        self.got, self.own, self.out, self.inn = bufs
        self.rows = self.out.shape[0] // chunks
        self.result = result
        self.held = held
        self.groups = (at.x * 2 + (1 - at.zh), at.x * 2 + at.zh)
        self.from_x, self.from_h, self.loads = {}, {}, {}

    @staticmethod
    def scratch(sz, rows, cols, dtype, held, kinds=2):
        return [
            pltpu.VMEM((sz.nx - 1, kinds, rows, cols), dtype),
            pltpu.VMEM((2, 8, 128) if held else (2, rows, cols), dtype),
            pltpu.VMEM((rows, cols), dtype),
            pltpu.VMEM((rows, cols), dtype),
        ]

    def chunk(self, j):
        return pl.ds(j * self.rows, self.rows)

    def start(self, which):
        at, net = self.at, self.net
        zh = 1 - at.zh if which == 0 else at.zh
        for j in range(self.chunks):
            for step in range(1, at.nx):
                p = at.x_of(step) * 2 + zh
                self.from_x[which, j, step] = net.remote(
                    self.view(p, j), self.got.at[step - 1, which, self.chunk(j), :], at.to_x(step)
                )
            if not self.held:
                self.loads[which, j] = net.local(
                    self.view(self.groups[which], j), self.own.at[which, self.chunk(j), :]
                )

    def term(self, which, j, i):
        rows = pl.ds(pl.multiple_of(j * self.rows + i * STRIP, STRIP), STRIP)
        if self.held:
            total = self.view(self.groups[which], j)[tile(i, STRIP), :].astype(F32)
        else:
            total = self.own[which, rows, :].astype(F32)
        for step in range(1, self.at.nx):
            total = total + self.got[step - 1, which, rows, :].astype(F32)
        return rows, total

    def ready(self, which, j):
        for step in range(1, self.at.nx):
            self.from_x[which, j, step].wait_recv()
        if not self.held:
            self.loads[which, j].wait()

    def add(self, j):
        self.ready(0, j)

        def body(i):
            rows, total = self.term(0, j, i)
            self.out[rows, :] = total.astype(self.out.dtype)

        loop(self.rows // STRIP, body)

    def hop(self, j):
        self.add(j)
        self.send(j)

    def send(self, j):
        self.from_h[j] = self.net.remote(
            self.out.at[self.chunk(j), :], self.inn.at[self.chunk(j), :], self.at.to_h
        )

    def close(self, j):
        self.ready(1, j)
        if j in self.from_h:
            self.from_h[j].wait_recv()

        def body(i):
            rows, total = self.term(1, j, i)
            self.result[rows, :] = (total + self.inn[rows, :].astype(F32)).astype(self.result.dtype)

        loop(self.rows // STRIP, body)


def attention_backward_kernel(
    sz,
    grad_low, grad_first_in, x_all, wqkv, w_out_own, qkv_all, ctx_all, grad_w_up, grad_w_down, grad_vec, down_sum, down_in,
    input_grad, out_wq, out_wk, out_wv, out_wo, out_wup, out_wdown, out_vec, out_bup,
    gb, xs, wq, wo, qkv, ctx, gfi, gv, dctx, dqkv, dk, dv, ig, dwq, dwo, dwo_own, res_q, res_o, res_u, res_d, res_v,
    vec_got, vec_sum, bup_out, *rest,
):
    *bufs, send, recv, local = rest
    sum_bufs, bufs = bufs[:7], bufs[7:]
    at = Place(sz)
    net = Copies(send, recv, local)
    t, d, h = sz.tokens, sz.width, sz.half
    two = 2 * t
    rw, rf = sz.row_shard, sz.hid_shard
    flips = range(1, TP)
    load_gb = net.local(grad_low, gb.at[pl.ds(0, t), :])
    load_wo = net.local(w_out_own, wo)
    load_qkv = net.local(qkv_all, qkv)
    load_ctx = net.local(ctx_all, ctx)
    load_gv = net.local(grad_vec, gv)
    greet([at.peer(f) for f in flips] + [at.to_h] + [at.to_x(s) for s in range(1, sz.nx)])
    load_gb.wait()
    gather = Gather(net, at, sz, gb, 0, t, tall=True)
    gather.send()

    up_rows, down_rows = sz.slab // 4, rf // 4
    sum_u = Reduce(
        net, at, lambda p, j: grad_w_up.at[pl.ds(p * sz.slab + j * up_rows, up_rows), :],
        bufs[0:4], 4, False, res_u,
    )
    sum_d = Reduce(
        net, at, lambda p, j: grad_w_down.at[pl.ds(p * rf + j * down_rows, down_rows), :],
        bufs[4:8], 4, False, res_d,
    )
    sum_q = Reduce(
        net, at, lambda p, j: dwq.at[pl.ds(p * sz.slab + j * up_rows, up_rows), :], bufs[8:12], 4, True, res_q
    )
    sum_o = Reduce(net, at, lambda p, j: dwo_own.at[p], bufs[12:16], 1, True, res_o)
    sum_v = Reduce(
        net, at, lambda p, j: gv.at[:, pl.ds(pl.multiple_of(p * sz.slab, sz.slab), sz.slab)],
        bufs[16:20], 1, True, res_v,
    )
    late = pl.ds(2 * down_rows, 2 * down_rows)
    load_sum = net.local(down_sum, sum_d.out.at[late, :])
    load_in = net.local(down_in, sum_d.inn.at[pl.ds(0, 2 * down_rows), :])
    sum_u.start(0)
    load_sum.wait()
    for j in (2, 3):
        sum_d.send(j)
    sum_u.start(1)
    load_x = net.local(x_all, xs)
    load_wq = net.local(wqkv, wq)
    load_gfi = net.local(grad_first_in, gfi)
    hops = [(sum_u, j) for j in range(4)]
    closes = [(s, j) for s in (sum_u, sum_d) for j in range(4)]

    def pump(count):
        for _ in range(min(count, len(hops))):
            item, j = hops.pop(0)
            item.hop(j)

    load_wo.wait()

    def context_grad(slot):
        gather.ready(slot)
        rows = pl.ds(slot * two, two)
        dctx[rows, :] = dot_nt(gb[rows, :], wo[...]).astype(BF16)

    context_grad(0)
    gather.relay()
    pump(1)
    context_grad(1)
    context_grad(2)
    gather.relay_last()
    pump(1)
    context_grad(3)
    pump(1)
    load_qkv.wait()

    def attend_back(k):
        q_cols = slice(k * HD, (k + 1) * HD)
        k_cols = slice(sz.cols + k * HD, sz.cols + (k + 1) * HD)
        v_cols = slice(2 * sz.cols + k * HD, 2 * sz.cols + (k + 1) * HD)
        turned = qkv[:, k_cols].T

        def body(i):
            rows = tile(i, 256)
            queries, grads = qkv[rows, q_cols], dctx[rows, q_cols]
            scores = dot_nt(qkv[:, k_cols], queries) * SCALE
            exps = jnp.exp(scores - jnp.max(scores, axis=0, keepdims=True))
            probs = exps * (1.0 / jnp.sum(exps, axis=0, keepdims=True))
            value_part = dot(probs.astype(BF16), grads)
            slopes = probs * dot_nt(qkv[:, v_cols], grads)
            score_grads = (slopes - probs * jnp.sum(slopes, axis=0, keepdims=True)).astype(BF16)
            key_part = dot(score_grads, queries)
            first = i == 0
            dv[...] = jnp.where(first, value_part, dv[...] + value_part)
            dk[...] = jnp.where(first, key_part, dk[...] + key_part)
            dqkv[rows, q_cols] = (dot(turned, score_grads).T * SCALE).astype(BF16)

        loop(sz.rows_all // 256, body)
        dqkv[:, k_cols] = (dk[...] * SCALE).astype(BF16)
        dqkv[:, v_cols] = dv[...].astype(BF16)

    attend_back(0)
    pump(2)
    for k in range(1, sz.heads):
        attend_back(k)
    pump(2)
    load_wq.wait()

    sums = Scatter(net, at, sz, sum_bufs, tall=True)
    for slot in (3, 1, 2, 0):
        rows = pl.ds(slot * two, two)

        def body(i, rows=rows, slot=slot):
            cols = tile(i, 512)
            sums.put(slot, cols, dot_nt(dqkv[rows, :], wq[cols, :]))

        loop(d // 512, body)
        sums.share(slot)
        if slot == 1:
            sums.send_diag()
    sums.send_free()
    pump(1)
    load_x.wait()
    load_ctx.wait()

    def qkv_grad(i):
        rows = tile(i, 512)
        dwq[rows, :] = dot_tn(xs[:, rows], dqkv[...]).astype(BF16)

    loop(d // 512, qkv_grad)
    sum_q.start(0)
    sum_d.start(1)
    sums.send_joined()

    def out_grad(i):
        cols = tile(i, 512)
        dwo[:, cols] = dot_tn(ctx[...], gb[:, cols]).astype(BF16)

    loop(d // 512, out_grad)
    group = at.t // sz.pieces
    member = at.t - group * sz.pieces
    wo_in = []
    for k in range(sz.heads):
        for f in range(1, sz.pieces):
            other = at.index_of(f) - group * sz.pieces
            wo_in.append(
                net.remote(
                    dwo.at[pl.ds((k * sz.pieces + other) * rw, rw), :],
                    dwo_own.at[member * sz.heads + k],
                    at.peer(f),
                )
            )
        net.local(
            dwo.at[pl.ds((k * sz.pieces + member) * rw, rw), :], dwo_own.at[member * sz.heads + k]
        ).wait()
    load_gv.wait()
    for k in range(sz.heads):
        lanes = at.head_lanes(sz, at.t, k)
        gv[0:1, lanes] = jnp.sum(dqkv[:, k * HD : (k + 1) * HD].astype(F32), axis=0, keepdims=True)
        at_v = 2 * sz.cols + k * HD
        gv[1:2, lanes] = jnp.sum(dqkv[:, at_v : at_v + HD].astype(F32), axis=0, keepdims=True)
    for copy in wo_in:
        copy.wait_recv()
    sum_o.start(0)
    sum_v.start(0)
    sum_q.hop(0)
    sum_q.start(1)
    sum_o.start(1)
    sum_v.start(1)
    load_gfi.wait()
    sum_q.hop(1)
    sums.wait()

    def final(i):
        rows = tile(i, STRIP)
        ig[rows, :] = (gfi[rows, :] + sums.total(i)).astype(BF16)

    loop(t // STRIP, final)
    own_rows = pl.ds(at.zh * h, h)
    net.keep(ig.at[own_rows, :], input_grad.at[at.zh])
    ig_far = net.remote(ig.at[pl.ds((1 - at.zh) * h, h), :], input_grad.at[at.zh], at.to_h)
    for j in (2, 3):
        sum_q.hop(j)
    sum_o.hop(0)
    sum_v.hop(0)
    load_in.wait()

    for item, j in closes:
        item.close(j)
    net.keep(res_d, out_wdown)

    def rows_of(buf, member):
        return buf.at[pl.ds(member * rw, rw), :]

    def up_parts(member):
        if not sz.by_lanes:
            return [(res_u.at[pl.ds(member * rw, rw), :], out_wup.at[at.t])]
        return [
            (
                res_u.at[pl.ds(member * rw, rw), pl.ds(p * rf, rf)],
                out_wup.at[:, pl.ds(pl.multiple_of((p * TP + at.t) * rf, rf), rf)],
            )
            for p in range(sz.parts)
        ]

    def qkv_parts(member):
        return [
            (
                res_q.at[pl.ds(member * rw, rw), pl.ds(which * sz.cols + k * HD, HD)],
                target.at[:, at.head_lanes(sz, at.t, k)],
            )
            for which, target in enumerate((out_wq, out_wk, out_wv))
            for k in range(sz.heads)
        ]

    net.kept.append(net.local_parts(up_parts(at.t), rows_of(res_u, at.t)))
    back_in = [
        net.remote_parts(up_parts(at.index_of(f)), rows_of(res_u, at.index_of(f)), at.peer(f)) for f in flips
    ]
    for j in range(4):
        sum_q.close(j)
    net.kept.append(net.local_parts(qkv_parts(at.t), rows_of(res_q, at.t)))
    back_in += [
        net.remote_parts(qkv_parts(at.index_of(f)), rows_of(res_q, at.index_of(f)), at.peer(f)) for f in flips
    ]
    sum_o.close(0)
    net.keep(res_o, out_wo)
    sum_v.close(0)

    def lanes_of(index):
        return pl.ds(pl.multiple_of(index // sz.pieces * HD, HD), HD)

    vec_got[at.t] = res_v[0:8, lanes_of(at.t)]
    vec_in = [
        net.remote(res_v.at[pl.ds(0, 8), lanes_of(at.index_of(f))], vec_got.at[at.t], at.peer(f)) for f in flips
    ]
    bup_out[...] = res_v[8:16, 0:rf]
    net.keep(bup_out, out_bup)
    for copy in vec_in:
        copy.wait_recv()
    total = vec_got[0]
    for member in range(1, TP):
        total = total + vec_got[member]
    vec_sum[...] = total
    net.keep(vec_sum, out_vec)
    for copy in back_in:
        copy.wait_recv()
    ig_far.wait_recv()
    net.finish()


def attention_backward(sz, *args):
    t, d, r = sz.tokens, sz.width, sz.rows_all
    rw, rf = sz.row_shard, sz.hid_shard
    wide = 3 * sz.cols
    shape = jax.ShapeDtypeStruct
    anywhere = pl.BlockSpec(memory_space=pl.ANY)
    outs = (
        shape((2, sz.half, d), BF16),
        shape((rw, d), BF16),
        shape((rw, d), BF16),
        shape((rw, d), BF16),
        shape((rw, d), BF16),
        shape((rw, sz.hidden) if sz.by_lanes else (TP, rw, sz.hid), BF16),
        shape((rf, d), BF16),
        shape((8, HD), F32),
        shape((8, rf), F32),
    )
    scratch = [
        pltpu.VMEM((r, d), BF16),
        pltpu.VMEM((r, d), BF16),
        pltpu.VMEM((d, wide), BF16),
        pltpu.VMEM((sz.cols, d), BF16),
        pltpu.VMEM((r, wide), BF16),
        pltpu.VMEM((r, sz.cols), BF16),
        pltpu.VMEM((t, d), F32),
        pltpu.VMEM((16, d), F32),
        pltpu.VMEM((r, sz.cols), BF16),
        pltpu.VMEM((r, wide), BF16),
        pltpu.VMEM((r, HD), F32),
        pltpu.VMEM((r, HD), F32),
        pltpu.VMEM((t, d), BF16),
        pltpu.VMEM((d, wide), BF16),
        pltpu.VMEM((sz.cols, d), BF16),
        pltpu.VMEM((sz.parts, rw, d), BF16),
        pltpu.VMEM((sz.slab, wide), BF16),
        pltpu.VMEM((rw, d), BF16),
        pltpu.VMEM((sz.slab, sz.hid), BF16),
        pltpu.VMEM((rf, d), BF16),
        pltpu.VMEM((16, sz.slab), F32),
        pltpu.VMEM((TP, 8, HD), F32),
        pltpu.VMEM((8, HD), F32),
        pltpu.VMEM((8, rf), F32),
        *Scatter.scratch(sz),
        *Reduce.scratch(sz, sz.slab, sz.hid, BF16, False),
        *Reduce.scratch(sz, rf, d, BF16, False),
        *Reduce.scratch(sz, sz.slab, wide, BF16, True),
        *Reduce.scratch(sz, rw, d, BF16, True),
        *Reduce.scratch(sz, 16, sz.slab, F32, True),
        pltpu.SemaphoreType.DMA((70 + 28 * sz.nx,)),
        pltpu.SemaphoreType.DMA((70 + 28 * sz.nx,)),
        pltpu.SemaphoreType.DMA((48,)),
    ]
    return pl.pallas_call(
        functools.partial(attention_backward_kernel, sz),
        out_shape=outs,
        in_specs=[anywhere] * 12,
        out_specs=[anywhere] * len(outs),
        scratch_shapes=scratch,
        compiler_params=pltpu.CompilerParams(
            collective_id=2, has_side_effects=True, vmem_limit_bytes=VMEM_LIMIT
        ),
        name="attention_backward",
    )(*args)


def widen_kernel(count, *refs):
    for src, dst in zip(refs[:count], refs[count:]):
        flat = len(src.shape) == 2

        def body(i, src=src, dst=dst, flat=flat):
            if flat:
                dst[tile(i, STRIP), :] = src[tile(i, STRIP), :].astype(F32)
            else:
                for j in range(src.shape[0]):
                    dst[j, tile(i, STRIP), :] = src[j, tile(i, STRIP), :].astype(F32)

        loop(src.shape[-2] // STRIP, body)


def widen(*arrays):
    whole = pl.BlockSpec(memory_space=pltpu.VMEM)
    return pl.pallas_call(
        functools.partial(widen_kernel, len(arrays)),
        out_shape=[jax.ShapeDtypeStruct(a.shape, F32) for a in arrays],
        in_specs=[whole] * len(arrays),
        out_specs=[whole] * len(arrays),
        compiler_params=pltpu.CompilerParams(vmem_limit_bytes=VMEM_LIMIT),
        name="widen",
    )(*arrays)


def per_device(
    sz, inputs, cotangent, w_query, w_key, w_value, w_out, b_query, b_value, b_out, ln1_gain, ln1_bias,
    w_up, b_up, w_down, b_down, ln2_gain, ln2_bias,
):
    rw, rf = sz.row_shard, sz.hid_shard
    t = lax.axis_index("zl") * 4 + lax.axis_index("y") * 2 + lax.axis_index("c")
    p = lax.axis_index("x") * 2 + lax.axis_index("zh")
    piece = t % sz.pieces
    rows = jnp.stack([b_query, b_value, b_out, ln1_gain, ln1_bias, b_down, ln2_gain, ln2_bias]).astype(F32)
    here = lax.broadcasted_iota(jnp.int32, (8, HD), 1) // rw == piece
    low = jnp.where(here, jnp.tile(rows, (1, sz.pieces)), 0.0)
    up = b_up.astype(F32)
    if rf >= HD:
        high = jnp.pad(up.reshape(rf // HD, HD), ((0, 8 - rf // HD), (0, 0)))
    else:
        each = HD // rf
        here = lax.broadcasted_iota(jnp.int32, (8, HD), 1) // rf == p % each
        high = jnp.where(here, jnp.tile(up[None], (8, each)), 0.0)
    vec_pack = jnp.concatenate([low, high], axis=0)

    up_rows = w_up
    if not sz.by_lanes:
        up_rows = w_up.reshape(rw, sz.parts, TP, rf).transpose(2, 0, 1, 3).reshape(TP, rw, sz.hid)

    x_all, wqkv, w_out_own, up_own, down_own, vec_all, bup_all, qkv, ctx, first_in, first_low = attention_forward(
        sz, inputs, w_query, w_key, w_value, w_out, up_rows, w_down, vec_pack
    )
    outputs, grad_first_in, grad_low, grad_up, grad_down, grad_vec, down_sum, down_in = feed_forward(
        sz, first_low, first_in, up_own, down_own, vec_all, bup_all, cotangent, w_down
    )
    *grads, out_vec, out_bup = attention_backward(
        sz, grad_low, grad_first_in, x_all, wqkv, w_out_own, qkv, ctx, grad_up, grad_down, grad_vec,
        down_sum, down_in,
    )
    input_grad, grad_wq, grad_wk, grad_wv, grad_wo, grad_wup, grad_wdown = widen(*grads)
    if not sz.by_lanes:
        grad_wup = grad_wup.reshape(TP, rw, sz.parts, rf).transpose(1, 2, 0, 3).reshape(rw, sz.hidden)
    vec = lax.dynamic_slice(out_vec, (0, piece * rw), (8, rw))
    return (
        outputs,
        input_grad,
        grad_wq,
        grad_wk,
        grad_wv,
        grad_wo,
        vec[0],
        vec[1],
        vec[2],
        vec[3],
        vec[4],
        grad_wup,
        out_bup[0],
        grad_wdown,
        vec[5],
        vec[6],
        vec[7],
    )


def solution(mesh):
    nx = mesh.shape["dp"]
    plane = Mesh(mesh.devices.reshape(nx, 2, mesh.shape["hd"] // 2, 2, mesh.shape["sq"] // 2), AXES)
    rows, matrix, vector = P("x", AXES[1:], None), P(AXES, None), P(AXES)

    def run(*args):
        batch, length, width = args[0].shape
        sz = Sizes(nx, width, args[11].shape[1], batch // nx * length // (2 * TP))
        call = jax.shard_map(
            functools.partial(per_device, sz),
            mesh=plane,
            in_specs=(rows, rows) + (matrix,) * 4 + (vector,) * 5 + (matrix, vector, matrix) + (vector,) * 3,
            out_specs=(rows, rows) + (matrix,) * 4 + (vector,) * 5 + (matrix, vector, matrix) + (vector,) * 3,
            check_vma=False,
        )
        return call(*args)

    return run
```

```python
import functools

import jax
import jax.numpy as jnp
from jax import lax
from jax.experimental import pallas as pl
from jax.experimental.pallas import tpu as pltpu
from jax.sharding import Mesh
from jax.sharding import PartitionSpec as P

F32 = jnp.float32
BF16 = jnp.bfloat16
HD = 128
EPSILON = 1e-12
TP = 8
STRIP = 16
VMEM_LIMIT = 60 * 2**20
AXES = ("x", "zh", "zl", "y", "c")
SCALE = HD ** (-0.5)


class Sizes:
    def __init__(self, groups_x, width, hidden, tokens):
        self.nx = groups_x
        self.parts = 2 * groups_x
        self.width = width
        self.hidden = hidden
        self.tokens = tokens
        self.half = tokens // 2
        self.rows_all = TP * tokens
        self.row_shard = width // (TP * self.parts)
        self.hid_shard = hidden // (TP * self.parts)
        self.pieces = HD // self.row_shard
        self.heads = width // HD // TP
        self.cols = self.heads * HD
        self.hid = hidden // TP
        self.slab = width // self.parts
        self.by_lanes = self.hid_shard % HD == 0


class Place:
    def __init__(self, sizes):
        self.x, self.zh, self.zl, self.y, self.c = (lax.axis_index(a) for a in AXES)
        self.nx = sizes.nx
        self.t = self.zl * 4 + self.y * 2 + self.c
        self.p = self.x * 2 + self.zh
        self.pz = self.x * 2 + (1 - self.zh)
        self.to_c = {"c": 1 - self.c}
        self.to_y = {"y": 1 - self.y}
        self.to_z = {"zl": 1 - self.zl}
        self.to_h = {"zh": 1 - self.zh}

    def peer(self, flip):
        target = {}
        if flip & 4:
            target["zl"] = 1 - self.zl
        if flip & 2:
            target["y"] = 1 - self.y
        if flip & 1:
            target["c"] = 1 - self.c
        return target

    def index_of(self, flip):
        zl = 1 - self.zl if flip & 4 else self.zl
        y = 1 - self.y if flip & 2 else self.y
        c = 1 - self.c if flip & 1 else self.c
        return zl * 4 + y * 2 + c

    def head_lanes(self, sz, member, k):
        group = member // sz.pieces
        head = ((member - group * sz.pieces) * sz.heads + k) * (TP // sz.pieces) + group
        return pl.ds(pl.multiple_of(head * HD, HD), HD)

    def to_x(self, step):
        return {"x": lax.rem(self.x + step, self.nx)}

    def x_of(self, step):
        return lax.rem(self.x + step, self.nx)


class Copies:
    def __init__(self, send, recv, local):
        self.send, self.recv, self.local_sems = send, recv, local
        self.n_remote = 0
        self.n_local = 0
        self.sent = []
        self.kept = []

    def remote(self, src, dst, target):
        i = self.n_remote
        self.n_remote += 1
        copy = pltpu.make_async_remote_copy(
            src_ref=src,
            dst_ref=dst,
            send_sem=self.send.at[i],
            recv_sem=self.recv.at[i],
            device_id=target,
            device_id_type=pl.DeviceIdType.MESH,
        )
        copy.start()
        self.sent.append(copy)
        return copy

    def remote_parts(self, pairs, whole, target):
        i = self.n_remote
        self.n_remote += 1

        def copy(src, dst):
            return pltpu.make_async_remote_copy(
                src_ref=src,
                dst_ref=dst,
                send_sem=self.send.at[i],
                recv_sem=self.recv.at[i],
                device_id=target,
                device_id_type=pl.DeviceIdType.MESH,
            )

        for src, dst in pairs:
            copy(src, dst).start()
        total = copy(whole, whole)
        self.sent.append(total)
        return total

    def local_parts(self, pairs, whole):
        i = self.n_local
        self.n_local += 1
        for src, dst in pairs:
            pltpu.make_async_copy(src, dst, self.local_sems.at[i]).start()
        return pltpu.make_async_copy(whole, whole, self.local_sems.at[i])

    def local(self, src, dst):
        i = self.n_local
        self.n_local += 1
        copy = pltpu.make_async_copy(src, dst, self.local_sems.at[i])
        copy.start()
        return copy

    def keep(self, src, dst):
        self.kept.append(self.local(src, dst))

    def left(self, copy):
        copy.wait_send()
        self.sent = [other for other in self.sent if other is not copy]

    def finish(self):
        for copy in self.kept:
            copy.wait()
        for copy in self.sent:
            copy.wait_send()


def greet(targets):
    barrier = pltpu.get_barrier_semaphore()
    for target in targets:
        pl.semaphore_signal(
            barrier, inc=1, device_id=target, device_id_type=pl.DeviceIdType.MESH
        )
    pl.semaphore_wait(barrier, len(targets))


def dot(left, right):
    return jnp.dot(left, right, preferred_element_type=F32)


def dot_nt(left, right):
    return lax.dot_general(left, right, (((1,), (1,)), ((), ())), preferred_element_type=F32)


def dot_tn(left, right):
    return lax.dot_general(left, right, (((0,), (0,)), ((), ())), preferred_element_type=F32)


def tile(i, size):
    return pl.ds(pl.multiple_of(i * size, size), size)


def loop(count, body):
    def step(i, carry):
        body(i)
        return carry

    lax.fori_loop(0, count, step, 0)


def normed(values):
    average = jnp.mean(values, axis=1, keepdims=True)
    centred = values - average
    variance = jnp.mean(centred * centred, axis=1, keepdims=True)
    scale = lax.rsqrt(variance + EPSILON)
    return centred * scale, scale


def normed_back(grad, xhat, scale):
    along = jnp.mean(grad * xhat, axis=1, keepdims=True)
    return scale * (grad - jnp.mean(grad, axis=1, keepdims=True) - xhat * along)


class Gather:
    def __init__(self, net, at, sz, buf, start, count, tall=False):
        self.net, self.at, self.sz, self.buf = net, at, sz, buf
        self.start, self.count, self.tall = start, count, tall
        half = sz.width // 2
        self.cols = (pl.ds(0, half), pl.ds(half, half))
        self.sib = [None] * 4

    def part(self, slot, core, cols=None):
        rows = pl.ds((slot * 2 + core) * self.sz.tokens + self.start, self.count)
        return self.buf.at[rows, :] if cols is None else self.buf.at[rows, cols]

    def send(self):
        net, at = self.net, self.at
        self.from_y = [None, None]
        self.from_z = [None, None]
        for h in (0, 1):
            self.from_y[h] = net.remote(
                self.part(0, 0, self.cols[h]), self.part(1, 0, self.cols[h]), at.to_y
            )
            self.from_z[1 - h] = net.remote(
                self.part(0, 0, self.cols[1 - h]), self.part(2, 0, self.cols[1 - h]), at.to_z
            )
        self.share(0)

    def share(self, slot):
        self.sib[slot] = self.net.remote(self.part(slot, 0), self.part(slot, 1), self.at.to_c)

    def relay(self):
        net, at = self.net, self.at
        if self.tall:
            to_y = []
            for h in (1, 0):
                self.from_z[h].wait_recv()
                to_y.append(
                    net.remote(
                        self.part(2, 0, self.cols[h]), self.part(3, 0, self.cols[h]), at.to_y
                    )
                )
            self.diag = tuple(to_y)
            self.share(2)
            for copy in self.from_y:
                copy.wait_recv()
            self.share(1)
            return
        self.from_y[0].wait_recv()
        to_z = net.remote(
            self.part(1, 0, self.cols[0]), self.part(3, 0, self.cols[0]), at.to_z
        )
        self.from_z[1].wait_recv()
        to_y = net.remote(
            self.part(2, 0, self.cols[1]), self.part(3, 0, self.cols[1]), at.to_y
        )
        self.diag = (to_z, to_y)
        self.from_y[1].wait_recv()
        self.share(1)
        self.from_z[0].wait_recv()
        self.share(2)

    def relay_last(self):
        for copy in self.diag:
            copy.wait_recv()
        self.share(3)

    def ready(self, slot):
        self.sib[slot].wait_recv()


class Scatter:
    def __init__(self, net, at, sz, bufs, tall=False):
        self.net, self.at, self.sz, self.tall = net, at, sz, tall
        self.mine, self.theirs, self.got, self.diag, self.diag_got, self.out, self.inn = bufs
        self.sib = [None] * 4

    @staticmethod
    def scratch(sz):
        t, d = sz.tokens, sz.width
        return [
            pltpu.VMEM((4 * t, d), F32),
            pltpu.VMEM((4 * t, d), BF16),
            pltpu.VMEM((4 * t, d), BF16),
            pltpu.VMEM((t, d), BF16),
            pltpu.VMEM((t, d), BF16),
            pltpu.VMEM((2 * t, d), BF16),
            pltpu.VMEM((2 * t, d), BF16),
        ]

    def put(self, slot, cols, value):
        t = self.sz.tokens
        self.mine[pl.ds(slot * t, t), cols] = value[:t]
        self.theirs[pl.ds(slot * t, t), cols] = value[t:].astype(BF16)

    def share(self, slot):
        rows = pl.ds(slot * self.sz.tokens, self.sz.tokens)
        self.sib[slot] = self.net.remote(self.theirs.at[rows, :], self.got.at[rows, :], self.at.to_c)

    def add(self, slot, start, count, dst, dst_start, extra=None):
        base = slot * self.sz.tokens + start

        def body(i):
            rows = pl.ds(pl.multiple_of(base + i * STRIP, STRIP), STRIP)
            total = self.mine[rows, :] + self.got[rows, :].astype(F32)
            if extra is not None:
                there = pl.ds(pl.multiple_of(start + i * STRIP, STRIP), STRIP)
                total = total + extra[there, :].astype(F32)
            dst[pl.ds(pl.multiple_of(dst_start + i * STRIP, STRIP), STRIP), :] = total.astype(BF16)

        loop(count // STRIP, body)

    def send_diag(self):
        net, at, h = self.net, self.at, self.sz.half
        self.sib[3].wait_recv()
        self.add(3, 0, 2 * h, self.diag, 0)
        low, high = pl.ds(0, h), pl.ds(h, h)
        self.d_low = net.remote(self.diag.at[low, :], self.diag_got.at[low, :], at.to_y)
        self.d_high = net.remote(
            self.diag.at[high, :], self.diag_got.at[high, :], at.to_y if self.tall else at.to_z
        )

    def half_out(self, side, start, target):
        rows = pl.ds(side * self.sz.tokens + start, self.sz.half)
        return self.net.remote(self.out.at[rows, :], self.inn.at[rows, :], target)

    def send_free(self):
        at, t, h = self.at, self.sz.tokens, self.sz.half
        self.sib[1].wait_recv()
        self.add(1, 0, h, self.out, 0)
        self.y_low = self.half_out(0, 0, at.to_y)
        if self.tall:
            self.add(1, h, h, self.out, h)
            self.y_high = self.half_out(0, h, at.to_y)
            return
        self.sib[2].wait_recv()
        self.add(2, h, h, self.out, t + h)
        self.z_high = self.half_out(1, h, at.to_z)

    def send_joined(self):
        at, t, h = self.at, self.sz.tokens, self.sz.half
        if self.tall:
            self.sib[2].wait_recv()
            self.d_low.wait_recv()
            self.add(2, 0, h, self.out, t, self.diag_got)
            self.z_low = self.half_out(1, 0, at.to_z)
            self.d_high.wait_recv()
            self.add(2, h, h, self.out, t + h, self.diag_got)
            self.z_high = self.half_out(1, h, at.to_z)
            return
        self.d_high.wait_recv()
        self.add(1, h, h, self.out, h, self.diag_got)
        self.y_high = self.half_out(0, h, at.to_y)
        self.d_low.wait_recv()
        self.add(2, 0, h, self.out, t, self.diag_got)
        self.z_low = self.half_out(1, 0, at.to_z)

    def settle(self):
        for copy in [*self.sib, self.d_low, self.d_high, self.y_low, self.z_high, self.y_high, self.z_low]:
            self.net.left(copy)

    def wait(self):
        self.sib[0].wait_recv()
        for copy in (self.y_low, self.z_high, self.y_high, self.z_low):
            copy.wait_recv()

    def total(self, i):
        t = self.sz.tokens
        rows = tile(i, STRIP)
        far = pl.ds(pl.multiple_of(t + i * STRIP, STRIP), STRIP)
        return (
            self.mine[rows, :]
            + self.got[rows, :].astype(F32)
            + self.inn[rows, :].astype(F32)
            + self.inn[far, :].astype(F32)
        )


class Spread:
    def __init__(self, net, at, view, source=None):
        self.net, self.at, self.view = net, at, view
        self.source = view(at.p) if source is None else source
        self.relayed = []

    def across(self):
        self.from_h = self.net.remote(self.source, self.view(self.at.p), self.at.to_h)

    def along(self):
        self.from_x = [
            self.net.remote(self.source, self.view(self.at.p), self.at.to_x(step))
            for step in range(1, self.at.nx)
        ]

    def relay(self):
        self.from_h.wait_recv()
        there = self.view(self.at.pz)
        self.relayed = [
            self.net.remote(there, there, self.at.to_x(step)) for step in range(1, self.at.nx)
        ]

    def near(self):
        for copy in self.from_x:
            copy.wait_recv()

    def far(self):
        for copy in self.relayed:
            copy.wait_recv()


def attention_forward_kernel(
    sz,
    xin, w_query, w_key, w_value, wout, wup_rows, wdown, vec_pack,
    x_all, wqkv, w_out_own, w_up, w_down, vec_all, bup_all, qkv_all, ctx_all, first_in, first_low,
    xs, wq, wo_got, wo, vecs, vec, bup, acc, qkv, ctx, fin, first, wu_own, wd_own, *rest,
):
    *sum_bufs, send, recv, local = rest
    at = Place(sz)
    net = Copies(send, recv, local)
    t, d, h = sz.tokens, sz.width, sz.half
    rw, rf = sz.row_shard, sz.hid_shard
    flips = range(1, TP)
    greet(
        [at.peer(f) for f in flips] + [at.to_h] + [at.to_x(s) for s in range(1, sz.nx)]
    )

    own_rows = pl.ds(at.zh * h, h)
    from_h = net.remote(xin.at[1 - at.zh], xs.at[own_rows, :], at.to_h)
    own_x = net.local(xin.at[at.zh], xs.at[own_rows, :])

    def wq_rows(p, member, count=1):
        return pl.ds((p * TP + member) * rw, count * rw)

    def wq_parts(member):
        return [
            (
                source.at[:, at.head_lanes(sz, member, k)],
                wq.at[wq_rows(at.p, at.t), pl.ds(which * sz.cols + k * HD, HD)],
            )
            for which, source in enumerate((w_query, w_key, w_value))
            for k in range(sz.heads)
        ]

    def wu_parts(member, dst):
        if not sz.by_lanes:
            return [(wup_rows.at[member], dst)]
        return [
            (
                wup_rows.at[:, pl.ds(pl.multiple_of((p * TP + member) * rf, rf), rf)],
                dst.at[:, pl.ds(p * rf, rf)],
            )
            for p in range(sz.parts)
        ]

    wq_mine, wu_mine = wq.at[wq_rows(at.p, at.t), :], w_up.at[wq_rows(at.p, at.t), :]
    own_wq = net.local_parts(wq_parts(at.t), wq_mine)
    own_vec = net.local(vec_pack, vecs.at[at.p * TP + at.t])
    own_wo = net.local(wout, wo_got.at[at.p])
    wu_here = net.local_parts(wu_parts(at.t, wu_own), wu_own)
    wd_here = net.local(wdown.at[pl.ds(0, rf // 2), :], wd_own)
    wq_in = [None] + [
        net.remote_parts(wq_parts(at.index_of(f)), wq_mine, at.peer(f)) for f in flips
    ]
    vec_in = [net.remote(vec_pack, vecs.at[at.p * TP + at.t], at.peer(f)) for f in flips]
    own_x.wait()
    near_rows = Gather(net, at, sz, xs, at.zh * h, h, tall=True)
    near_rows.send()

    def chip_block(buf, f):
        member = at.index_of(f) - at.c
        return lambda p: buf.at[wq_rows(p, member, 2), :]

    wq_spread = [Spread(net, at, chip_block(wq, f)) for f in (0, 2, 4, 6)]
    for f, item in zip((0, 2, 4, 6), wq_spread):
        if f == 0:
            own_wq.wait()
        else:
            wq_in[f].wait_recv()
        wq_in[f + 1].wait_recv()
        item.across()
        item.along()
    own_vec.wait()
    for copy in vec_in:
        copy.wait_recv()
    vec_spread = Spread(net, at, lambda p: vecs.at[pl.ds(p * TP, TP)])
    wo_spread = Spread(net, at, lambda p: wo_got.at[p], wout)
    vec_spread.across()
    vec_spread.along()
    wo_spread.along()
    from_h.wait_recv()
    far_rows = Gather(net, at, sz, xs, (1 - at.zh) * h, h, tall=True)
    far_rows.send()
    near_rows.relay()
    far_rows.relay()
    wq_spread[0].relay()
    near_rows.relay_last()
    far_rows.relay_last()
    vec_spread.relay()
    wq_spread[1].relay()
    wo_spread.across()
    wu_here.wait()
    own_wu = net.local(wu_own, w_up.at[wq_rows(at.p, at.t), :])
    wd_here.wait()
    net.keep(wd_own, w_down.at[pl.ds(at.p * (rf // 2), rf // 2), :])
    wu_in = [None] + [
        net.remote_parts(wu_parts(at.index_of(f), wu_mine), wu_mine, at.peer(f)) for f in flips
    ]

    def accumulate(zh, first_part):
        def body(i):
            rows = tile(i, 256)
            total = jnp.zeros((256, 3 * sz.cols), F32) if first_part else acc[rows, :]
            for x in range(sz.nx):
                block = tile(x * 2 + zh, sz.slab)
                total = total + dot(xs[rows, block], wq[block, :])
            acc[rows, :] = total

        loop(sz.rows_all // 256, body)

    for slot in range(4):
        near_rows.ready(slot)
        far_rows.ready(slot)
    for item in wq_spread:
        item.near()
    net.keep(xs, x_all)
    accumulate(at.zh, True)
    for item in wq_spread[2:]:
        item.relay()
    wd_chunk = rf // 4
    wd_spread = [
        Spread(
            net,
            at,
            lambda p, j=j: w_down.at[pl.ds(p * 2 * wd_chunk + j * wd_chunk, wd_chunk), :],
            wdown.at[pl.ds(j * wd_chunk, wd_chunk), :],
        )
        for j in range(2)
    ]
    for item in wd_spread:
        item.across()
    vec_spread.near()
    vec_spread.far()
    for j in range(d // HD):
        piece = vecs[j * sz.pieces, 0:8]
        for k in range(1, sz.pieces):
            piece = piece + vecs[j * sz.pieces + k, 0:8]
        vec[:, j * HD : (j + 1) * HD] = piece
    if rf >= HD:
        for p in range(sz.parts):
            for j in range(rf // HD):
                lanes = pl.ds(p * rf + j * HD, HD)
                bup[0:1, lanes] = vecs[p * TP + at.t, 8 + j : 9 + j]
    else:
        for j in range(sz.hid // HD):
            each = HD // rf
            row = vecs[j * each * TP + at.t, 8:9]
            for k in range(1, each):
                row = row + vecs[(j * each + k) * TP + at.t, 8:9]
            bup[0:1, j * HD : (j + 1) * HD] = row
    net.keep(vec, vec_all)
    net.keep(bup, bup_all)
    for item in wq_spread:
        item.far()
    accumulate(1 - at.zh, False)
    wo_spread.relay()
    for item in wd_spread:
        item.along()

    group = at.t // sz.pieces
    member = at.t - group * sz.pieces
    for k in range(sz.heads):
        lanes = at.head_lanes(sz, at.t, k)

        def biased(i, k=k, lanes=lanes):
            rows = tile(i, 256)
            for which in range(3):
                cols = slice(which * sz.cols + k * HD, which * sz.cols + (k + 1) * HD)
                value = acc[rows, cols]
                if which != 1:
                    value = value + vec[which // 2 : which // 2 + 1, lanes]
                qkv[rows, cols] = value.astype(BF16)

        loop(sz.rows_all // 256, biased)
    net.keep(wq, wqkv)
    net.keep(qkv, qkv_all)

    def attend(k):
        q_cols = slice(k * HD, (k + 1) * HD)
        k_cols = slice(sz.cols + k * HD, sz.cols + (k + 1) * HD)
        v_cols = slice(2 * sz.cols + k * HD, 2 * sz.cols + (k + 1) * HD)

        def body(i):
            rows = tile(i, 256)
            scores = dot_nt(qkv[rows, q_cols], qkv[:, k_cols]) * SCALE
            top = jnp.max(scores, axis=1, keepdims=True)
            exps = jnp.exp(scores - top)
            probs = exps * (1.0 / jnp.sum(exps, axis=1, keepdims=True))
            ctx[rows, q_cols] = dot(probs.astype(BF16), qkv[:, v_cols]).astype(BF16)

        loop(sz.rows_all // 256, body)

    for k in range(sz.heads):
        attend(k)
    net.keep(ctx, ctx_all)

    own_wo.wait()
    wo_spread.near()
    wo_spread.far()

    def wo_rows(k, piece):
        return pl.ds((k * sz.pieces + piece) * rw, rw)

    for k in range(sz.heads):
        net.local(wo_got.at[member * sz.heads + k], wo.at[wo_rows(k, member), :]).wait()
    wo_in = []
    for f in range(1, sz.pieces):
        other = at.index_of(f) - group * sz.pieces
        for k in range(sz.heads):
            wo_in.append(
                net.remote(wo_got.at[other * sz.heads + k], wo.at[wo_rows(k, member), :], at.peer(f))
            )
    for copy in wo_in:
        copy.wait_recv()
    net.keep(wo, w_out_own)
    wu_spread = [Spread(net, at, chip_block(w_up, f)) for f in (0, 2, 4, 6)]
    own_wu.wait()
    for f, item in zip((0, 2, 4, 6), wu_spread):
        if f:
            wu_in[f].wait_recv()
        wu_in[f + 1].wait_recv()
        item.across()
    for item in wu_spread:
        item.along()

    sums = Scatter(net, at, sz, sum_bufs, tall=True)
    for slot in (3, 1, 2, 0):
        rows = pl.ds(slot * 2 * t, 2 * t)

        def body(i, rows=rows, slot=slot):
            cols = tile(i, 512)
            sums.put(slot, cols, dot(ctx[rows, :], wo[:, cols]))

        loop(d // 512, body)
        sums.share(slot)
        if slot == 3:
            sums.send_diag()
    sums.send_free()
    sums.send_joined()
    for item in wd_spread:
        item.relay()
    sums.wait()

    def norm(i):
        rows = tile(i, STRIP)
        value = xs[rows, :].astype(F32) + sums.total(i) + vec[2:3, :]
        fin[rows, :] = value
        xhat, _ = normed(value)
        first[rows, :] = (xhat * vec[3:4, :] + vec[4:5, :]).astype(BF16)

    loop(t // STRIP, norm)
    net.keep(fin, first_in)
    net.keep(first, first_low)
    for item in wu_spread[:3]:
        item.relay()
    wu_spread[3].from_h.wait_recv()
    for item in wu_spread + wd_spread:
        item.near()
        item.far()
    net.finish()


def attention_forward(sz, *args):
    t, d, r = sz.tokens, sz.width, sz.rows_all
    shape = jax.ShapeDtypeStruct
    anywhere = pl.BlockSpec(memory_space=pl.ANY)
    outs = (
        shape((r, d), BF16),
        shape((d, 3 * sz.cols), BF16),
        shape((sz.cols, d), BF16),
        shape((d, sz.hid), BF16),
        shape((sz.hid // 2, d), BF16),
        shape((8, d), F32),
        shape((8, sz.hid), F32),
        shape((r, 3 * sz.cols), BF16),
        shape((r, sz.cols), BF16),
        shape((t, d), F32),
        shape((t, d), BF16),
    )
    scratch = [
        pltpu.VMEM((r, d), BF16),
        pltpu.VMEM((d, 3 * sz.cols), BF16),
        pltpu.VMEM((sz.parts, sz.row_shard, d), BF16),
        pltpu.VMEM((sz.cols, d), BF16),
        pltpu.VMEM((sz.parts * TP, 16, HD), F32),
        pltpu.VMEM((8, d), F32),
        pltpu.VMEM((8, sz.hid), F32),
        pltpu.VMEM((r, 3 * sz.cols), F32),
        pltpu.VMEM((r, 3 * sz.cols), BF16),
        pltpu.VMEM((r, sz.cols), BF16),
        pltpu.VMEM((t, d), F32),
        pltpu.VMEM((t, d), BF16),
        pltpu.VMEM((sz.row_shard, sz.hid), BF16),
        pltpu.VMEM((sz.hid_shard // 2, d), BF16),
        *Scatter.scratch(sz),
        pltpu.SemaphoreType.DMA((80 + 28 * sz.nx,)),
        pltpu.SemaphoreType.DMA((80 + 28 * sz.nx,)),
        pltpu.SemaphoreType.DMA((24,)),
    ]
    return pl.pallas_call(
        functools.partial(attention_forward_kernel, sz),
        out_shape=outs,
        in_specs=[anywhere] * 8,
        out_specs=[anywhere] * len(outs),
        scratch_shapes=scratch,
        compiler_params=pltpu.CompilerParams(
            collective_id=0, has_side_effects=True, vmem_limit_bytes=VMEM_LIMIT
        ),
        name="attention_forward",
    )(*args)


GELU_A = 0.7978845608028654
GELU_B = 0.044715


def gate(values):
    inner = jnp.tanh(GELU_A * (values + GELU_B * values * values * values))
    return 0.5 * values * (1.0 + inner)


def gate_slope(values):
    square = values * values
    inner = jnp.tanh(GELU_A * (values + GELU_B * square * values))
    rise = GELU_A * (1.0 + 3.0 * GELU_B * square)
    return 0.5 * (1.0 + inner) + 0.5 * values * (1.0 - inner * inner) * rise


def feed_forward_kernel(
    sz,
    first_low, first_in, w_up, w_down_half, vec_all, bup_all, cot_in, wdown,
    outputs, grad_first_in, grad_low, grad_w_up, grad_w_down, grad_vec, down_sum, down_in,
    fa, wu, wd, vec, bup, fin, cot, hid, act, gh, g2, g2s, out, gv, dwu, dwd, *rest,
):
    *bufs, send, recv, local = rest
    sum_bufs, bufs = bufs[:7], bufs[7:]
    at = Place(sz)
    net = Copies(send, recv, local)
    t, d, h = sz.tokens, sz.width, sz.half
    two = 2 * t
    rf = sz.hid_shard
    load_first = net.local(first_low, fa.at[pl.ds(0, t), :])

    def up_rows(p, f):
        start = (p * TP + at.index_of(f) - at.c) * sz.row_shard
        return pl.ds(pl.multiple_of(start, 2 * sz.row_shard), 2 * sz.row_shard)

    load_up = []
    for step in range(sz.nx):
        for zh in (at.zh, 1 - at.zh):
            for f in (0, 2, 4, 6):
                if step == 0 or zh is at.zh or f != 6:
                    rows = up_rows(at.x_of(step) * 2 + zh, f)
                    load_up.append(net.local(w_up.at[rows, :], wu.at[rows, :]))
    load_bup = net.local(bup_all, bup)
    load_down = [
        net.local(w_down_half.at[pl.ds(p * (rf // 2), rf // 2), :], wd.at[pl.ds(p * rf, rf // 2), :])
        for p in range(sz.parts)
    ]
    late_own = pl.ds(at.p * rf + rf // 2, rf // 2)
    load_down.append(net.local(wdown.at[pl.ds(rf // 2, rf // 2), :], wd.at[late_own, :]))
    load_vec = net.local(vec_all, vec)
    load_fin = net.local(first_in, fin)
    own_rows = pl.ds(at.zh * h, h)
    load_cot = net.local(cot_in.at[at.zh], cot.at[own_rows, :])
    greet([at.to_c, at.to_y, at.to_z, at.to_h] + [at.to_x(s) for s in range(1, sz.nx)])
    load_first.wait()
    firsts = Gather(net, at, sz, fa, 0, t, tall=True)
    firsts.send()
    wd_chunk = rf // 4
    wd_spread = [
        Spread(
            net,
            at,
            lambda p, j=j: wd.at[pl.ds(p * rf + j * wd_chunk, wd_chunk), :],
            wdown.at[pl.ds(j * wd_chunk, wd_chunk), :],
        )
        for j in (2, 3)
    ]
    last_up = [
        net.remote(w_up.at[up_rows(at.pz, 6), :], wu.at[up_rows(at.pz, 6), :], at.to_x(step))
        for step in range(1, sz.nx)
    ]
    for item in wd_spread:
        item.across()
        item.along()
    gv[...] = jnp.zeros_like(gv)

    sums = Scatter(net, at, sz, sum_bufs)
    load_bup.wait()
    for copy in load_up:
        copy.wait()
    for copy in last_up:
        copy.wait_recv()

    def project_up(slot):
        firsts.ready(slot)
        rows = pl.ds(slot * two, two)

        def up(i):
            cols = tile(i, 512)
            value = dot(fa[rows, :], wu[:, cols]) + bup[0:1, cols]
            hid[rows, cols] = value
            act[rows, cols] = gate(value).astype(BF16)

        loop(sz.hid // 512, up)

    project_up(0)
    firsts.relay()
    wd_spread[0].relay()
    project_up(2)
    project_up(1)
    firsts.relay_last()
    project_up(3)
    wd_spread[1].relay()
    cot_far = net.remote(cot_in.at[1 - at.zh], cot.at[own_rows, :], at.to_h)
    for copy in load_down:
        copy.wait()
    for item in wd_spread:
        item.near()
        item.far()
    for slot in (3, 1, 2, 0):
        rows = pl.ds(slot * two, two)

        def down(i, rows=rows, slot=slot):
            cols = tile(i, 512)
            sums.put(slot, cols, dot(act[rows, :], wd[:, cols]))

        loop(d // 512, down)
        sums.share(slot)
        if slot == 1:
            sums.send_diag()
    sums.send_free()
    sums.send_joined()
    load_vec.wait()
    load_fin.wait()
    load_cot.wait()
    cot_far.wait_recv()
    sums.wait()

    def strip_sum(row, value):
        gv[row : row + 1, :] = gv[row : row + 1, :] + jnp.sum(value, axis=0, keepdims=True)

    def second_norm(i):
        rows = tile(i, STRIP)
        xhat, _ = normed(fin[rows, :])
        value = xhat * vec[3:4, :] + vec[4:5, :] + sums.total(i) + vec[5:6, :]
        xhat, scale = normed(value)
        out[rows, :] = (xhat * vec[6:7, :] + vec[7:8, :]).astype(BF16)
        grad = cot[rows, :].astype(F32)
        strip_sum(6, grad * xhat)
        strip_sum(7, grad)
        grad = normed_back(grad * vec[6:7, :], xhat, scale)
        g2s[rows, :] = grad
        low = grad.astype(BF16)
        g2[rows, :] = low
        strip_sum(5, low.astype(F32))

    loop(t // STRIP, second_norm)
    gather = Gather(net, at, sz, g2, 0, t)
    gather.send()
    net.keep(out.at[own_rows, :], outputs.at[at.zh])
    sums.settle()

    def back(slot):
        gather.ready(slot)
        rows = pl.ds(slot * two, two)

        def down(i):
            cols = tile(i, 512)
            value = dot_nt(g2[rows, :], wd[cols, :])
            gh[rows, cols] = (value * gate_slope(hid[rows, cols])).astype(BF16)

        loop(sz.hid // 512, down)

        def up(i):
            cols = tile(i, 512)
            sums.put(slot, cols, dot_nt(gh[rows, :], wu[cols, :]))

        loop(d // 512, up)
        sums.share(slot)

    back(0)
    gather.relay()
    back(1)
    back(2)
    sums.send_free()
    gather.relay_last()
    out_far = net.remote(out.at[pl.ds((1 - at.zh) * h, h), :], outputs.at[at.zh], at.to_h)
    back(3)
    sums.send_diag()

    def down_grad(i):
        rows, cols = tile(i // (d // 512), 512), tile(i % (d // 512), 512)
        dwd[rows, cols] = dot_tn(act[:, rows], g2[:, cols]).astype(BF16)

    loop((sz.hid // 512) * (d // 512), down_grad)
    net.keep(dwd, grad_w_down)
    down_rows = sz.hid_shard // 4
    sum_d = Reduce(
        net, at, lambda p, j: dwd.at[pl.ds(p * sz.hid_shard + j * down_rows, down_rows), :], bufs, 4, True, None
    )
    sum_d.start(0)
    sums.send_joined()
    sum_d.hop(0)

    def up_grad(i):
        rows, cols = tile(i // (sz.hid // 512), 512), tile(i % (sz.hid // 512), 512)
        dwu[rows, cols] = dot_tn(fa[:, rows], gh[:, cols]).astype(BF16)

    loop((sz.hid // 512) * (d // 512), up_grad)
    net.keep(dwu, grad_w_up)
    sum_d.hop(1)
    for p in range(sz.parts):
        rf = sz.hid_shard
        gv[8:9, p * sz.slab : p * sz.slab + rf] = jnp.sum(
            gh[:, p * rf : (p + 1) * rf].astype(F32), axis=0, keepdims=True
        )
    sums.wait()

    def first_norm(i):
        rows = tile(i, STRIP)
        xhat, scale = normed(fin[rows, :])
        grad = g2s[rows, :] + sums.total(i)
        strip_sum(3, grad * xhat)
        strip_sum(4, grad)
        grad = normed_back(grad * vec[3:4, :], xhat, scale)
        g2s[rows, :] = grad
        low = grad.astype(BF16)
        out_low[rows, :] = low
        strip_sum(2, low.astype(F32))

    out_low = cot
    loop(t // STRIP, first_norm)
    net.keep(g2s, grad_first_in)
    net.keep(out_low, grad_low)
    net.keep(gv, grad_vec)
    for j in (2, 3):
        sum_d.add(j)
    late = pl.ds(2 * down_rows, 2 * down_rows)
    early = pl.ds(0, 2 * down_rows)
    net.keep(sum_d.out.at[late, :], down_sum)
    for j in (0, 1):
        sum_d.from_h[j].wait_recv()
    net.keep(sum_d.inn.at[early, :], down_in)
    out_far.wait_recv()
    net.finish()


def feed_forward(sz, *args):
    t, d, r = sz.tokens, sz.width, sz.rows_all
    shape = jax.ShapeDtypeStruct
    anywhere = pl.BlockSpec(memory_space=pl.ANY)
    outs = (
        shape((2, sz.half, d), BF16),
        shape((t, d), F32),
        shape((t, d), BF16),
        shape((d, sz.hid), BF16),
        shape((sz.hid, d), BF16),
        shape((16, d), F32),
        shape((sz.hid_shard // 2, d), BF16),
        shape((sz.hid_shard // 2, d), BF16),
    )
    scratch = [
        pltpu.VMEM((r, d), BF16),
        pltpu.VMEM((d, sz.hid), BF16),
        pltpu.VMEM((sz.hid, d), BF16),
        pltpu.VMEM((8, d), F32),
        pltpu.VMEM((8, sz.hid), F32),
        pltpu.VMEM((t, d), F32),
        pltpu.VMEM((t, d), BF16),
        pltpu.VMEM((r, sz.hid), F32),
        pltpu.VMEM((r, sz.hid), BF16),
        pltpu.VMEM((r, sz.hid), BF16),
        pltpu.VMEM((r, d), BF16),
        pltpu.VMEM((t, d), F32),
        pltpu.VMEM((t, d), BF16),
        pltpu.VMEM((16, d), F32),
        pltpu.VMEM((d, sz.hid), BF16),
        pltpu.VMEM((sz.hid, d), BF16),
        *Scatter.scratch(sz),
        *Reduce.scratch(sz, sz.hid_shard, d, BF16, True, 1),
        pltpu.SemaphoreType.DMA((64 + 10 * sz.nx,)),
        pltpu.SemaphoreType.DMA((64 + 10 * sz.nx,)),
        pltpu.SemaphoreType.DMA((24 + 12 * sz.nx,)),
    ]
    return pl.pallas_call(
        functools.partial(feed_forward_kernel, sz),
        out_shape=outs,
        in_specs=[anywhere] * 8,
        out_specs=[anywhere] * len(outs),
        scratch_shapes=scratch,
        compiler_params=pltpu.CompilerParams(
            collective_id=1, has_side_effects=True, vmem_limit_bytes=VMEM_LIMIT
        ),
        name="feed_forward",
    )(*args)


class Reduce:
    def __init__(self, net, at, view, bufs, chunks, held, result):
        self.net, self.at, self.view, self.chunks = net, at, view, chunks
        self.got, self.own, self.out, self.inn = bufs
        self.rows = self.out.shape[0] // chunks
        self.result = result
        self.held = held
        self.groups = (at.x * 2 + (1 - at.zh), at.x * 2 + at.zh)
        self.from_x, self.from_h, self.loads = {}, {}, {}

    @staticmethod
    def scratch(sz, rows, cols, dtype, held, kinds=2):
        return [
            pltpu.VMEM((sz.nx - 1, kinds, rows, cols), dtype),
            pltpu.VMEM((2, 8, 128) if held else (2, rows, cols), dtype),
            pltpu.VMEM((rows, cols), dtype),
            pltpu.VMEM((rows, cols), dtype),
        ]

    def chunk(self, j):
        return pl.ds(j * self.rows, self.rows)

    def start(self, which):
        at, net = self.at, self.net
        zh = 1 - at.zh if which == 0 else at.zh
        for j in range(self.chunks):
            for step in range(1, at.nx):
                p = at.x_of(step) * 2 + zh
                self.from_x[which, j, step] = net.remote(
                    self.view(p, j), self.got.at[step - 1, which, self.chunk(j), :], at.to_x(step)
                )
            if not self.held:
                self.loads[which, j] = net.local(
                    self.view(self.groups[which], j), self.own.at[which, self.chunk(j), :]
                )

    def term(self, which, j, i):
        rows = pl.ds(pl.multiple_of(j * self.rows + i * STRIP, STRIP), STRIP)
        if self.held:
            total = self.view(self.groups[which], j)[tile(i, STRIP), :].astype(F32)
        else:
            total = self.own[which, rows, :].astype(F32)
        for step in range(1, self.at.nx):
            total = total + self.got[step - 1, which, rows, :].astype(F32)
        return rows, total

    def ready(self, which, j):
        for step in range(1, self.at.nx):
            self.from_x[which, j, step].wait_recv()
        if not self.held:
            self.loads[which, j].wait()

    def add(self, j):
        self.ready(0, j)

        def body(i):
            rows, total = self.term(0, j, i)
            self.out[rows, :] = total.astype(self.out.dtype)

        loop(self.rows // STRIP, body)

    def hop(self, j):
        self.add(j)
        self.send(j)

    def send(self, j):
        self.from_h[j] = self.net.remote(
            self.out.at[self.chunk(j), :], self.inn.at[self.chunk(j), :], self.at.to_h
        )

    def close(self, j):
        self.ready(1, j)
        if j in self.from_h:
            self.from_h[j].wait_recv()

        def body(i):
            rows, total = self.term(1, j, i)
            self.result[rows, :] = (total + self.inn[rows, :].astype(F32)).astype(self.result.dtype)

        loop(self.rows // STRIP, body)


def attention_backward_kernel(
    sz,
    grad_low, grad_first_in, x_all, wqkv, w_out_own, qkv_all, ctx_all, grad_w_up, grad_w_down, grad_vec, down_sum, down_in,
    input_grad, out_wq, out_wk, out_wv, out_wo, out_wup, out_wdown, out_vec, out_bup,
    gb, xs, wq, wo, qkv, ctx, gfi, gv, dctx, dqkv, dk, dv, ig, dwq, dwo, dwo_own, res_q, res_o, res_u, res_d, res_v,
    vec_got, vec_sum, bup_out, *rest,
):
    *bufs, send, recv, local = rest
    sum_bufs, bufs = bufs[:7], bufs[7:]
    at = Place(sz)
    net = Copies(send, recv, local)
    t, d, h = sz.tokens, sz.width, sz.half
    two = 2 * t
    rw, rf = sz.row_shard, sz.hid_shard
    flips = range(1, TP)
    load_gb = net.local(grad_low, gb.at[pl.ds(0, t), :])
    load_wo = net.local(w_out_own, wo)
    load_qkv = net.local(qkv_all, qkv)
    load_ctx = net.local(ctx_all, ctx)
    load_gv = net.local(grad_vec, gv)
    greet([at.peer(f) for f in flips] + [at.to_h] + [at.to_x(s) for s in range(1, sz.nx)])
    load_gb.wait()
    gather = Gather(net, at, sz, gb, 0, t, tall=True)
    gather.send()

    up_rows, down_rows = sz.slab // 4, rf // 4
    sum_u = Reduce(
        net, at, lambda p, j: grad_w_up.at[pl.ds(p * sz.slab + j * up_rows, up_rows), :],
        bufs[0:4], 4, False, res_u,
    )
    sum_d = Reduce(
        net, at, lambda p, j: grad_w_down.at[pl.ds(p * rf + j * down_rows, down_rows), :],
        bufs[4:8], 4, False, res_d,
    )
    sum_q = Reduce(
        net, at, lambda p, j: dwq.at[pl.ds(p * sz.slab + j * up_rows, up_rows), :], bufs[8:12], 4, True, res_q
    )
    sum_o = Reduce(net, at, lambda p, j: dwo_own.at[p], bufs[12:16], 1, True, res_o)
    sum_v = Reduce(
        net, at, lambda p, j: gv.at[:, pl.ds(pl.multiple_of(p * sz.slab, sz.slab), sz.slab)],
        bufs[16:20], 1, True, res_v,
    )
    late = pl.ds(2 * down_rows, 2 * down_rows)
    load_sum = net.local(down_sum, sum_d.out.at[late, :])
    load_in = net.local(down_in, sum_d.inn.at[pl.ds(0, 2 * down_rows), :])
    sum_u.start(0)
    load_sum.wait()
    for j in (2, 3):
        sum_d.send(j)
    sum_u.start(1)
    load_x = net.local(x_all, xs)
    load_wq = net.local(wqkv, wq)
    load_gfi = net.local(grad_first_in, gfi)
    hops = [(sum_u, j) for j in range(4)]

    def pump(count):
        for _ in range(min(count, len(hops))):
            item, j = hops.pop(0)
            item.hop(j)

    load_wo.wait()

    def context_grad(slot):
        gather.ready(slot)
        rows = pl.ds(slot * two, two)
        dctx[rows, :] = dot_nt(gb[rows, :], wo[...]).astype(BF16)

    context_grad(0)
    gather.relay()
    pump(1)
    context_grad(1)
    context_grad(2)
    gather.relay_last()
    pump(1)
    context_grad(3)
    pump(1)
    load_qkv.wait()

    def attend_back(k):
        q_cols = slice(k * HD, (k + 1) * HD)
        k_cols = slice(sz.cols + k * HD, sz.cols + (k + 1) * HD)
        v_cols = slice(2 * sz.cols + k * HD, 2 * sz.cols + (k + 1) * HD)
        turned = qkv[:, k_cols].T

        def body(i):
            rows = tile(i, 256)
            queries, grads = qkv[rows, q_cols], dctx[rows, q_cols]
            scores = dot_nt(qkv[:, k_cols], queries) * SCALE
            exps = jnp.exp(scores - jnp.max(scores, axis=0, keepdims=True))
            probs = exps * (1.0 / jnp.sum(exps, axis=0, keepdims=True))
            value_part = dot(probs.astype(BF16), grads)
            slopes = probs * dot_nt(qkv[:, v_cols], grads)
            score_grads = (slopes - probs * jnp.sum(slopes, axis=0, keepdims=True)).astype(BF16)
            key_part = dot(score_grads, queries)
            first = i == 0
            dv[...] = jnp.where(first, value_part, dv[...] + value_part)
            dk[...] = jnp.where(first, key_part, dk[...] + key_part)
            dqkv[rows, q_cols] = (dot(turned, score_grads).T * SCALE).astype(BF16)

        loop(sz.rows_all // 256, body)
        dqkv[:, k_cols] = (dk[...] * SCALE).astype(BF16)
        dqkv[:, v_cols] = dv[...].astype(BF16)

    attend_back(0)
    pump(2)
    for k in range(1, sz.heads):
        attend_back(k)
    pump(2)
    load_wq.wait()

    sums = Scatter(net, at, sz, sum_bufs, tall=True)
    for slot in (3, 1, 2, 0):
        rows = pl.ds(slot * two, two)

        def body(i, rows=rows, slot=slot):
            cols = tile(i, 512)
            sums.put(slot, cols, dot_nt(dqkv[rows, :], wq[cols, :]))

        loop(d // 512, body)
        sums.share(slot)
        if slot == 1:
            sums.send_diag()
    sums.send_free()
    pump(1)
    load_x.wait()
    load_ctx.wait()

    def qkv_grad(i):
        rows = tile(i, 512)
        dwq[rows, :] = dot_tn(xs[:, rows], dqkv[...]).astype(BF16)

    loop(d // 512, qkv_grad)
    sum_q.start(0)
    sum_d.start(1)
    sums.send_joined()

    def out_grad(i):
        cols = tile(i, 512)
        dwo[:, cols] = dot_tn(ctx[...], gb[:, cols]).astype(BF16)

    loop(d // 512, out_grad)
    group = at.t // sz.pieces
    member = at.t - group * sz.pieces
    wo_in = []
    for k in range(sz.heads):
        for f in range(1, sz.pieces):
            other = at.index_of(f) - group * sz.pieces
            wo_in.append(
                net.remote(
                    dwo.at[pl.ds((k * sz.pieces + other) * rw, rw), :],
                    dwo_own.at[member * sz.heads + k],
                    at.peer(f),
                )
            )
        net.local(
            dwo.at[pl.ds((k * sz.pieces + member) * rw, rw), :], dwo_own.at[member * sz.heads + k]
        ).wait()
    load_gv.wait()
    for k in range(sz.heads):
        lanes = at.head_lanes(sz, at.t, k)
        gv[0:1, lanes] = jnp.sum(dqkv[:, k * HD : (k + 1) * HD].astype(F32), axis=0, keepdims=True)
        at_v = 2 * sz.cols + k * HD
        gv[1:2, lanes] = jnp.sum(dqkv[:, at_v : at_v + HD].astype(F32), axis=0, keepdims=True)
    for copy in wo_in:
        copy.wait_recv()
    sum_o.start(0)
    sum_v.start(0)
    sum_q.hop(0)
    sum_q.start(1)
    sum_o.start(1)
    sum_v.start(1)
    load_gfi.wait()
    sum_q.hop(1)
    sums.wait()

    def final(i):
        rows = tile(i, STRIP)
        ig[rows, :] = (gfi[rows, :] + sums.total(i)).astype(BF16)

    loop(t // STRIP, final)
    own_rows = pl.ds(at.zh * h, h)
    net.keep(ig.at[own_rows, :], input_grad.at[at.zh])
    for j in (2, 3):
        sum_q.hop(j)
    sum_o.hop(0)
    sum_v.hop(0)
    ig_far = net.remote(ig.at[pl.ds((1 - at.zh) * h, h), :], input_grad.at[at.zh], at.to_h)
    load_in.wait()

    for j in range(4):
        sum_u.close(j)

    def rows_of(buf, member):
        return buf.at[pl.ds(member * rw, rw), :]

    def up_parts(member):
        if not sz.by_lanes:
            return [(res_u.at[pl.ds(member * rw, rw), :], out_wup.at[at.t])]
        return [
            (
                res_u.at[pl.ds(member * rw, rw), pl.ds(p * rf, rf)],
                out_wup.at[:, pl.ds(pl.multiple_of((p * TP + at.t) * rf, rf), rf)],
            )
            for p in range(sz.parts)
        ]

    def qkv_parts(member):
        return [
            (
                res_q.at[pl.ds(member * rw, rw), pl.ds(which * sz.cols + k * HD, HD)],
                target.at[:, at.head_lanes(sz, at.t, k)],
            )
            for which, target in enumerate((out_wq, out_wk, out_wv))
            for k in range(sz.heads)
        ]

    net.kept.append(net.local_parts(up_parts(at.t), rows_of(res_u, at.t)))
    back_in = [
        net.remote_parts(up_parts(at.index_of(f)), rows_of(res_u, at.index_of(f)), at.peer(f)) for f in flips
    ]
    for j in range(4):
        sum_d.close(j)
    net.keep(res_d, out_wdown)
    for j in range(4):
        sum_q.close(j)
    net.kept.append(net.local_parts(qkv_parts(at.t), rows_of(res_q, at.t)))
    back_in += [
        net.remote_parts(qkv_parts(at.index_of(f)), rows_of(res_q, at.index_of(f)), at.peer(f)) for f in flips
    ]
    sum_o.close(0)
    net.keep(res_o, out_wo)
    sum_v.close(0)

    def lanes_of(index):
        return pl.ds(pl.multiple_of(index // sz.pieces * HD, HD), HD)

    vec_got[at.t] = res_v[0:8, lanes_of(at.t)]
    vec_in = [
        net.remote(res_v.at[pl.ds(0, 8), lanes_of(at.index_of(f))], vec_got.at[at.t], at.peer(f)) for f in flips
    ]
    bup_out[...] = res_v[8:16, 0:rf]
    net.keep(bup_out, out_bup)
    for copy in vec_in:
        copy.wait_recv()
    total = vec_got[0]
    for member in range(1, TP):
        total = total + vec_got[member]
    vec_sum[...] = total
    net.keep(vec_sum, out_vec)
    for copy in back_in:
        copy.wait_recv()
    ig_far.wait_recv()
    net.finish()


def attention_backward(sz, *args):
    t, d, r = sz.tokens, sz.width, sz.rows_all
    rw, rf = sz.row_shard, sz.hid_shard
    wide = 3 * sz.cols
    shape = jax.ShapeDtypeStruct
    anywhere = pl.BlockSpec(memory_space=pl.ANY)
    outs = (
        shape((2, sz.half, d), BF16),
        shape((rw, d), BF16),
        shape((rw, d), BF16),
        shape((rw, d), BF16),
        shape((rw, d), BF16),
        shape((rw, sz.hidden) if sz.by_lanes else (TP, rw, sz.hid), BF16),
        shape((rf, d), BF16),
        shape((8, HD), F32),
        shape((8, rf), F32),
    )
    scratch = [
        pltpu.VMEM((r, d), BF16),
        pltpu.VMEM((r, d), BF16),
        pltpu.VMEM((d, wide), BF16),
        pltpu.VMEM((sz.cols, d), BF16),
        pltpu.VMEM((r, wide), BF16),
        pltpu.VMEM((r, sz.cols), BF16),
        pltpu.VMEM((t, d), F32),
        pltpu.VMEM((16, d), F32),
        pltpu.VMEM((r, sz.cols), BF16),
        pltpu.VMEM((r, wide), BF16),
        pltpu.VMEM((r, HD), F32),
        pltpu.VMEM((r, HD), F32),
        pltpu.VMEM((t, d), BF16),
        pltpu.VMEM((d, wide), BF16),
        pltpu.VMEM((sz.cols, d), BF16),
        pltpu.VMEM((sz.parts, rw, d), BF16),
        pltpu.VMEM((sz.slab, wide), BF16),
        pltpu.VMEM((rw, d), BF16),
        pltpu.VMEM((sz.slab, sz.hid), BF16),
        pltpu.VMEM((rf, d), BF16),
        pltpu.VMEM((16, sz.slab), F32),
        pltpu.VMEM((TP, 8, HD), F32),
        pltpu.VMEM((8, HD), F32),
        pltpu.VMEM((8, rf), F32),
        *Scatter.scratch(sz),
        *Reduce.scratch(sz, sz.slab, sz.hid, BF16, False),
        *Reduce.scratch(sz, rf, d, BF16, False),
        *Reduce.scratch(sz, sz.slab, wide, BF16, True),
        *Reduce.scratch(sz, rw, d, BF16, True),
        *Reduce.scratch(sz, 16, sz.slab, F32, True),
        pltpu.SemaphoreType.DMA((70 + 28 * sz.nx,)),
        pltpu.SemaphoreType.DMA((70 + 28 * sz.nx,)),
        pltpu.SemaphoreType.DMA((48,)),
    ]
    return pl.pallas_call(
        functools.partial(attention_backward_kernel, sz),
        out_shape=outs,
        in_specs=[anywhere] * 12,
        out_specs=[anywhere] * len(outs),
        scratch_shapes=scratch,
        compiler_params=pltpu.CompilerParams(
            collective_id=2, has_side_effects=True, vmem_limit_bytes=VMEM_LIMIT
        ),
        name="attention_backward",
    )(*args)


def widen_kernel(count, *refs):
    for src, dst in zip(refs[:count], refs[count:]):
        flat = len(src.shape) == 2

        def body(i, src=src, dst=dst, flat=flat):
            if flat:
                dst[tile(i, STRIP), :] = src[tile(i, STRIP), :].astype(F32)
            else:
                for j in range(src.shape[0]):
                    dst[j, tile(i, STRIP), :] = src[j, tile(i, STRIP), :].astype(F32)

        loop(src.shape[-2] // STRIP, body)


def widen(*arrays):
    whole = pl.BlockSpec(memory_space=pltpu.VMEM)
    return pl.pallas_call(
        functools.partial(widen_kernel, len(arrays)),
        out_shape=[jax.ShapeDtypeStruct(a.shape, F32) for a in arrays],
        in_specs=[whole] * len(arrays),
        out_specs=[whole] * len(arrays),
        compiler_params=pltpu.CompilerParams(vmem_limit_bytes=VMEM_LIMIT),
        name="widen",
    )(*arrays)


def per_device(
    sz, inputs, cotangent, w_query, w_key, w_value, w_out, b_query, b_value, b_out, ln1_gain, ln1_bias,
    w_up, b_up, w_down, b_down, ln2_gain, ln2_bias,
):
    rw, rf = sz.row_shard, sz.hid_shard
    t = lax.axis_index("zl") * 4 + lax.axis_index("y") * 2 + lax.axis_index("c")
    p = lax.axis_index("x") * 2 + lax.axis_index("zh")
    piece = t % sz.pieces
    rows = jnp.stack([b_query, b_value, b_out, ln1_gain, ln1_bias, b_down, ln2_gain, ln2_bias]).astype(F32)
    here = lax.broadcasted_iota(jnp.int32, (8, HD), 1) // rw == piece
    low = jnp.where(here, jnp.tile(rows, (1, sz.pieces)), 0.0)
    up = b_up.astype(F32)
    if rf >= HD:
        high = jnp.pad(up.reshape(rf // HD, HD), ((0, 8 - rf // HD), (0, 0)))
    else:
        each = HD // rf
        here = lax.broadcasted_iota(jnp.int32, (8, HD), 1) // rf == p % each
        high = jnp.where(here, jnp.tile(up[None], (8, each)), 0.0)
    vec_pack = jnp.concatenate([low, high], axis=0)

    up_rows = w_up
    if not sz.by_lanes:
        up_rows = w_up.reshape(rw, sz.parts, TP, rf).transpose(2, 0, 1, 3).reshape(TP, rw, sz.hid)

    x_all, wqkv, w_out_own, up_own, down_own, vec_all, bup_all, qkv, ctx, first_in, first_low = attention_forward(
        sz, inputs, w_query, w_key, w_value, w_out, up_rows, w_down, vec_pack
    )
    outputs, grad_first_in, grad_low, grad_up, grad_down, grad_vec, down_sum, down_in = feed_forward(
        sz, first_low, first_in, up_own, down_own, vec_all, bup_all, cotangent, w_down
    )
    *grads, out_vec, out_bup = attention_backward(
        sz, grad_low, grad_first_in, x_all, wqkv, w_out_own, qkv, ctx, grad_up, grad_down, grad_vec,
        down_sum, down_in,
    )
    input_grad, grad_wq, grad_wk, grad_wv, grad_wo, grad_wup, grad_wdown = widen(*grads)
    if not sz.by_lanes:
        grad_wup = grad_wup.reshape(TP, rw, sz.parts, rf).transpose(1, 2, 0, 3).reshape(rw, sz.hidden)
    vec = lax.dynamic_slice(out_vec, (0, piece * rw), (8, rw))
    return (
        outputs,
        input_grad,
        grad_wq,
        grad_wk,
        grad_wv,
        grad_wo,
        vec[0],
        vec[1],
        vec[2],
        vec[3],
        vec[4],
        grad_wup,
        out_bup[0],
        grad_wdown,
        vec[5],
        vec[6],
        vec[7],
    )


def solution(mesh):
    nx = mesh.shape["dp"]
    plane = Mesh(mesh.devices.reshape(nx, 2, mesh.shape["hd"] // 2, 2, mesh.shape["sq"] // 2), AXES)
    rows, matrix, vector = P("x", AXES[1:], None), P(AXES, None), P(AXES)

    def run(*args):
        batch, length, width = args[0].shape
        sz = Sizes(nx, width, args[11].shape[1], batch // nx * length // (2 * TP))
        call = jax.shard_map(
            functools.partial(per_device, sz),
            mesh=plane,
            in_specs=(rows, rows) + (matrix,) * 4 + (vector,) * 5 + (matrix, vector, matrix) + (vector,) * 3,
            out_specs=(rows, rows) + (matrix,) * 4 + (vector,) * 5 + (matrix, vector, matrix) + (vector,) * 3,
            check_vma=False,
        )
        return call(*args)

    return run
```

```python
import functools

import jax
import jax.numpy as jnp
from jax import lax
from jax.experimental import pallas as pl
from jax.experimental.pallas import tpu as pltpu
from jax.sharding import Mesh
from jax.sharding import PartitionSpec as P

F32 = jnp.float32
BF16 = jnp.bfloat16
HD = 128
EPSILON = 1e-12
TP = 8
STRIP = 16
VMEM_LIMIT = 60 * 2**20
AXES = ("x", "zh", "zl", "y", "c")
SCALE = HD ** (-0.5)


class Sizes:
    def __init__(self, groups_x, width, hidden, tokens):
        self.nx = groups_x
        self.parts = 2 * groups_x
        self.width = width
        self.hidden = hidden
        self.tokens = tokens
        self.half = tokens // 2
        self.rows_all = TP * tokens
        self.row_shard = width // (TP * self.parts)
        self.hid_shard = hidden // (TP * self.parts)
        self.pieces = HD // self.row_shard
        self.heads = width // HD // TP
        self.cols = self.heads * HD
        self.hid = hidden // TP
        self.slab = width // self.parts
        self.by_lanes = self.hid_shard % HD == 0


class Place:
    def __init__(self, sizes):
        self.x, self.zh, self.zl, self.y, self.c = (lax.axis_index(a) for a in AXES)
        self.nx = sizes.nx
        self.t = self.zl * 4 + self.y * 2 + self.c
        self.p = self.x * 2 + self.zh
        self.pz = self.x * 2 + (1 - self.zh)
        self.to_c = {"c": 1 - self.c}
        self.to_y = {"y": 1 - self.y}
        self.to_z = {"zl": 1 - self.zl}
        self.to_h = {"zh": 1 - self.zh}

    def peer(self, flip):
        target = {}
        if flip & 4:
            target["zl"] = 1 - self.zl
        if flip & 2:
            target["y"] = 1 - self.y
        if flip & 1:
            target["c"] = 1 - self.c
        return target

    def index_of(self, flip):
        zl = 1 - self.zl if flip & 4 else self.zl
        y = 1 - self.y if flip & 2 else self.y
        c = 1 - self.c if flip & 1 else self.c
        return zl * 4 + y * 2 + c

    def head_lanes(self, sz, member, k):
        group = member // sz.pieces
        head = ((member - group * sz.pieces) * sz.heads + k) * (TP // sz.pieces) + group
        return pl.ds(pl.multiple_of(head * HD, HD), HD)

    def to_x(self, step):
        return {"x": lax.rem(self.x + step, self.nx)}

    def x_of(self, step):
        return lax.rem(self.x + step, self.nx)


class Copies:
    def __init__(self, send, recv, local):
        self.send, self.recv, self.local_sems = send, recv, local
        self.n_remote = 0
        self.n_local = 0
        self.sent = []
        self.kept = []

    def remote(self, src, dst, target):
        i = self.n_remote
        self.n_remote += 1
        copy = pltpu.make_async_remote_copy(
            src_ref=src,
            dst_ref=dst,
            send_sem=self.send.at[i],
            recv_sem=self.recv.at[i],
            device_id=target,
            device_id_type=pl.DeviceIdType.MESH,
        )
        copy.start()
        self.sent.append(copy)
        return copy

    def remote_parts(self, pairs, whole, target):
        i = self.n_remote
        self.n_remote += 1

        def copy(src, dst):
            return pltpu.make_async_remote_copy(
                src_ref=src,
                dst_ref=dst,
                send_sem=self.send.at[i],
                recv_sem=self.recv.at[i],
                device_id=target,
                device_id_type=pl.DeviceIdType.MESH,
            )

        for src, dst in pairs:
            copy(src, dst).start()
        total = copy(whole, whole)
        self.sent.append(total)
        return total

    def local_parts(self, pairs, whole):
        i = self.n_local
        self.n_local += 1
        for src, dst in pairs:
            pltpu.make_async_copy(src, dst, self.local_sems.at[i]).start()
        return pltpu.make_async_copy(whole, whole, self.local_sems.at[i])

    def local(self, src, dst):
        i = self.n_local
        self.n_local += 1
        copy = pltpu.make_async_copy(src, dst, self.local_sems.at[i])
        copy.start()
        return copy

    def keep(self, src, dst):
        self.kept.append(self.local(src, dst))

    def left(self, copy):
        copy.wait_send()
        self.sent = [other for other in self.sent if other is not copy]

    def finish(self):
        for copy in self.kept:
            copy.wait()
        for copy in self.sent:
            copy.wait_send()


def greet(targets):
    barrier = pltpu.get_barrier_semaphore()
    for target in targets:
        pl.semaphore_signal(
            barrier, inc=1, device_id=target, device_id_type=pl.DeviceIdType.MESH
        )
    pl.semaphore_wait(barrier, len(targets))


def dot(left, right):
    return jnp.dot(left, right, preferred_element_type=F32)


def dot_nt(left, right):
    return lax.dot_general(left, right, (((1,), (1,)), ((), ())), preferred_element_type=F32)


def dot_tn(left, right):
    return lax.dot_general(left, right, (((0,), (0,)), ((), ())), preferred_element_type=F32)


def tile(i, size):
    return pl.ds(pl.multiple_of(i * size, size), size)


def loop(count, body):
    def step(i, carry):
        body(i)
        return carry

    lax.fori_loop(0, count, step, 0)


def normed(values):
    average = jnp.mean(values, axis=1, keepdims=True)
    centred = values - average
    variance = jnp.mean(centred * centred, axis=1, keepdims=True)
    scale = lax.rsqrt(variance + EPSILON)
    return centred * scale, scale


def normed_back(grad, xhat, scale):
    along = jnp.mean(grad * xhat, axis=1, keepdims=True)
    return scale * (grad - jnp.mean(grad, axis=1, keepdims=True) - xhat * along)


class Gather:
    def __init__(self, net, at, sz, buf, start, count, tall=False):
        self.net, self.at, self.sz, self.buf = net, at, sz, buf
        self.start, self.count, self.tall = start, count, tall
        half = sz.width // 2
        self.cols = (pl.ds(0, half), pl.ds(half, half))
        self.sib = [None] * 4

    def part(self, slot, core, cols=None):
        rows = pl.ds((slot * 2 + core) * self.sz.tokens + self.start, self.count)
        return self.buf.at[rows, :] if cols is None else self.buf.at[rows, cols]

    def send(self):
        net, at = self.net, self.at
        self.from_y = [None, None]
        self.from_z = [None, None]
        for h in (0, 1):
            self.from_y[h] = net.remote(
                self.part(0, 0, self.cols[h]), self.part(1, 0, self.cols[h]), at.to_y
            )
            self.from_z[1 - h] = net.remote(
                self.part(0, 0, self.cols[1 - h]), self.part(2, 0, self.cols[1 - h]), at.to_z
            )
        self.share(0)

    def share(self, slot):
        self.sib[slot] = self.net.remote(self.part(slot, 0), self.part(slot, 1), self.at.to_c)

    def relay(self):
        net, at = self.net, self.at
        if self.tall:
            to_y = []
            for h in (1, 0):
                self.from_z[h].wait_recv()
                to_y.append(
                    net.remote(
                        self.part(2, 0, self.cols[h]), self.part(3, 0, self.cols[h]), at.to_y
                    )
                )
            self.diag = tuple(to_y)
            self.share(2)
            for copy in self.from_y:
                copy.wait_recv()
            self.share(1)
            return
        self.from_y[0].wait_recv()
        to_z = net.remote(
            self.part(1, 0, self.cols[0]), self.part(3, 0, self.cols[0]), at.to_z
        )
        self.from_z[1].wait_recv()
        to_y = net.remote(
            self.part(2, 0, self.cols[1]), self.part(3, 0, self.cols[1]), at.to_y
        )
        self.diag = (to_z, to_y)
        self.from_y[1].wait_recv()
        self.share(1)
        self.from_z[0].wait_recv()
        self.share(2)

    def relay_last(self):
        for copy in self.diag:
            copy.wait_recv()
        self.share(3)

    def ready(self, slot):
        self.sib[slot].wait_recv()


class Scatter:
    def __init__(self, net, at, sz, bufs, tall=False):
        self.net, self.at, self.sz, self.tall = net, at, sz, tall
        self.mine, self.theirs, self.got, self.diag, self.diag_got, self.out, self.inn = bufs
        self.sib = [None] * 4

    @staticmethod
    def scratch(sz):
        t, d = sz.tokens, sz.width
        return [
            pltpu.VMEM((4 * t, d), F32),
            pltpu.VMEM((4 * t, d), BF16),
            pltpu.VMEM((4 * t, d), BF16),
            pltpu.VMEM((t, d), BF16),
            pltpu.VMEM((t, d), BF16),
            pltpu.VMEM((2 * t, d), BF16),
            pltpu.VMEM((2 * t, d), BF16),
        ]

    def put(self, slot, cols, value):
        t = self.sz.tokens
        self.mine[pl.ds(slot * t, t), cols] = value[:t]
        self.theirs[pl.ds(slot * t, t), cols] = value[t:].astype(BF16)

    def share(self, slot):
        rows = pl.ds(slot * self.sz.tokens, self.sz.tokens)
        self.sib[slot] = self.net.remote(self.theirs.at[rows, :], self.got.at[rows, :], self.at.to_c)

    def add(self, slot, start, count, dst, dst_start, extra=None):
        base = slot * self.sz.tokens + start

        def body(i):
            rows = pl.ds(pl.multiple_of(base + i * STRIP, STRIP), STRIP)
            total = self.mine[rows, :] + self.got[rows, :].astype(F32)
            if extra is not None:
                there = pl.ds(pl.multiple_of(start + i * STRIP, STRIP), STRIP)
                total = total + extra[there, :].astype(F32)
            dst[pl.ds(pl.multiple_of(dst_start + i * STRIP, STRIP), STRIP), :] = total.astype(BF16)

        loop(count // STRIP, body)

    def send_diag(self):
        net, at, h = self.net, self.at, self.sz.half
        self.sib[3].wait_recv()
        self.add(3, 0, 2 * h, self.diag, 0)
        low, high = pl.ds(0, h), pl.ds(h, h)
        self.d_low = net.remote(self.diag.at[low, :], self.diag_got.at[low, :], at.to_y)
        self.d_high = net.remote(
            self.diag.at[high, :], self.diag_got.at[high, :], at.to_y if self.tall else at.to_z
        )

    def half_out(self, side, start, target):
        rows = pl.ds(side * self.sz.tokens + start, self.sz.half)
        return self.net.remote(self.out.at[rows, :], self.inn.at[rows, :], target)

    def send_free(self):
        at, t, h = self.at, self.sz.tokens, self.sz.half
        self.sib[1].wait_recv()
        self.add(1, 0, h, self.out, 0)
        self.y_low = self.half_out(0, 0, at.to_y)
        if self.tall:
            self.add(1, h, h, self.out, h)
            self.y_high = self.half_out(0, h, at.to_y)
            return
        self.sib[2].wait_recv()
        self.add(2, h, h, self.out, t + h)
        self.z_high = self.half_out(1, h, at.to_z)

    def send_joined(self):
        at, t, h = self.at, self.sz.tokens, self.sz.half
        if self.tall:
            self.sib[2].wait_recv()
            self.d_low.wait_recv()
            self.add(2, 0, h, self.out, t, self.diag_got)
            self.z_low = self.half_out(1, 0, at.to_z)
            self.d_high.wait_recv()
            self.add(2, h, h, self.out, t + h, self.diag_got)
            self.z_high = self.half_out(1, h, at.to_z)
            return
        self.d_high.wait_recv()
        self.add(1, h, h, self.out, h, self.diag_got)
        self.y_high = self.half_out(0, h, at.to_y)
        self.d_low.wait_recv()
        self.add(2, 0, h, self.out, t, self.diag_got)
        self.z_low = self.half_out(1, 0, at.to_z)

    def settle(self):
        for copy in [*self.sib, self.d_low, self.d_high, self.y_low, self.z_high, self.y_high, self.z_low]:
            self.net.left(copy)

    def wait(self):
        self.sib[0].wait_recv()
        for copy in (self.y_low, self.z_high, self.y_high, self.z_low):
            copy.wait_recv()

    def total(self, i):
        t = self.sz.tokens
        rows = tile(i, STRIP)
        far = pl.ds(pl.multiple_of(t + i * STRIP, STRIP), STRIP)
        return (
            self.mine[rows, :]
            + self.got[rows, :].astype(F32)
            + self.inn[rows, :].astype(F32)
            + self.inn[far, :].astype(F32)
        )


class Spread:
    def __init__(self, net, at, view, source=None):
        self.net, self.at, self.view = net, at, view
        self.source = view(at.p) if source is None else source
        self.relayed = []

    def across(self):
        self.from_h = self.net.remote(self.source, self.view(self.at.p), self.at.to_h)

    def along(self):
        self.from_x = [
            self.net.remote(self.source, self.view(self.at.p), self.at.to_x(step))
            for step in range(1, self.at.nx)
        ]

    def relay(self):
        self.from_h.wait_recv()
        there = self.view(self.at.pz)
        self.relayed = [
            self.net.remote(there, there, self.at.to_x(step)) for step in range(1, self.at.nx)
        ]

    def near(self):
        for copy in self.from_x:
            copy.wait_recv()

    def far(self):
        for copy in self.relayed:
            copy.wait_recv()


def attention_forward_kernel(
    sz,
    xin, w_query, w_key, w_value, wout, wup_rows, wdown, vec_pack,
    x_all, wqkv, w_out_own, w_up, w_down, vec_all, bup_all, qkv_all, ctx_all, first_in, first_low,
    xs, wq, wo_got, wo, vecs, vec, bup, acc, qkv, ctx, fin, first, wu_own, wd_own, *rest,
):
    *sum_bufs, send, recv, local = rest
    at = Place(sz)
    net = Copies(send, recv, local)
    t, d, h = sz.tokens, sz.width, sz.half
    rw, rf = sz.row_shard, sz.hid_shard
    flips = range(1, TP)
    greet(
        [at.peer(f) for f in flips] + [at.to_h] + [at.to_x(s) for s in range(1, sz.nx)]
    )

    own_rows = pl.ds(at.zh * h, h)
    from_h = net.remote(xin.at[1 - at.zh], xs.at[own_rows, :], at.to_h)
    own_x = net.local(xin.at[at.zh], xs.at[own_rows, :])

    def wq_rows(p, member, count=1):
        return pl.ds((p * TP + member) * rw, count * rw)

    def wq_parts(member):
        return [
            (
                source.at[:, at.head_lanes(sz, member, k)],
                wq.at[wq_rows(at.p, at.t), pl.ds(which * sz.cols + k * HD, HD)],
            )
            for which, source in enumerate((w_query, w_key, w_value))
            for k in range(sz.heads)
        ]

    def wu_parts(member, dst):
        if not sz.by_lanes:
            return [(wup_rows.at[member], dst)]
        return [
            (
                wup_rows.at[:, pl.ds(pl.multiple_of((p * TP + member) * rf, rf), rf)],
                dst.at[:, pl.ds(p * rf, rf)],
            )
            for p in range(sz.parts)
        ]

    wq_mine, wu_mine = wq.at[wq_rows(at.p, at.t), :], w_up.at[wq_rows(at.p, at.t), :]
    own_wq = net.local_parts(wq_parts(at.t), wq_mine)
    own_vec = net.local(vec_pack, vecs.at[at.p * TP + at.t])
    own_wo = net.local(wout, wo_got.at[at.p])
    wu_here = net.local_parts(wu_parts(at.t, wu_own), wu_own)
    wd_here = net.local(wdown.at[pl.ds(0, rf // 2), :], wd_own)
    wq_in = [None] + [
        net.remote_parts(wq_parts(at.index_of(f)), wq_mine, at.peer(f)) for f in flips
    ]
    vec_in = [net.remote(vec_pack, vecs.at[at.p * TP + at.t], at.peer(f)) for f in flips]
    own_x.wait()
    near_rows = Gather(net, at, sz, xs, at.zh * h, h, tall=True)
    near_rows.send()

    def chip_block(buf, f):
        member = at.index_of(f) - at.c
        return lambda p: buf.at[wq_rows(p, member, 2), :]

    wq_spread = [Spread(net, at, chip_block(wq, f)) for f in (0, 2, 4, 6)]
    for f, item in zip((0, 2, 4, 6), wq_spread):
        if f == 0:
            own_wq.wait()
        else:
            wq_in[f].wait_recv()
        wq_in[f + 1].wait_recv()
        item.across()
        item.along()
    own_vec.wait()
    for copy in vec_in:
        copy.wait_recv()
    vec_spread = Spread(net, at, lambda p: vecs.at[pl.ds(p * TP, TP)])
    wo_spread = Spread(net, at, lambda p: wo_got.at[p], wout)
    vec_spread.across()
    vec_spread.along()
    wo_spread.along()
    from_h.wait_recv()
    far_rows = Gather(net, at, sz, xs, (1 - at.zh) * h, h, tall=True)
    far_rows.send()
    near_rows.relay()
    far_rows.relay()
    wq_spread[0].relay()
    near_rows.relay_last()
    far_rows.relay_last()
    vec_spread.relay()
    wq_spread[1].relay()
    wo_spread.across()
    wu_here.wait()
    own_wu = net.local(wu_own, w_up.at[wq_rows(at.p, at.t), :])
    wd_here.wait()
    net.keep(wd_own, w_down.at[pl.ds(at.p * (rf // 2), rf // 2), :])
    wu_in = [None] + [
        net.remote_parts(wu_parts(at.index_of(f), wu_mine), wu_mine, at.peer(f)) for f in flips
    ]

    def accumulate(zh, first_part):
        def body(i):
            rows = tile(i, 256)
            total = jnp.zeros((256, 3 * sz.cols), F32) if first_part else acc[rows, :]
            for x in range(sz.nx):
                block = tile(x * 2 + zh, sz.slab)
                total = total + dot(xs[rows, block], wq[block, :])
            acc[rows, :] = total

        loop(sz.rows_all // 256, body)

    for slot in range(4):
        near_rows.ready(slot)
        far_rows.ready(slot)
    for item in wq_spread:
        item.near()
    net.keep(xs, x_all)
    accumulate(at.zh, True)
    for item in wq_spread[2:]:
        item.relay()
    wd_chunk = rf // 4
    wd_spread = [
        Spread(
            net,
            at,
            lambda p, j=j: w_down.at[pl.ds(p * 2 * wd_chunk + j * wd_chunk, wd_chunk), :],
            wdown.at[pl.ds(j * wd_chunk, wd_chunk), :],
        )
        for j in range(2)
    ]
    for item in wd_spread:
        item.across()
    vec_spread.near()
    vec_spread.far()
    for j in range(d // HD):
        piece = vecs[j * sz.pieces, 0:8]
        for k in range(1, sz.pieces):
            piece = piece + vecs[j * sz.pieces + k, 0:8]
        vec[:, j * HD : (j + 1) * HD] = piece
    if rf >= HD:
        for p in range(sz.parts):
            for j in range(rf // HD):
                lanes = pl.ds(p * rf + j * HD, HD)
                bup[0:1, lanes] = vecs[p * TP + at.t, 8 + j : 9 + j]
    else:
        for j in range(sz.hid // HD):
            each = HD // rf
            row = vecs[j * each * TP + at.t, 8:9]
            for k in range(1, each):
                row = row + vecs[(j * each + k) * TP + at.t, 8:9]
            bup[0:1, j * HD : (j + 1) * HD] = row
    net.keep(vec, vec_all)
    net.keep(bup, bup_all)
    for item in wq_spread:
        item.far()
    accumulate(1 - at.zh, False)
    wo_spread.relay()
    for item in wd_spread:
        item.along()

    group = at.t // sz.pieces
    member = at.t - group * sz.pieces
    for k in range(sz.heads):
        lanes = at.head_lanes(sz, at.t, k)

        def biased(i, k=k, lanes=lanes):
            rows = tile(i, 256)
            for which in range(3):
                cols = slice(which * sz.cols + k * HD, which * sz.cols + (k + 1) * HD)
                value = acc[rows, cols]
                if which != 1:
                    value = value + vec[which // 2 : which // 2 + 1, lanes]
                qkv[rows, cols] = value.astype(BF16)

        loop(sz.rows_all // 256, biased)
    net.keep(wq, wqkv)
    net.keep(qkv, qkv_all)

    def attend(k):
        q_cols = slice(k * HD, (k + 1) * HD)
        k_cols = slice(sz.cols + k * HD, sz.cols + (k + 1) * HD)
        v_cols = slice(2 * sz.cols + k * HD, 2 * sz.cols + (k + 1) * HD)

        def body(i):
            rows = tile(i, 256)
            scores = dot_nt(qkv[rows, q_cols], qkv[:, k_cols]) * SCALE
            top = jnp.max(scores, axis=1, keepdims=True)
            exps = jnp.exp(scores - top)
            probs = exps * (1.0 / jnp.sum(exps, axis=1, keepdims=True))
            ctx[rows, q_cols] = dot(probs.astype(BF16), qkv[:, v_cols]).astype(BF16)

        loop(sz.rows_all // 256, body)

    for k in range(sz.heads):
        attend(k)
    net.keep(ctx, ctx_all)

    own_wo.wait()
    wo_spread.near()
    wo_spread.far()

    def wo_rows(k, piece):
        return pl.ds((k * sz.pieces + piece) * rw, rw)

    for k in range(sz.heads):
        net.local(wo_got.at[member * sz.heads + k], wo.at[wo_rows(k, member), :]).wait()
    wo_in = []
    for f in range(1, sz.pieces):
        other = at.index_of(f) - group * sz.pieces
        for k in range(sz.heads):
            wo_in.append(
                net.remote(wo_got.at[other * sz.heads + k], wo.at[wo_rows(k, member), :], at.peer(f))
            )
    for copy in wo_in:
        copy.wait_recv()
    net.keep(wo, w_out_own)
    wu_spread = [Spread(net, at, chip_block(w_up, f)) for f in (0, 2, 4, 6)]
    own_wu.wait()
    for f, item in zip((0, 2, 4, 6), wu_spread):
        if f:
            wu_in[f].wait_recv()
        wu_in[f + 1].wait_recv()
        item.across()
    for item in wu_spread:
        item.along()

    sums = Scatter(net, at, sz, sum_bufs, tall=True)
    for slot in (3, 1, 2, 0):
        rows = pl.ds(slot * 2 * t, 2 * t)

        def body(i, rows=rows, slot=slot):
            cols = tile(i, 512)
            sums.put(slot, cols, dot(ctx[rows, :], wo[:, cols]))

        loop(d // 512, body)
        sums.share(slot)
        if slot == 3:
            sums.send_diag()
    sums.send_free()
    sums.send_joined()
    for item in wd_spread:
        item.relay()
    sums.wait()

    def norm(i):
        rows = tile(i, STRIP)
        value = xs[rows, :].astype(F32) + sums.total(i) + vec[2:3, :]
        fin[rows, :] = value
        xhat, _ = normed(value)
        first[rows, :] = (xhat * vec[3:4, :] + vec[4:5, :]).astype(BF16)

    loop(t // STRIP, norm)
    net.keep(fin, first_in)
    net.keep(first, first_low)
    for item in wu_spread[:3]:
        item.relay()
    wu_spread[3].from_h.wait_recv()
    for item in wu_spread + wd_spread:
        item.near()
        item.far()
    net.finish()


def attention_forward(sz, *args):
    t, d, r = sz.tokens, sz.width, sz.rows_all
    shape = jax.ShapeDtypeStruct
    anywhere = pl.BlockSpec(memory_space=pl.ANY)
    outs = (
        shape((r, d), BF16),
        shape((d, 3 * sz.cols), BF16),
        shape((sz.cols, d), BF16),
        shape((d, sz.hid), BF16),
        shape((sz.hid // 2, d), BF16),
        shape((8, d), F32),
        shape((8, sz.hid), F32),
        shape((r, 3 * sz.cols), BF16),
        shape((r, sz.cols), BF16),
        shape((t, d), F32),
        shape((t, d), BF16),
    )
    scratch = [
        pltpu.VMEM((r, d), BF16),
        pltpu.VMEM((d, 3 * sz.cols), BF16),
        pltpu.VMEM((sz.parts, sz.row_shard, d), BF16),
        pltpu.VMEM((sz.cols, d), BF16),
        pltpu.VMEM((sz.parts * TP, 16, HD), F32),
        pltpu.VMEM((8, d), F32),
        pltpu.VMEM((8, sz.hid), F32),
        pltpu.VMEM((r, 3 * sz.cols), F32),
        pltpu.VMEM((r, 3 * sz.cols), BF16),
        pltpu.VMEM((r, sz.cols), BF16),
        pltpu.VMEM((t, d), F32),
        pltpu.VMEM((t, d), BF16),
        pltpu.VMEM((sz.row_shard, sz.hid), BF16),
        pltpu.VMEM((sz.hid_shard // 2, d), BF16),
        *Scatter.scratch(sz),
        pltpu.SemaphoreType.DMA((80 + 28 * sz.nx,)),
        pltpu.SemaphoreType.DMA((80 + 28 * sz.nx,)),
        pltpu.SemaphoreType.DMA((24,)),
    ]
    return pl.pallas_call(
        functools.partial(attention_forward_kernel, sz),
        out_shape=outs,
        in_specs=[anywhere] * 8,
        out_specs=[anywhere] * len(outs),
        scratch_shapes=scratch,
        compiler_params=pltpu.CompilerParams(
            collective_id=0, has_side_effects=True, vmem_limit_bytes=VMEM_LIMIT
        ),
        name="attention_forward",
    )(*args)


GELU_A = 0.7978845608028654
GELU_B = 0.044715


def gate(values):
    inner = jnp.tanh(GELU_A * (values + GELU_B * values * values * values))
    return 0.5 * values * (1.0 + inner)


def gate_slope(values):
    square = values * values
    inner = jnp.tanh(GELU_A * (values + GELU_B * square * values))
    rise = GELU_A * (1.0 + 3.0 * GELU_B * square)
    return 0.5 * (1.0 + inner) + 0.5 * values * (1.0 - inner * inner) * rise


def feed_forward_kernel(
    sz,
    first_low, first_in, w_up, w_down_half, vec_all, bup_all, cot_in, wdown,
    outputs, grad_first_in, grad_low, grad_w_up, grad_w_down, grad_vec, down_sum, down_in,
    fa, wu, wd, vec, bup, fin, cot, hid, act, gh, g2, g2s, out, gv, dwu, dwd, *rest,
):
    *bufs, send, recv, local = rest
    sum_bufs, bufs = bufs[:7], bufs[7:]
    at = Place(sz)
    net = Copies(send, recv, local)
    t, d, h = sz.tokens, sz.width, sz.half
    two = 2 * t
    rf = sz.hid_shard
    load_first = net.local(first_low, fa.at[pl.ds(0, t), :])

    def up_rows(p, f):
        start = (p * TP + at.index_of(f) - at.c) * sz.row_shard
        return pl.ds(pl.multiple_of(start, 2 * sz.row_shard), 2 * sz.row_shard)

    load_up = []
    for step in range(sz.nx):
        for zh in (at.zh, 1 - at.zh):
            for f in (0, 2, 4, 6):
                if step == 0 or zh is at.zh or f != 6:
                    rows = up_rows(at.x_of(step) * 2 + zh, f)
                    load_up.append(net.local(w_up.at[rows, :], wu.at[rows, :]))
    load_bup = net.local(bup_all, bup)
    load_down = [
        net.local(w_down_half.at[pl.ds(p * (rf // 2), rf // 2), :], wd.at[pl.ds(p * rf, rf // 2), :])
        for p in range(sz.parts)
    ]
    late_own = pl.ds(at.p * rf + rf // 2, rf // 2)
    load_down.append(net.local(wdown.at[pl.ds(rf // 2, rf // 2), :], wd.at[late_own, :]))
    load_vec = net.local(vec_all, vec)
    load_fin = net.local(first_in, fin)
    own_rows = pl.ds(at.zh * h, h)
    load_cot = net.local(cot_in.at[at.zh], cot.at[own_rows, :])
    greet([at.to_c, at.to_y, at.to_z, at.to_h] + [at.to_x(s) for s in range(1, sz.nx)])
    load_first.wait()
    firsts = Gather(net, at, sz, fa, 0, t, tall=True)
    firsts.send()
    wd_chunk = rf // 4
    wd_spread = [
        Spread(
            net,
            at,
            lambda p, j=j: wd.at[pl.ds(p * rf + j * wd_chunk, wd_chunk), :],
            wdown.at[pl.ds(j * wd_chunk, wd_chunk), :],
        )
        for j in (2, 3)
    ]
    last_up = [
        net.remote(w_up.at[up_rows(at.pz, 6), :], wu.at[up_rows(at.pz, 6), :], at.to_x(step))
        for step in range(1, sz.nx)
    ]
    for item in wd_spread:
        item.across()
        item.along()
    gv[...] = jnp.zeros_like(gv)

    sums = Scatter(net, at, sz, sum_bufs)
    load_bup.wait()
    for copy in load_up:
        copy.wait()
    for copy in last_up:
        copy.wait_recv()

    def project_up(slot):
        firsts.ready(slot)
        rows = pl.ds(slot * two, two)

        def up(i):
            cols = tile(i, 512)
            value = dot(fa[rows, :], wu[:, cols]) + bup[0:1, cols]
            hid[rows, cols] = value
            act[rows, cols] = gate(value).astype(BF16)

        loop(sz.hid // 512, up)

    project_up(0)
    firsts.relay()
    wd_spread[0].relay()
    project_up(2)
    project_up(1)
    firsts.relay_last()
    project_up(3)
    wd_spread[1].relay()
    cot_far = net.remote(cot_in.at[1 - at.zh], cot.at[own_rows, :], at.to_h)
    for copy in load_down:
        copy.wait()
    for item in wd_spread:
        item.near()
        item.far()
    for slot in (3, 1, 2, 0):
        rows = pl.ds(slot * two, two)

        def down(i, rows=rows, slot=slot):
            cols = tile(i, 512)
            sums.put(slot, cols, dot(act[rows, :], wd[:, cols]))

        loop(d // 512, down)
        sums.share(slot)
        if slot == 1:
            sums.send_diag()
    sums.send_free()
    sums.send_joined()
    load_vec.wait()
    load_fin.wait()
    load_cot.wait()
    cot_far.wait_recv()
    sums.wait()

    def strip_sum(row, value):
        gv[row : row + 1, :] = gv[row : row + 1, :] + jnp.sum(value, axis=0, keepdims=True)

    def second_norm(i):
        rows = tile(i, STRIP)
        xhat, _ = normed(fin[rows, :])
        value = xhat * vec[3:4, :] + vec[4:5, :] + sums.total(i) + vec[5:6, :]
        xhat, scale = normed(value)
        out[rows, :] = (xhat * vec[6:7, :] + vec[7:8, :]).astype(BF16)
        grad = cot[rows, :].astype(F32)
        strip_sum(6, grad * xhat)
        strip_sum(7, grad)
        grad = normed_back(grad * vec[6:7, :], xhat, scale)
        g2s[rows, :] = grad
        low = grad.astype(BF16)
        g2[rows, :] = low
        strip_sum(5, low.astype(F32))

    loop(t // STRIP, second_norm)
    gather = Gather(net, at, sz, g2, 0, t)
    gather.send()
    net.keep(out.at[own_rows, :], outputs.at[at.zh])
    sums.settle()

    def back(slot):
        gather.ready(slot)
        rows = pl.ds(slot * two, two)

        def down(i):
            cols = tile(i, 512)
            value = dot_nt(g2[rows, :], wd[cols, :])
            gh[rows, cols] = (value * gate_slope(hid[rows, cols])).astype(BF16)

        loop(sz.hid // 512, down)

        def up(i):
            cols = tile(i, 512)
            sums.put(slot, cols, dot_nt(gh[rows, :], wu[cols, :]))

        loop(d // 512, up)
        sums.share(slot)

    back(0)
    gather.relay()
    back(1)
    back(2)
    sums.send_free()
    gather.relay_last()
    out_far = net.remote(out.at[pl.ds((1 - at.zh) * h, h), :], outputs.at[at.zh], at.to_h)
    back(3)
    sums.send_diag()

    def down_grad(i):
        rows, cols = tile(i // (d // 512), 512), tile(i % (d // 512), 512)
        dwd[rows, cols] = dot_tn(act[:, rows], g2[:, cols]).astype(BF16)

    loop((sz.hid // 512) * (d // 512), down_grad)
    net.keep(dwd, grad_w_down)
    down_rows = sz.hid_shard // 4
    sum_d = Reduce(
        net, at, lambda p, j: dwd.at[pl.ds(p * sz.hid_shard + j * down_rows, down_rows), :], bufs, 4, True, None
    )
    sum_d.start(0)
    sums.send_joined()

    def up_grad(i):
        rows, cols = tile(i // (sz.hid // 512), 512), tile(i % (sz.hid // 512), 512)
        dwu[rows, cols] = dot_tn(fa[:, rows], gh[:, cols]).astype(BF16)

    loop((sz.hid // 512) * (d // 512), up_grad)
    net.keep(dwu, grad_w_up)
    sum_d.hop(0)
    for p in range(sz.parts):
        rf = sz.hid_shard
        gv[8:9, p * sz.slab : p * sz.slab + rf] = jnp.sum(
            gh[:, p * rf : (p + 1) * rf].astype(F32), axis=0, keepdims=True
        )
    sums.wait()

    def first_norm(i):
        rows = tile(i, STRIP)
        xhat, scale = normed(fin[rows, :])
        grad = g2s[rows, :] + sums.total(i)
        strip_sum(3, grad * xhat)
        strip_sum(4, grad)
        grad = normed_back(grad * vec[3:4, :], xhat, scale)
        g2s[rows, :] = grad
        low = grad.astype(BF16)
        out_low[rows, :] = low
        strip_sum(2, low.astype(F32))

    out_low = cot
    loop(t // STRIP, first_norm)
    net.keep(g2s, grad_first_in)
    net.keep(out_low, grad_low)
    net.keep(gv, grad_vec)
    for j in (1, 2, 3):
        sum_d.add(j)
    late = pl.ds(down_rows, 3 * down_rows)
    early = pl.ds(0, down_rows)
    net.keep(sum_d.out.at[late, :], down_sum)
    sum_d.from_h[0].wait_recv()
    net.keep(sum_d.inn.at[early, :], down_in)
    out_far.wait_recv()
    net.finish()


def feed_forward(sz, *args):
    t, d, r = sz.tokens, sz.width, sz.rows_all
    shape = jax.ShapeDtypeStruct
    anywhere = pl.BlockSpec(memory_space=pl.ANY)
    outs = (
        shape((2, sz.half, d), BF16),
        shape((t, d), F32),
        shape((t, d), BF16),
        shape((d, sz.hid), BF16),
        shape((sz.hid, d), BF16),
        shape((16, d), F32),
        shape((sz.hid_shard // 4 * 3, d), BF16),
        shape((sz.hid_shard // 4, d), BF16),
    )
    scratch = [
        pltpu.VMEM((r, d), BF16),
        pltpu.VMEM((d, sz.hid), BF16),
        pltpu.VMEM((sz.hid, d), BF16),
        pltpu.VMEM((8, d), F32),
        pltpu.VMEM((8, sz.hid), F32),
        pltpu.VMEM((t, d), F32),
        pltpu.VMEM((t, d), BF16),
        pltpu.VMEM((r, sz.hid), F32),
        pltpu.VMEM((r, sz.hid), BF16),
        pltpu.VMEM((r, sz.hid), BF16),
        pltpu.VMEM((r, d), BF16),
        pltpu.VMEM((t, d), F32),
        pltpu.VMEM((t, d), BF16),
        pltpu.VMEM((16, d), F32),
        pltpu.VMEM((d, sz.hid), BF16),
        pltpu.VMEM((sz.hid, d), BF16),
        *Scatter.scratch(sz),
        *Reduce.scratch(sz, sz.hid_shard, d, BF16, True, 1),
        pltpu.SemaphoreType.DMA((64 + 10 * sz.nx,)),
        pltpu.SemaphoreType.DMA((64 + 10 * sz.nx,)),
        pltpu.SemaphoreType.DMA((24 + 12 * sz.nx,)),
    ]
    return pl.pallas_call(
        functools.partial(feed_forward_kernel, sz),
        out_shape=outs,
        in_specs=[anywhere] * 8,
        out_specs=[anywhere] * len(outs),
        scratch_shapes=scratch,
        compiler_params=pltpu.CompilerParams(
            collective_id=1, has_side_effects=True, vmem_limit_bytes=VMEM_LIMIT
        ),
        name="feed_forward",
    )(*args)


class Reduce:
    def __init__(self, net, at, view, bufs, chunks, held, result):
        self.net, self.at, self.view, self.chunks = net, at, view, chunks
        self.got, self.own, self.out, self.inn = bufs
        self.rows = self.out.shape[0] // chunks
        self.result = result
        self.held = held
        self.groups = (at.x * 2 + (1 - at.zh), at.x * 2 + at.zh)
        self.from_x, self.from_h, self.loads = {}, {}, {}

    @staticmethod
    def scratch(sz, rows, cols, dtype, held, kinds=2):
        return [
            pltpu.VMEM((sz.nx - 1, kinds, rows, cols), dtype),
            pltpu.VMEM((2, 8, 128) if held else (2, rows, cols), dtype),
            pltpu.VMEM((rows, cols), dtype),
            pltpu.VMEM((rows, cols), dtype),
        ]

    def chunk(self, j):
        return pl.ds(j * self.rows, self.rows)

    def start(self, which):
        at, net = self.at, self.net
        zh = 1 - at.zh if which == 0 else at.zh
        for j in range(self.chunks):
            for step in range(1, at.nx):
                p = at.x_of(step) * 2 + zh
                self.from_x[which, j, step] = net.remote(
                    self.view(p, j), self.got.at[step - 1, which, self.chunk(j), :], at.to_x(step)
                )
            if not self.held:
                self.loads[which, j] = net.local(
                    self.view(self.groups[which], j), self.own.at[which, self.chunk(j), :]
                )

    def term(self, which, j, i):
        rows = pl.ds(pl.multiple_of(j * self.rows + i * STRIP, STRIP), STRIP)
        if self.held:
            total = self.view(self.groups[which], j)[tile(i, STRIP), :].astype(F32)
        else:
            total = self.own[which, rows, :].astype(F32)
        for step in range(1, self.at.nx):
            total = total + self.got[step - 1, which, rows, :].astype(F32)
        return rows, total

    def ready(self, which, j):
        for step in range(1, self.at.nx):
            self.from_x[which, j, step].wait_recv()
        if not self.held:
            self.loads[which, j].wait()

    def add(self, j):
        self.ready(0, j)

        def body(i):
            rows, total = self.term(0, j, i)
            self.out[rows, :] = total.astype(self.out.dtype)

        loop(self.rows // STRIP, body)

    def hop(self, j):
        self.add(j)
        self.send(j)

    def send(self, j):
        self.from_h[j] = self.net.remote(
            self.out.at[self.chunk(j), :], self.inn.at[self.chunk(j), :], self.at.to_h
        )

    def close(self, j):
        self.ready(1, j)
        if j in self.from_h:
            self.from_h[j].wait_recv()

        def body(i):
            rows, total = self.term(1, j, i)
            self.result[rows, :] = (total + self.inn[rows, :].astype(F32)).astype(self.result.dtype)

        loop(self.rows // STRIP, body)


def attention_backward_kernel(
    sz,
    grad_low, grad_first_in, x_all, wqkv, w_out_own, qkv_all, ctx_all, grad_w_up, grad_w_down, grad_vec, down_sum, down_in,
    input_grad, out_wq, out_wk, out_wv, out_wo, out_wup, out_wdown, out_vec, out_bup,
    gb, xs, wq, wo, qkv, ctx, gfi, gv, dctx, dqkv, dk, dv, ig, dwq, dwo, dwo_own, res_q, res_o, res_u, res_d, res_v,
    vec_got, vec_sum, bup_out, *rest,
):
    *bufs, send, recv, local = rest
    sum_bufs, bufs = bufs[:7], bufs[7:]
    at = Place(sz)
    net = Copies(send, recv, local)
    t, d, h = sz.tokens, sz.width, sz.half
    two = 2 * t
    rw, rf = sz.row_shard, sz.hid_shard
    flips = range(1, TP)
    load_gb = net.local(grad_low, gb.at[pl.ds(0, t), :])
    load_wo = net.local(w_out_own, wo)
    load_qkv = net.local(qkv_all, qkv)
    load_ctx = net.local(ctx_all, ctx)
    load_gv = net.local(grad_vec, gv)
    greet([at.peer(f) for f in flips] + [at.to_h] + [at.to_x(s) for s in range(1, sz.nx)])
    load_gb.wait()
    gather = Gather(net, at, sz, gb, 0, t, tall=True)
    gather.send()

    up_rows, down_rows = sz.slab // 4, rf // 4
    sum_u = Reduce(
        net, at, lambda p, j: grad_w_up.at[pl.ds(p * sz.slab + j * up_rows, up_rows), :],
        bufs[0:4], 4, False, res_u,
    )
    sum_d = Reduce(
        net, at, lambda p, j: grad_w_down.at[pl.ds(p * rf + j * down_rows, down_rows), :],
        bufs[4:8], 4, False, res_d,
    )
    sum_q = Reduce(
        net, at, lambda p, j: dwq.at[pl.ds(p * sz.slab + j * up_rows, up_rows), :], bufs[8:12], 4, True, res_q
    )
    sum_o = Reduce(net, at, lambda p, j: dwo_own.at[p], bufs[12:16], 1, True, res_o)
    sum_v = Reduce(
        net, at, lambda p, j: gv.at[:, pl.ds(pl.multiple_of(p * sz.slab, sz.slab), sz.slab)],
        bufs[16:20], 1, True, res_v,
    )
    late = pl.ds(down_rows, 3 * down_rows)
    load_sum = net.local(down_sum, sum_d.out.at[late, :])
    load_in = net.local(down_in, sum_d.inn.at[pl.ds(0, down_rows), :])
    sum_u.start(0)
    load_sum.wait()
    for j in (1, 2, 3):
        sum_d.send(j)
    sum_u.start(1)
    load_x = net.local(x_all, xs)
    load_wq = net.local(wqkv, wq)
    load_gfi = net.local(grad_first_in, gfi)
    hops = [(sum_u, j) for j in range(4)]

    def pump(count):
        for _ in range(min(count, len(hops))):
            item, j = hops.pop(0)
            item.hop(j)

    load_wo.wait()

    def context_grad(slot):
        gather.ready(slot)
        rows = pl.ds(slot * two, two)
        dctx[rows, :] = dot_nt(gb[rows, :], wo[...]).astype(BF16)

    context_grad(0)
    gather.relay()
    pump(1)
    context_grad(1)
    context_grad(2)
    gather.relay_last()
    pump(1)
    context_grad(3)
    pump(1)
    load_qkv.wait()

    def attend_back(k):
        q_cols = slice(k * HD, (k + 1) * HD)
        k_cols = slice(sz.cols + k * HD, sz.cols + (k + 1) * HD)
        v_cols = slice(2 * sz.cols + k * HD, 2 * sz.cols + (k + 1) * HD)
        turned = qkv[:, k_cols].T

        def body(i):
            rows = tile(i, 256)
            queries, grads = qkv[rows, q_cols], dctx[rows, q_cols]
            scores = dot_nt(qkv[:, k_cols], queries) * SCALE
            exps = jnp.exp(scores - jnp.max(scores, axis=0, keepdims=True))
            probs = exps * (1.0 / jnp.sum(exps, axis=0, keepdims=True))
            value_part = dot(probs.astype(BF16), grads)
            slopes = probs * dot_nt(qkv[:, v_cols], grads)
            score_grads = (slopes - probs * jnp.sum(slopes, axis=0, keepdims=True)).astype(BF16)
            key_part = dot(score_grads, queries)
            first = i == 0
            dv[...] = jnp.where(first, value_part, dv[...] + value_part)
            dk[...] = jnp.where(first, key_part, dk[...] + key_part)
            dqkv[rows, q_cols] = (dot(turned, score_grads).T * SCALE).astype(BF16)

        loop(sz.rows_all // 256, body)
        dqkv[:, k_cols] = (dk[...] * SCALE).astype(BF16)
        dqkv[:, v_cols] = dv[...].astype(BF16)

    attend_back(0)
    pump(2)
    for k in range(1, sz.heads):
        attend_back(k)
    pump(2)
    load_wq.wait()

    sums = Scatter(net, at, sz, sum_bufs, tall=True)
    for slot in (3, 1, 2, 0):
        rows = pl.ds(slot * two, two)

        def body(i, rows=rows, slot=slot):
            cols = tile(i, 512)
            sums.put(slot, cols, dot_nt(dqkv[rows, :], wq[cols, :]))

        loop(d // 512, body)
        sums.share(slot)
        if slot == 1:
            sums.send_diag()
    sums.send_free()
    pump(1)
    load_x.wait()
    load_ctx.wait()

    def qkv_grad(i):
        rows = tile(i, 512)
        dwq[rows, :] = dot_tn(xs[:, rows], dqkv[...]).astype(BF16)

    loop(d // 512, qkv_grad)
    sum_q.start(0)
    sum_d.start(1)
    sums.send_joined()

    def out_grad(i):
        cols = tile(i, 512)
        dwo[:, cols] = dot_tn(ctx[...], gb[:, cols]).astype(BF16)

    loop(d // 512, out_grad)
    group = at.t // sz.pieces
    member = at.t - group * sz.pieces
    wo_in = []
    for k in range(sz.heads):
        for f in range(1, sz.pieces):
            other = at.index_of(f) - group * sz.pieces
            wo_in.append(
                net.remote(
                    dwo.at[pl.ds((k * sz.pieces + other) * rw, rw), :],
                    dwo_own.at[member * sz.heads + k],
                    at.peer(f),
                )
            )
        net.local(
            dwo.at[pl.ds((k * sz.pieces + member) * rw, rw), :], dwo_own.at[member * sz.heads + k]
        ).wait()
    load_gv.wait()
    for k in range(sz.heads):
        lanes = at.head_lanes(sz, at.t, k)
        gv[0:1, lanes] = jnp.sum(dqkv[:, k * HD : (k + 1) * HD].astype(F32), axis=0, keepdims=True)
        at_v = 2 * sz.cols + k * HD
        gv[1:2, lanes] = jnp.sum(dqkv[:, at_v : at_v + HD].astype(F32), axis=0, keepdims=True)
    for copy in wo_in:
        copy.wait_recv()
    sum_o.start(0)
    sum_v.start(0)
    sum_q.hop(0)
    sum_q.start(1)
    sum_o.start(1)
    sum_v.start(1)
    load_gfi.wait()
    sum_q.hop(1)
    sums.wait()

    def final(i):
        rows = tile(i, STRIP)
        ig[rows, :] = (gfi[rows, :] + sums.total(i)).astype(BF16)

    loop(t // STRIP, final)
    own_rows = pl.ds(at.zh * h, h)
    net.keep(ig.at[own_rows, :], input_grad.at[at.zh])
    for j in (2, 3):
        sum_q.hop(j)
    sum_o.hop(0)
    sum_v.hop(0)
    ig_far = net.remote(ig.at[pl.ds((1 - at.zh) * h, h), :], input_grad.at[at.zh], at.to_h)
    load_in.wait()

    for j in range(4):
        sum_u.close(j)

    def rows_of(buf, member):
        return buf.at[pl.ds(member * rw, rw), :]

    def up_parts(member):
        if not sz.by_lanes:
            return [(res_u.at[pl.ds(member * rw, rw), :], out_wup.at[at.t])]
        return [
            (
                res_u.at[pl.ds(member * rw, rw), pl.ds(p * rf, rf)],
                out_wup.at[:, pl.ds(pl.multiple_of((p * TP + at.t) * rf, rf), rf)],
            )
            for p in range(sz.parts)
        ]

    def qkv_parts(member):
        return [
            (
                res_q.at[pl.ds(member * rw, rw), pl.ds(which * sz.cols + k * HD, HD)],
                target.at[:, at.head_lanes(sz, at.t, k)],
            )
            for which, target in enumerate((out_wq, out_wk, out_wv))
            for k in range(sz.heads)
        ]

    net.kept.append(net.local_parts(up_parts(at.t), rows_of(res_u, at.t)))
    back_in = [
        net.remote_parts(up_parts(at.index_of(f)), rows_of(res_u, at.index_of(f)), at.peer(f)) for f in flips
    ]
    for j in range(4):
        sum_d.close(j)
    net.keep(res_d, out_wdown)
    for j in range(4):
        sum_q.close(j)
    net.kept.append(net.local_parts(qkv_parts(at.t), rows_of(res_q, at.t)))
    back_in += [
        net.remote_parts(qkv_parts(at.index_of(f)), rows_of(res_q, at.index_of(f)), at.peer(f)) for f in flips
    ]
    sum_o.close(0)
    net.keep(res_o, out_wo)
    sum_v.close(0)

    def lanes_of(index):
        return pl.ds(pl.multiple_of(index // sz.pieces * HD, HD), HD)

    vec_got[at.t] = res_v[0:8, lanes_of(at.t)]
    vec_in = [
        net.remote(res_v.at[pl.ds(0, 8), lanes_of(at.index_of(f))], vec_got.at[at.t], at.peer(f)) for f in flips
    ]
    bup_out[...] = res_v[8:16, 0:rf]
    net.keep(bup_out, out_bup)
    for copy in vec_in:
        copy.wait_recv()
    total = vec_got[0]
    for member in range(1, TP):
        total = total + vec_got[member]
    vec_sum[...] = total
    net.keep(vec_sum, out_vec)
    for copy in back_in:
        copy.wait_recv()
    ig_far.wait_recv()
    net.finish()


def attention_backward(sz, *args):
    t, d, r = sz.tokens, sz.width, sz.rows_all
    rw, rf = sz.row_shard, sz.hid_shard
    wide = 3 * sz.cols
    shape = jax.ShapeDtypeStruct
    anywhere = pl.BlockSpec(memory_space=pl.ANY)
    outs = (
        shape((2, sz.half, d), BF16),
        shape((rw, d), BF16),
        shape((rw, d), BF16),
        shape((rw, d), BF16),
        shape((rw, d), BF16),
        shape((rw, sz.hidden) if sz.by_lanes else (TP, rw, sz.hid), BF16),
        shape((rf, d), BF16),
        shape((8, HD), F32),
        shape((8, rf), F32),
    )
    scratch = [
        pltpu.VMEM((r, d), BF16),
        pltpu.VMEM((r, d), BF16),
        pltpu.VMEM((d, wide), BF16),
        pltpu.VMEM((sz.cols, d), BF16),
        pltpu.VMEM((r, wide), BF16),
        pltpu.VMEM((r, sz.cols), BF16),
        pltpu.VMEM((t, d), F32),
        pltpu.VMEM((16, d), F32),
        pltpu.VMEM((r, sz.cols), BF16),
        pltpu.VMEM((r, wide), BF16),
        pltpu.VMEM((r, HD), F32),
        pltpu.VMEM((r, HD), F32),
        pltpu.VMEM((t, d), BF16),
        pltpu.VMEM((d, wide), BF16),
        pltpu.VMEM((sz.cols, d), BF16),
        pltpu.VMEM((sz.parts, rw, d), BF16),
        pltpu.VMEM((sz.slab, wide), BF16),
        pltpu.VMEM((rw, d), BF16),
        pltpu.VMEM((sz.slab, sz.hid), BF16),
        pltpu.VMEM((rf, d), BF16),
        pltpu.VMEM((16, sz.slab), F32),
        pltpu.VMEM((TP, 8, HD), F32),
        pltpu.VMEM((8, HD), F32),
        pltpu.VMEM((8, rf), F32),
        *Scatter.scratch(sz),
        *Reduce.scratch(sz, sz.slab, sz.hid, BF16, False),
        *Reduce.scratch(sz, rf, d, BF16, False),
        *Reduce.scratch(sz, sz.slab, wide, BF16, True),
        *Reduce.scratch(sz, rw, d, BF16, True),
        *Reduce.scratch(sz, 16, sz.slab, F32, True),
        pltpu.SemaphoreType.DMA((70 + 28 * sz.nx,)),
        pltpu.SemaphoreType.DMA((70 + 28 * sz.nx,)),
        pltpu.SemaphoreType.DMA((48,)),
    ]
    return pl.pallas_call(
        functools.partial(attention_backward_kernel, sz),
        out_shape=outs,
        in_specs=[anywhere] * 12,
        out_specs=[anywhere] * len(outs),
        scratch_shapes=scratch,
        compiler_params=pltpu.CompilerParams(
            collective_id=2, has_side_effects=True, vmem_limit_bytes=VMEM_LIMIT
        ),
        name="attention_backward",
    )(*args)


def widen_kernel(count, *refs):
    for src, dst in zip(refs[:count], refs[count:]):
        flat = len(src.shape) == 2

        def body(i, src=src, dst=dst, flat=flat):
            if flat:
                dst[tile(i, STRIP), :] = src[tile(i, STRIP), :].astype(F32)
            else:
                for j in range(src.shape[0]):
                    dst[j, tile(i, STRIP), :] = src[j, tile(i, STRIP), :].astype(F32)

        loop(src.shape[-2] // STRIP, body)


def widen(*arrays):
    whole = pl.BlockSpec(memory_space=pltpu.VMEM)
    return pl.pallas_call(
        functools.partial(widen_kernel, len(arrays)),
        out_shape=[jax.ShapeDtypeStruct(a.shape, F32) for a in arrays],
        in_specs=[whole] * len(arrays),
        out_specs=[whole] * len(arrays),
        compiler_params=pltpu.CompilerParams(vmem_limit_bytes=VMEM_LIMIT),
        name="widen",
    )(*arrays)


def per_device(
    sz, inputs, cotangent, w_query, w_key, w_value, w_out, b_query, b_value, b_out, ln1_gain, ln1_bias,
    w_up, b_up, w_down, b_down, ln2_gain, ln2_bias,
):
    rw, rf = sz.row_shard, sz.hid_shard
    t = lax.axis_index("zl") * 4 + lax.axis_index("y") * 2 + lax.axis_index("c")
    p = lax.axis_index("x") * 2 + lax.axis_index("zh")
    piece = t % sz.pieces
    rows = jnp.stack([b_query, b_value, b_out, ln1_gain, ln1_bias, b_down, ln2_gain, ln2_bias]).astype(F32)
    here = lax.broadcasted_iota(jnp.int32, (8, HD), 1) // rw == piece
    low = jnp.where(here, jnp.tile(rows, (1, sz.pieces)), 0.0)
    up = b_up.astype(F32)
    if rf >= HD:
        high = jnp.pad(up.reshape(rf // HD, HD), ((0, 8 - rf // HD), (0, 0)))
    else:
        each = HD // rf
        here = lax.broadcasted_iota(jnp.int32, (8, HD), 1) // rf == p % each
        high = jnp.where(here, jnp.tile(up[None], (8, each)), 0.0)
    vec_pack = jnp.concatenate([low, high], axis=0)

    up_rows = w_up
    if not sz.by_lanes:
        up_rows = w_up.reshape(rw, sz.parts, TP, rf).transpose(2, 0, 1, 3).reshape(TP, rw, sz.hid)

    x_all, wqkv, w_out_own, up_own, down_own, vec_all, bup_all, qkv, ctx, first_in, first_low = attention_forward(
        sz, inputs, w_query, w_key, w_value, w_out, up_rows, w_down, vec_pack
    )
    outputs, grad_first_in, grad_low, grad_up, grad_down, grad_vec, down_sum, down_in = feed_forward(
        sz, first_low, first_in, up_own, down_own, vec_all, bup_all, cotangent, w_down
    )
    *grads, out_vec, out_bup = attention_backward(
        sz, grad_low, grad_first_in, x_all, wqkv, w_out_own, qkv, ctx, grad_up, grad_down, grad_vec,
        down_sum, down_in,
    )
    input_grad, grad_wq, grad_wk, grad_wv, grad_wo, grad_wup, grad_wdown = widen(*grads)
    if not sz.by_lanes:
        grad_wup = grad_wup.reshape(TP, rw, sz.parts, rf).transpose(1, 2, 0, 3).reshape(rw, sz.hidden)
    vec = lax.dynamic_slice(out_vec, (0, piece * rw), (8, rw))
    return (
        outputs,
        input_grad,
        grad_wq,
        grad_wk,
        grad_wv,
        grad_wo,
        vec[0],
        vec[1],
        vec[2],
        vec[3],
        vec[4],
        grad_wup,
        out_bup[0],
        grad_wdown,
        vec[5],
        vec[6],
        vec[7],
    )


def solution(mesh):
    nx = mesh.shape["dp"]
    plane = Mesh(mesh.devices.reshape(nx, 2, mesh.shape["hd"] // 2, 2, mesh.shape["sq"] // 2), AXES)
    rows, matrix, vector = P("x", AXES[1:], None), P(AXES, None), P(AXES)

    def run(*args):
        batch, length, width = args[0].shape
        sz = Sizes(nx, width, args[11].shape[1], batch // nx * length // (2 * TP))
        call = jax.shard_map(
            functools.partial(per_device, sz),
            mesh=plane,
            in_specs=(rows, rows) + (matrix,) * 4 + (vector,) * 5 + (matrix, vector, matrix) + (vector,) * 3,
            out_specs=(rows, rows) + (matrix,) * 4 + (vector,) * 5 + (matrix, vector, matrix) + (vector,) * 3,
            check_vma=False,
        )
        return call(*args)

    return run
```
